32 devices in a mesh: dp: 4 (over y, core), space: 8 (over z, x).
Axes of the slice: x: 2, y: 2, z: 4, core: 2. Of those that a mesh axis runs over, the one named last changes fastest.
Arguments:
- inputs: bfloat16 [12, 8, 4, 8192], P('dp', 'space'), may hold values from -6 to 6
- mask_one: int32 [12, 8, 16, 8192], P('dp', 'space'), may hold values 0 or 1
- place_one: int32 [12, 8, 16, 1024], P('dp', 'space'), may hold values from 0 to 7
- pooled_one: bfloat16 [12, 8, 16, 1024], P('dp', 'space'), may hold values from 0 to 2
- w_two: bfloat16 [27, 16, 32], replicated, may hold values from -0.21875 to 0.21875
- mask_two: int32 [12, 8, 32, 1024], P('dp', 'space'), may hold values 0 or 1
- place_two: int32 [12, 8, 32, 128], P('dp', 'space'), may hold values from 0 to 7
- grad_two: bfloat16 [12, 8, 32, 128], P('dp', 'space'), may hold values from -24 to 24
Outputs:
- grad_pooled: bfloat16 [12, 8, 16, 1024], P('dp', 'space')
- grad_w_one: float32 [27, 4, 16], replicated
- grad_w_two: float32 [27, 16, 32], replicated
The draws below stay inside these ranges and needn't reach their ends.
All inputs are finite; a program needn't handle non-finite values. No bound on the sum of `mask_one` or of `mask_two` on one device may be relied on, other than what follows from the above.
Results may differ from the reference program's by a relative error of at most 0.0029.
Values may be sent and summed in bfloat16 or wider, within the bound.
No kernel may reach another device: no remote copies, remote signals or barrier semaphores. Data moves between devices by JAX's collectives and lax.ppermute only.
A program may use at most 128 MiB of HBM per device.

```python
import jax
import jax.numpy as jnp
from jax import lax

C_IN = 4
C_ONE = 16
C_TWO = 32
BX = 4
BY = 8
BZ = 256
SIDE = 2
SAMPLES = 12
BLOCKS = 8
CELLS = 8192
TERMS_ONE = 786432
TERMS_TWO = 98304


def touch_ends(array, key, least, high):
    longest = array.shape.index(max(array.shape))
    spots = []
    for shift in (0, 1):
        where = [jax.random.randint(jax.random.fold_in(key, axis), (), 0, length) for axis, length in enumerate(array.shape)]
        where[longest] = (where[longest] + shift) % array.shape[longest]
        spots.append(tuple(where))
    return array.at[spots[0]].set(least).at[spots[1]].set(high)


def steps_of(own_key, extent, split, low, high):
    gain = 1.0
    for axis_at, parts in split:
        steps = jax.random.uniform(jax.random.fold_in(jax.random.fold_in(own_key, 6), axis_at), (parts,), jnp.float32, low / len(split), high / len(split))
        gain = gain * jnp.repeat(jnp.exp(steps), extent[axis_at] // parts).reshape((-1,) + (1,) * (len(extent) - 1 - axis_at))
    return gain


def bell_draw(rng, shape, deviation, most, split=(), dtype=jnp.bfloat16):
    loudness = steps_of(rng, shape, split, -0.22, 0.18) if split else 1.0
    values = jax.random.normal(rng, shape, jnp.float32) * deviation * loudness
    return jnp.minimum(jnp.maximum(values, -most), most).astype(dtype)


def setup_inputs(seed: int = 0) -> dict:
    seeds = jax.random.split(jax.random.key(seed), 9)
    inputs = bell_draw(seeds[0], (SAMPLES, BLOCKS, C_IN, CELLS), 1.0, 6.0, ((0, 4), (1, 8)))
    mask_one = touch_ends((jax.random.randint(seeds[1], (SAMPLES, BLOCKS, C_ONE, CELLS), 0, 2) < 1).astype(jnp.int32), jax.random.fold_in(seeds[1], 1), 0, 1)
    place_one = touch_ends(jax.random.randint(seeds[2], (SAMPLES, BLOCKS, C_ONE, CELLS // 8), 0, 8), jax.random.fold_in(seeds[2], 1), 0, 7).astype(jnp.int32)
    pooled_one = jnp.clip(2.0 * jax.random.uniform(seeds[3], (SAMPLES, BLOCKS, C_ONE, CELLS // 8), jnp.float32) ** steps_of(seeds[3], (SAMPLES, BLOCKS, C_ONE, CELLS // 8), ((0, 4), (1, 8)), -0.2, 0.2), 0.0, 2.0).astype(jnp.bfloat16)
    w_two = bell_draw(seeds[4], (27, C_ONE, C_TWO), (27 * C_TWO) ** -0.5, 0.21875)
    mask_two = touch_ends((jax.random.randint(seeds[5], (SAMPLES, BLOCKS, C_TWO, CELLS // 8), 0, 2) < 1).astype(jnp.int32), jax.random.fold_in(seeds[5], 1), 0, 1)
    place_two = touch_ends(jax.random.randint(seeds[6], (SAMPLES, BLOCKS, C_TWO, CELLS // 64), 0, 8), jax.random.fold_in(seeds[6], 1), 0, 7).astype(jnp.int32)
    grad_two = bell_draw(seeds[7], (SAMPLES, BLOCKS, C_TWO, CELLS // 64), 4.0, 24.0, ((0, 4), (1, 8)))
    return {"inputs": inputs, "mask_one": mask_one, "place_one": place_one, "pooled_one": pooled_one, "w_two": w_two, "mask_two": mask_two, "place_two": place_two, "grad_two": grad_two}


def to_box(blocks, channels, size_x, size_y, size_z):
    shaped = blocks.reshape(SIDE, SIDE, SIDE, channels, size_x, size_y, size_z)
    shaped = jnp.transpose(shaped, (3, 0, 4, 1, 5, 2, 6))
    return shaped.reshape(channels, SIDE * size_x, SIDE * size_y, SIDE * size_z)


def from_box(whole, channels, size_x, size_y, size_z):
    shaped = whole.reshape(channels, SIDE, size_x, SIDE, size_y, SIDE, size_z)
    shaped = jnp.transpose(shaped, (1, 3, 5, 0, 2, 4, 6))
    return shaped.reshape(SIDE * SIDE * SIDE, channels, size_x * size_y * size_z)


def spread(pooled, position):
    zeros = jnp.zeros_like(pooled)
    pieces = [jnp.where(position == k, pooled, zeros) for k in range(8)]
    stacked = jnp.stack(pieces, axis=-1)
    chans, size_x, size_y, size_z = pooled.shape
    stacked = stacked.reshape(chans, size_x, size_y, size_z, 2, 2, 2)
    stacked = jnp.transpose(stacked, (0, 1, 4, 2, 5, 3, 6))
    return stacked.reshape(chans, 2 * size_x, 2 * size_y, 2 * size_z)


def offsets():
    return [(ox, oy, oz) for ox in (-1, 0, 1) for oy in (-1, 0, 1) for oz in (-1, 0, 1)]


def one_sample(inputs, mask_one, place_one, pooled_one, w_two, mask_two, place_two, grad_two):
    half_x, half_y, half_z = BX // 2, BY // 2, BZ // 2
    quarter_x, quarter_y, quarter_z = BX // 4, BY // 4, BZ // 4
    gtwo = to_box(grad_two, C_TWO, quarter_x, quarter_y, quarter_z)
    ptwo = to_box(place_two, C_TWO, quarter_x, quarter_y, quarter_z)
    mtwo = to_box(mask_two, C_TWO, half_x, half_y, half_z)
    grad_conv_two = jnp.where(mtwo == 1, spread(gtwo, ptwo), jnp.zeros((), jnp.bfloat16)).astype(jnp.bfloat16)
    pooled = to_box(pooled_one, C_ONE, half_x, half_y, half_z)
    flat_two = grad_conv_two.reshape(C_TWO, -1)
    wgrad_two = []
    grad_sum = jnp.zeros((C_ONE, flat_two.shape[1]), jnp.float32)
    for index, (ox, oy, oz) in enumerate(offsets()):
        ahead = jnp.roll(pooled, (-ox, -oy, -oz), axis=(1, 2, 3)).reshape(C_ONE, -1)
        wgrad_two.append(jnp.dot(ahead, flat_two.T, preferred_element_type=jnp.float32))
        behind = jnp.roll(grad_conv_two, (ox, oy, oz), axis=(1, 2, 3)).reshape(C_TWO, -1)
        grad_sum = grad_sum + jnp.dot(w_two[index], behind, preferred_element_type=jnp.float32)
    grad_pooled = grad_sum.astype(jnp.bfloat16).reshape(C_ONE, SIDE * half_x, SIDE * half_y, SIDE * half_z)
    pone = to_box(place_one, C_ONE, half_x, half_y, half_z)
    mone = to_box(mask_one, C_ONE, BX, BY, BZ)
    grad_conv_one = jnp.where(mone == 1, spread(grad_pooled, pone), jnp.zeros((), jnp.bfloat16)).astype(jnp.bfloat16)
    flat_one = grad_conv_one.reshape(C_ONE, -1)
    source = to_box(inputs, C_IN, BX, BY, BZ)
    wgrad_one = []
    for ox, oy, oz in offsets():
        ahead = jnp.roll(source, (-ox, -oy, -oz), axis=(1, 2, 3)).reshape(C_IN, -1)
        wgrad_one.append(jnp.dot(ahead, flat_one.T, preferred_element_type=jnp.float32))
    blocks_out = from_box(grad_pooled, C_ONE, half_x, half_y, half_z)
    return blocks_out, jnp.stack(wgrad_one), jnp.stack(wgrad_two)


def reference(inputs, mask_one, place_one, pooled_one, w_two, mask_two, place_two, grad_two):
    def per_sample(items):
        return one_sample(items[0], items[1], items[2], items[3], w_two, items[4], items[5], items[6])

    grad_pooled, wgrad_one, wgrad_two = lax.map(per_sample, (inputs, mask_one, place_one, pooled_one, mask_two, place_two, grad_two))
    grad_w_one = jnp.sum(wgrad_one, axis=0) * (float(TERMS_ONE) ** -0.5)
    grad_w_two = jnp.sum(wgrad_two, axis=0) * (float(TERMS_TWO) ** -0.5)
    return grad_pooled, grad_w_one, grad_w_two
```

```python
import functools

import jax
import jax.numpy as jnp
from jax import lax
from jax.experimental import pallas as pl
from jax.experimental.pallas import tpu as pltpu
from jax.sharding import PartitionSpec as P

C_IN = 4
C_ONE = 16
C_TWO = 32
BX = 4
BY = 8
BZ = 256
HX, HY, HZ = BX // 2, BY // 2, BZ // 2
QY, QZ = HY // 2, HZ // 2
LANES = 128
PACK = 16
OFFS = (-1, 0, 1)
GRAD_W_TWO = 27 * C_TWO
WIDTH = 1024
ONE_AT = WIDTH - LANES
NT = (((1,), (1,)), ((), ()))
f32, bf16, i32 = jnp.float32, jnp.bfloat16, jnp.int32


def iota(shape, dim):
    return lax.broadcasted_iota(i32, shape, dim)


def doubling():
    return (iota((LANES, 2 * LANES), 0) == iota((LANES, 2 * LANES), 1) // 2).astype(bf16)


def prepare(samples, grad, place, mask, source, vp, edge, own, faces_x, ends_y, mids_y):
    rows = samples * C_TWO
    table = doubling()
    values = jnp.dot(grad[...].reshape(rows, LANES), table, preferred_element_type=f32)
    spots = place[...].reshape(rows, LANES).astype(f32).astype(bf16)
    wide = jnp.dot(spots, table, preferred_element_type=f32)
    parity = (iota((rows, LANES), 1) % 2).astype(f32)
    halves = []
    for qy in range(QY):
        v = values[:, qy * LANES : (qy + 1) * LANES]
        p = wide[:, qy * LANES : (qy + 1) * LANES] - parity
        total = jnp.zeros((rows, LANES), f32)
        for x in range(HX):
            for dy in range(2):
                at = (x * HY + 2 * qy + dy) * LANES
                on = mask[:, 0, :, at : at + LANES].reshape(rows, LANES) == 1
                total = total + jnp.where(on & (p == 4.0 * x + 2.0 * dy), v, 0.0)
        halves.append(total)
    kept = jnp.concatenate(halves, axis=1).astype(bf16)
    v = lax.dot_general(kept, table, NT, preferred_element_type=f32).astype(bf16)
    vp[0:rows] = v
    vp[rows : 2 * rows] = spots
    lane = iota((LANES, LANES), 0)
    spot = (lane // QZ) * 2 + (lane % QZ == QZ - 1).astype(i32)
    spot = jnp.where((lane % QZ == 0) | (lane % QZ == QZ - 1), spot, -LANES)
    column = iota((LANES, LANES), 1)
    packed = jnp.zeros((C_TWO, LANES), f32)
    for s in range(samples):
        for t, field in enumerate((v, spots)):
            pick = (spot + (8 * s + 4 * t) == column).astype(bf16)
            packed = packed + jnp.dot(
                field[s * C_TWO : (s + 1) * C_TWO], pick, preferred_element_type=f32
            )
    edge[0:C_TWO] = packed.astype(bf16)
    pieces = [source[s, 0].astype(f32) for s in range(samples)]
    pieces.append(jnp.zeros((PACK - samples * C_IN, BX * BY * BZ), f32))
    cells = jnp.concatenate(pieces, axis=0)
    packed_cells = cells.astype(bf16)
    own[...] = packed_cells
    plane = BY * BZ
    faces_x[:, 0:plane] = packed_cells[:, 0:plane]
    faces_x[:, plane : 2 * plane] = packed_cells[:, (BX - 1) * plane :]
    for ref, pair in ((ends_y, (0, BX - 1)), (mids_y, (1, BX - 2))):
        for i, x in enumerate(pair):
            for j, y in enumerate((0, BY - 1)):
                at = (x * BY + y) * BZ
                ref[:, (2 * i + j) * BZ : (2 * i + j + 1) * BZ] = packed_cells[:, at : at + BZ]
    lane = iota((PACK, LANES), 1)
    ends = jnp.zeros((PACK, LANES), f32)
    for row in range(BX * BY):
        for last in range(2):
            at = row * BZ + last * (BZ - 1)
            ends = jnp.where(lane == 2 * row + last, cells[:, at : at + 1], ends)
    edge[C_TWO : C_TWO + PACK] = ends.astype(bf16)


def select_one(samples, place, mask, weights, chosen, flat_weights):
    rows = samples * C_ONE
    table = doubling()
    parity = (iota((rows, BZ), 1) % 2).astype(f32)
    for x in range(HX):
        for y in range(HY):
            at = (x * HY + y) * LANES
            spots = place[:, 0, :, at : at + LANES].reshape(rows, LANES).astype(f32).astype(bf16)
            wide = jnp.dot(spots, table, preferred_element_type=f32) - parity
            for dx in range(2):
                for dy in range(2):
                    to = ((2 * x + dx) * BY + 2 * y + dy) * BZ
                    on = mask[:, 0, :, to : to + BZ].reshape(rows, BZ) == 1
                    hit = on & (wide == 4.0 * dx + 2.0 * dy)
                    chosen[:, to : to + BZ] = jnp.where(hit, 1.0, 0.0).astype(bf16)
    flat_weights[...] = jnp.concatenate([weights[o] for o in range(27)], axis=1)


def main(samples, scale_one, scale_two, where, n_vp, n_edge, n_x, n_y, *refs):
    vps, refs = refs[:n_vp], refs[n_vp:]
    edges, refs = refs[:n_edge], refs[n_edge:]
    xs, refs = refs[:n_x], refs[n_x:]
    ys, refs = refs[:n_y], refs[n_y:]
    own, pooled, chosen, weights, out, sums, fields, conv_one, ahead = refs
    rows = samples * C_TWO
    lane_z = iota((C_TWO, LANES), 1)
    width = 3 * QY * LANES
    k = iota((2 * LANES, width), 0)
    j = iota((2 * LANES, width), 1)
    shift = j // (QY * LANES) - 1
    qy = (j // LANES) % QY
    z = j % LANES - shift
    inside = (z >= 0) & (z < LANES)
    window = qy * QZ + z // 2
    beyond = LANES + qy * 2 + (z < 0).astype(i32)
    tables = []
    for s in range(samples):
        tables.append(
            [
                (k == jnp.where(inside, window, beyond + (8 * s + 4 * t))).astype(bf16)
                for t in range(2)
            ]
        )
    parity = [((lane_z - oz) & 1).astype(f32) for oz in OFFS]
    first = iota((C_TWO, LANES), 1) < 0
    for a, nx in enumerate(OFFS):
        for b, ny in enumerate(OFFS):
            vp = vps[where["vp"][nx, ny]]
            low, high = (edges[where["edge"][nx, ny, nz]] for nz in (-1, 1))
            if low is high:
                edge = low[0:C_TWO]
            else:
                edge = jnp.where(lane_z % 2 == 1, low[0:C_TWO].astype(f32), high[0:C_TWO].astype(f32)).astype(bf16)
            for s in range(samples):
                at = s * C_TWO
                v = jnp.concatenate([vp[at : at + C_TWO], edge], axis=1)
                p = jnp.concatenate([vp[rows + at : rows + at + C_TWO], edge], axis=1)
                v = jnp.dot(v, tables[s][0], preferred_element_type=f32)
                p = jnp.dot(p, tables[s][1], preferred_element_type=f32)
                for x in {-1: (HX - 1,), 0: range(HX), 1: (0,)}[nx]:
                    for y in {-1: (HY - 1,), 0: range(HY), 1: (0,)}[ny]:
                        px, py = x + 1 + nx * HX, y + 1 + ny * HY
                        to = (px * (HY + 2) + py) * LANES
                        for i in range(3):
                            at_z = (i * QY + y // 2) * LANES
                            hit = p[:, at_z : at_z + LANES] - parity[i] == 4.0 * (x % 2) + 2.0 * (y % 2)
                            fields[s, i * C_TWO : (i + 1) * C_TWO, to : to + LANES] = jnp.where(
                                hit, v[:, at_z : at_z + LANES], 0.0
                            ).astype(bf16)
    line = HY * HZ
    grad_two = jnp.zeros((C_ONE, GRAD_W_TWO), f32)
    results = []
    for s in range(samples):
        parts = []
        for x in range(HX):
            behind = []
            for ox in OFFS:
                for oy in OFFS:
                    at = ((x + 1 - ox) * (HY + 2) + 1 - oy) * LANES
                    behind.append(fields[s, :, at : at + line])
            behind = jnp.concatenate(behind, axis=0)
            got = jnp.dot(weights[...], behind, preferred_element_type=f32).astype(bf16)
            out[s, 0, :, x * line : (x + 1) * line] = got
            parts.append(got)
            grad_two = grad_two + lax.dot_general(
                pooled[s, 0, :, x * line : (x + 1) * line], behind, NT, preferred_element_type=f32
            )
        results.append(jnp.concatenate(parts, axis=1))
    sums[:, 0:GRAD_W_TWO] = grad_two * scale_two
    sums[:, GRAD_W_TWO:ONE_AT] = jnp.zeros((C_ONE, ONE_AT - GRAD_W_TWO), f32)
    grad_pooled = jnp.concatenate(results, axis=0)
    table = doubling()
    for x in range(HX):
        for y in range(HY):
            at = (x * HY + y) * LANES
            wide = jnp.dot(grad_pooled[:, at : at + LANES], table, preferred_element_type=f32).astype(bf16)
            for dx in range(2):
                for dy in range(2):
                    to = ((2 * x + dx) * BY + 2 * y + dy) * BZ
                    conv_one[:, to : to + BZ] = wide * chosen[:, to : to + BZ]
    lane = iota((PACK, BZ), 1)
    plane = BY * BZ
    for px in range(BX + 2):
        nx = -1 if px == 0 else 1 if px == BX + 1 else 0
        x = (px - 1) % BX
        for py in range(BY + 2):
            ny = -1 if py == 0 else 1 if py == BY + 1 else 0
            y = (py - 1) % BY
            far_y = 0 if y == 0 else 1
            if ny == 0 and nx == 0:
                row = own[:, (x * BY + y) * BZ : (x * BY + y + 1) * BZ]
            elif ny == 0:
                at = (0 if x == 0 else 1) * plane + y * BZ
                row = xs[where["x"][nx]][:, at : at + BZ]
            else:
                at = ((2 if x >= 2 else 0) + far_y) * BZ
                row = ys[where["y"][nx, ny, x in (0, BX - 1)]][:, at : at + BZ]
            row = row.astype(f32)
            below = edges[where["edge"][nx, ny, -1]][C_TWO : C_TWO + PACK].astype(f32)
            above = edges[where["edge"][nx, ny, 1]][C_TWO : C_TWO + PACK].astype(f32)
            at = 2 * (x * BY + y)
            to = (px * (BY + 2) + py) * BZ
            before = jnp.where(lane == 0, below[:, at + 1 : at + 2], pltpu.roll(row, 1, 1))
            after = jnp.where(lane == BZ - 1, above[:, at : at + 1], pltpu.roll(row, BZ - 1, 1))
            for i, piece in enumerate((before, row, after)):
                ahead[i * PACK : (i + 1) * PACK, to : to + BZ] = piece.astype(bf16)
    rows_one = samples * C_ONE
    count = 27 * PACK
    product = jnp.zeros((rows_one, count), f32)
    for x in range(BX):
        pieces = []
        for ox in OFFS:
            for oy in OFFS:
                at = ((x + 1 + ox) * (BY + 2) + 1 + oy) * BZ
                pieces.append(ahead[:, at : at + plane])
        product = product + lax.dot_general(
            conv_one[:, x * plane : (x + 1) * plane],
            jnp.concatenate(pieces, axis=0),
            NT,
            preferred_element_type=f32,
        )
    sample_of = (iota((C_ONE, count), 1) % PACK) // C_IN
    folded = jnp.zeros((C_ONE, count), f32)
    for s in range(samples):
        folded = folded + jnp.where(sample_of == s, product[s * C_ONE : (s + 1) * C_ONE], 0.0)
    k = iota((count, LANES), 0)
    fold = ((k // PACK) * C_IN + k % C_IN == iota((count, LANES), 1)).astype(f32)
    sums[:, ONE_AT:] = (
        jnp.dot(folded, fold, preferred_element_type=f32, precision=lax.Precision.HIGHEST) * scale_one
    )


def finish(mine, theirs, grad_one, grad_two):
    total = mine[...] + theirs[...]
    for o in range(27):
        grad_two[o] = total[:, o * C_TWO : (o + 1) * C_TWO]
    turned = total[:, ONE_AT:].T
    for o in range(27):
        grad_one[o] = turned[o * C_IN : (o + 1) * C_IN]


def call(body, shapes, operands, scratch=(), flops=0, moved=0):
    return pl.pallas_call(
        body,
        out_shape=shapes,
        in_specs=[pl.BlockSpec(memory_space=pltpu.VMEM)] * len(operands),
        out_specs=jax.tree.map(lambda _: pl.BlockSpec(memory_space=pltpu.VMEM), shapes),
        scratch_shapes=list(scratch),
        compiler_params=pltpu.CompilerParams(vmem_limit_bytes=32 * 2**20),
        cost_estimate=pl.CostEstimate(flops=flops, bytes_accessed=moved, transcendentals=0),
    )(*operands)


def block_side(blocks):
    return min(k for k in range(1, blocks + 1) if k * k * k >= blocks)


def neighbour(array, side, stride, of):
    blocks = lax.axis_size("space")
    pairs = []
    for i in range(blocks):
        c = i // stride % side
        pairs.append((i + ((c + of) % side - c) * stride, i))
    return lax.ppermute(array, "space", pairs)


def both_sides(array, side, stride):
    below = neighbour(array, side, stride, -1)
    return {-1: below, 1: below if side == 2 else neighbour(array, side, stride, 1)}


def swapped(array, axis, bit):
    size = lax.axis_size(axis)
    return lax.ppermute(array, axis, [(i, i ^ bit) for i in range(size)])


def local(inputs, mask_one, place_one, pooled_one, w_two, mask_two, place_two, grad_two):
    blocks = lax.axis_size("space")
    side = block_side(blocks)
    samples = inputs.shape[0]
    cells = inputs.shape[3]
    half_cells = HX * HY * HZ
    shape = jax.ShapeDtypeStruct
    vp, edge, own, faces_x, ends_y, mids_y = call(
        functools.partial(prepare, samples),
        (
            shape((2 * samples * C_TWO, LANES), bf16),
            shape((C_TWO + PACK, LANES), bf16),
            shape((PACK, cells), bf16),
            shape((PACK, 2 * BY * BZ), bf16),
            shape((PACK, 4 * BZ), bf16),
            shape((PACK, 4 * BZ), bf16),
        ),
        (grad_two, place_two, mask_two, inputs),
        flops=2 * 10**7,
        moved=2**20,
    )
    chosen, flat_weights = call(
        functools.partial(select_one, samples),
        (shape((samples * C_ONE, cells), bf16), shape((C_ONE, 27 * C_TWO), bf16)),
        (place_one, mask_one, w_two),
        flops=2 * 10**7,
        moved=3 * 2**20,
    )
    edge_z = both_sides(edge, side, 1)
    vp_at = {(0, 0): vp}
    edge_at = {(0, 0, n): edge_z[n] for n in (-1, 1)}
    for n, got in both_sides(vp, side, side * side).items():
        vp_at[n, 0] = got
    for nz in (-1, 1):
        if nz == 1 and side == 2:
            for n in (-1, 1):
                edge_at[n, 0, 1] = edge_at[n, 0, -1]
            continue
        for n, got in both_sides(edge_z[nz], side, side * side).items():
            edge_at[n, 0, nz] = got
    ends_at = {(0, n): got for n, got in both_sides(ends_y, side, side).items()}
    mids_at = {(0, n): got for n, got in both_sides(mids_y, side, side).items()}
    for nx in OFFS:
        if nx == 1 and side == 2:
            for n in (-1, 1):
                vp_at[1, n] = vp_at[-1, n]
            continue
        for n, got in both_sides(vp_at[nx, 0], side, side).items():
            vp_at[nx, n] = got
    for nx in OFFS:
        for nz in (-1, 1):
            for n in (-1, 1):
                if side == 2 and (nx == 1 or nz == 1):
                    edge_at[nx, n, nz] = edge_at[-abs(nx), n, -1]
            if side == 2 and (nx == 1 or nz == 1):
                continue
            for n, got in both_sides(edge_at[nx, 0, nz], side, side).items():
                edge_at[nx, n, nz] = got
    faces_at = both_sides(faces_x, side, side * side)
    for ny in (-1, 1):
        if ny == 1 and side == 2:
            for n in (-1, 1):
                ends_at[n, 1] = ends_at[n, -1]
            continue
        for n, got in both_sides(ends_at[0, ny], side, side * side).items():
            ends_at[n, ny] = got

    def distinct(table):
        arrays, places = [], {}
        for key, array in table.items():
            found = [i for i, a in enumerate(arrays) if a is array]
            if not found:
                arrays.append(array)
            places[key] = found[0] if found else len(arrays) - 1
        return arrays, places

    y_at = {(nx, ny, True): a for (nx, ny), a in ends_at.items()}
    y_at.update({(nx, ny, False): a for (nx, ny), a in mids_at.items()})
    vps, where_vp = distinct(vp_at)
    edges, where_edge = distinct(edge_at)
    xs, where_x = distinct(faces_at)
    ys, where_y = distinct(y_at)
    where = {"vp": where_vp, "edge": where_edge, "x": where_x, "y": where_y}
    total = lax.axis_size("dp") * samples * blocks * cells
    body = functools.partial(
        main,
        samples,
        float(total) ** -0.5,
        float(total // 8) ** -0.5,
        where,
        len(vps),
        len(edges),
        len(xs),
        len(ys),
    )
    grad_pooled, sums = call(
        body,
        (shape((samples, 1, C_ONE, half_cells), bf16), shape((C_ONE, WIDTH), f32)),
        (*vps, *edges, *xs, *ys, own, pooled_one, chosen, flat_weights),
        scratch=(
            pltpu.VMEM((samples, 3 * C_TWO, (HX + 2) * (HY + 2) * HZ), bf16),
            pltpu.VMEM((samples * C_ONE, cells), bf16),
            pltpu.VMEM((3 * PACK, (BX + 2) * (BY + 2) * BZ), bf16),
        ),
        flops=10**9,
        moved=3 * 2**20,
    )
    steps = []
    for axis in ("dp", "space"):
        bit = 1
        while bit < lax.axis_size(axis):
            steps.append((axis, bit))
            bit *= 2
    for axis, bit in steps[:-1]:
        sums = sums + swapped(sums, axis, bit)
    grad_w_one, grad_w_two = call(
        finish,
        (shape((27, C_IN, C_ONE), f32), shape((27, C_ONE, C_TWO), f32)),
        (sums, swapped(sums, *steps[-1])),
    )
    return grad_pooled, grad_w_one, grad_w_two


def solution(mesh):
    split = P("dp", "space", None, None)
    return jax.shard_map(
        local,
        mesh=mesh,
        in_specs=(split, split, split, split, P(), split, split, split),
        out_specs=(split, P(), P()),
        check_vma=False,
    )
```

```python
import functools

import jax
import jax.numpy as jnp
from jax import lax
from jax.experimental import pallas as pl
from jax.experimental.pallas import tpu as pltpu
from jax.sharding import PartitionSpec as P

C_IN = 4
C_ONE = 16
C_TWO = 32
BX = 4
BY = 8
BZ = 256
HX, HY, HZ = BX // 2, BY // 2, BZ // 2
QY, QZ = HY // 2, HZ // 2
LANES = 128
PACK = 16
EDGE = C_TWO + PACK
OFFS = (-1, 0, 1)
GRAD_W_TWO = 27 * C_TWO
WIDTH = 1024
ONE_AT = WIDTH - LANES
STRIDE_ONE = LANES // C_IN
TABLE = 3 * QY * LANES
NT = (((1,), (1,)), ((), ()))
f32, bf16, i32 = jnp.float32, jnp.bfloat16, jnp.int32


def iota(shape, dim):
    return lax.broadcasted_iota(i32, shape, dim)


def doubling():
    return (iota((LANES, 2 * LANES), 0) == iota((LANES, 2 * LANES), 1) // 2).astype(bf16)


def fetch(pairs, sems):
    copies = [pltpu.make_async_copy(a, b, sems.at[i]) for i, (a, b) in enumerate(pairs)]
    for copy in copies:
        copy.start()
    return copies


def prepare(samples, *refs):
    far, (to_x, to_y, own), near, sems = refs[:4], refs[4:7], refs[7:11], refs[11]
    grad, place, mask, source = near
    copies = fetch(tuple(zip(far, near)), sems)
    rows = samples * C_TWO
    table = doubling()
    copies[0].wait()
    copies[1].wait()
    values = jnp.dot(grad[...].reshape(rows, LANES), table, preferred_element_type=f32)
    spots = place[...].reshape(rows, LANES).astype(f32).astype(bf16)
    wide = jnp.dot(spots, table, preferred_element_type=f32)
    parity = (iota((rows, LANES), 1) % 2).astype(f32)
    copies[2].wait()
    halves = []
    for qy in range(QY):
        v = values[:, qy * LANES : (qy + 1) * LANES]
        p = wide[:, qy * LANES : (qy + 1) * LANES] - parity
        total = jnp.zeros((rows, LANES), f32)
        for x in range(HX):
            for dy in range(2):
                at = (x * HY + 2 * qy + dy) * LANES
                on = mask[:, 0, :, at : at + LANES].reshape(rows, LANES) == 1
                total = total + jnp.where(on & (p == 4.0 * x + 2.0 * dy), v, 0.0)
        halves.append(total)
    kept = jnp.concatenate(halves, axis=1).astype(bf16)
    v = lax.dot_general(kept, table, NT, preferred_element_type=f32).astype(bf16)
    used = samples * C_IN
    for ref, at in ((to_x, BY * 4 * used), (to_y, 4 * 4 * used)):
        ref[at : at + rows] = v
        ref[at + rows : at + 2 * rows] = spots
    copies[3].wait()
    pieces = [source[s, 0].astype(f32) for s in range(samples)]
    if used < PACK:
        pieces.append(jnp.zeros((PACK - used, BX * BY * BZ), f32))
    cells = jnp.concatenate(pieces, axis=0)
    own[...] = cells.astype(bf16)
    for t in range(BY):
        group = []
        for x in (0, BX - 1):
            for y in (t // 2, BY - 1 - t // 2):
                at = (x * BY + y) * BZ + (t % 2) * LANES
                group.append(cells[0:used, at : at + LANES])
        to_x[4 * used * t : 4 * used * (t + 1)] = jnp.concatenate(group, axis=0).astype(bf16)
    for t in range(4):
        group = []
        for x in range(BX):
            at = (x * BY + (BY - 1) * (t // 2)) * BZ + (t % 2) * LANES
            group.append(cells[0:used, at : at + LANES])
        to_y[4 * used * t : 4 * used * (t + 1)] = jnp.concatenate(group, axis=0).astype(bf16)


def ends(samples, vp_row, to_x, own, edge):
    rows = samples * C_TWO
    lane = iota((LANES, LANES), 0)
    spot = (lane // QZ) * 2 + (lane % QZ == QZ - 1).astype(i32)
    spot = jnp.where((lane % QZ == 0) | (lane % QZ == QZ - 1), spot, -LANES)
    column = iota((LANES, LANES), 1)
    packed = jnp.zeros((C_TWO, LANES), f32)
    for s in range(samples):
        for t in range(2):
            pick = (spot + (8 * s + 4 * t) == column).astype(bf16)
            at = vp_row + t * rows + s * C_TWO
            packed = packed + jnp.dot(to_x[at : at + C_TWO], pick, preferred_element_type=f32)
    edge[0:C_TWO] = packed.astype(bf16)
    lane = iota((PACK, LANES), 1)
    packed = jnp.zeros((PACK, LANES), f32)
    for row in range(BX * BY):
        left = own[:, row * BZ : row * BZ + LANES].astype(f32)
        right = own[:, (row + 1) * BZ - LANES : (row + 1) * BZ].astype(f32)
        packed = jnp.where(lane == 2 * row, left[:, 0:1], packed)
        packed = jnp.where(lane == 2 * row + 1, right[:, LANES - 1 :], packed)
    edge[C_TWO:EDGE] = packed.astype(bf16)


def select_one(samples, *refs):
    far, (chosen, flat_weights, expand), near, sems = refs[:3], refs[3:6], refs[6:9], refs[9]
    place, mask, weights = near
    copies = fetch(tuple(zip(far, near)), sems)
    k = iota((2 * LANES, TABLE), 0)
    j = iota((1, TABLE), 1)
    shift = j // (QY * LANES) - 1
    qy = (j // LANES) % QY
    z = j % LANES - shift
    beyond = LANES + qy * 2 + (z < 0).astype(i32)
    expand[...] = (k == jnp.where((z >= 0) & (z < LANES), qy * QZ + z // 2, beyond)).astype(bf16)
    rows = samples * C_ONE
    table = doubling()
    parity = (iota((rows, BZ), 1) % 2).astype(f32)
    copies[2].wait()
    flat_weights[...] = jnp.concatenate([weights[o] for o in range(27)], axis=1)
    copies[0].wait()
    copies[1].wait()
    for x in range(HX):
        for y in range(HY):
            at = (x * HY + y) * LANES
            spots = place[:, 0, :, at : at + LANES].reshape(rows, LANES).astype(f32).astype(bf16)
            wide = jnp.dot(spots, table, preferred_element_type=f32) - parity
            for dx in range(2):
                for dy in range(2):
                    to = ((2 * x + dx) * BY + 2 * y + dy) * BZ
                    on = mask[:, 0, :, to : to + BZ].reshape(rows, BZ) == 1
                    hit = on & (wide == 4.0 * dx + 2.0 * dy)
                    chosen[:, to : to + BZ] = jnp.where(hit, 1.0, 0.0).astype(bf16)


def layer_two(samples, scale, vp_at, edge_at, *refs):
    blocks, (pooled, weights, expand, out, kept, sums, fields) = refs[:-7], refs[-7:]
    rows = samples * C_TWO
    parity_lane = iota((rows, LANES), 1)
    odd = iota((C_TWO, LANES), 1) % 2 == 1
    groups = {}
    for nx in OFFS:
        for ny in OFFS:
            key = (vp_at[nx, ny], edge_at[nx, ny, -1], edge_at[nx, ny, 1])
            groups.setdefault(key, []).append((nx, ny))
    for ((ref, at), low, high), places in groups.items():
        edge = blocks[low[0]][low[1] : low[1] + C_TWO].astype(f32)
        if low != high:
            other = blocks[high[0]][high[1] : high[1] + C_TWO].astype(f32)
            edge = jnp.where(odd, edge, other)
        parts = []
        for t in range(2):
            for s in range(samples):
                by = 8 * s + 4 * t
                parts.append(pltpu.roll(edge, LANES - by, 1) if by else edge)
        both = jnp.concatenate(
            [blocks[ref][at : at + 2 * rows], jnp.concatenate(parts, axis=0).astype(bf16)], axis=1
        )
        wide = jnp.dot(both, expand[...], preferred_element_type=f32)
        for i, oz in enumerate(OFFS):
            parity = ((parity_lane - oz) & 1).astype(f32)
            for qy in range(QY):
                lanes = slice((i * QY + qy) * LANES, (i * QY + qy + 1) * LANES)
                v = wide[0:rows, lanes].astype(bf16)
                p = (wide[rows : 2 * rows, lanes] - parity).astype(bf16)
                for x in range(HX):
                    for dy in range(2):
                        y = 2 * qy + dy
                        spots = []
                        for nx, ny in places:
                            near_x = nx == 0 or x == (HX - 1 if nx < 0 else 0)
                            near_y = ny == 0 or y == (HY - 1 if ny < 0 else 0)
                            if near_x and near_y:
                                spots.append((x + 1 + nx * HX) * (HY + 2) + y + 1 + ny * HY)
                        if not spots:
                            continue
                        cells = jnp.where(p == 4.0 * x + 2.0 * dy, v, jnp.zeros_like(v))
                        for spot in spots:
                            for s in range(samples):
                                fields[s, i * C_TWO : (i + 1) * C_TWO, spot * LANES : (spot + 1) * LANES] = (
                                    cells[s * C_TWO : (s + 1) * C_TWO]
                                )
    line = HY * HZ
    total = jnp.zeros((C_ONE, GRAD_W_TWO), f32)
    for s in range(samples):
        for x in range(HX):
            behind = []
            for ox in OFFS:
                for oy in OFFS:
                    at = ((x + 1 - ox) * (HY + 2) + 1 - oy) * LANES
                    behind.append(fields[s, :, at : at + line])
            behind = jnp.concatenate(behind, axis=0)
            got = jnp.dot(weights[...], behind, preferred_element_type=f32)
            got = got.astype(bf16)
            out[s, 0, :, x * line : (x + 1) * line] = got
            kept[s * C_ONE : (s + 1) * C_ONE, x * line : (x + 1) * line] = got
            total = total + lax.dot_general(
                pooled[s, 0, :, x * line : (x + 1) * line], behind, NT, preferred_element_type=f32
            )
    sums[:, 0:GRAD_W_TWO] = total * scale
    sums[:, GRAD_W_TWO:ONE_AT] = jnp.zeros((C_ONE, ONE_AT - GRAD_W_TWO), f32)


def layer_one(samples, scale, face_at, line_at, edge_at, *refs):
    blocks, (own, grad, chosen, before_sums, sums, conv_one, ahead) = refs[:-7], refs[-7:]
    used = samples * C_IN
    sums[:, 0:ONE_AT] = before_sums[...]
    lane = iota((PACK, BZ), 1)
    plane = BY * BZ
    for px in range(BX + 2):
        nx = -1 if px == 0 else 1 if px == BX + 1 else 0
        x = (px - 1) % BX
        for py in range(BY + 2):
            ny = -1 if py == 0 else 1 if py == BY + 1 else 0
            y = (py - 1) % BY
            if nx == 0 and ny == 0:
                row = own[:, (x * BY + y) * BZ : (x * BY + y + 1) * BZ].astype(f32)
            else:
                if ny == 0 or nx != 0:
                    ref, at = face_at[nx] if ny == 0 else line_at[nx, ny]
                    tile = 2 * min(y, BY - 1 - y)
                    chunk = 2 * (0 if x == 0 else 1) + (1 if y >= BY // 2 else 0)
                else:
                    ref, at = line_at[nx, ny]
                    tile = 2 * (0 if y == 0 else 1)
                    chunk = x
                halves = []
                for t in (tile, tile + 1):
                    four = blocks[ref][at + 4 * used * t : at + 4 * used * (t + 1)].astype(f32)
                    halves.append(four[chunk * used : (chunk + 1) * used])
                row = jnp.concatenate(halves, axis=1)
                if used < PACK:
                    row = jnp.concatenate([row, jnp.zeros((PACK - used, BZ), f32)], axis=0)
            ends = []
            for nz in (-1, 1):
                ref, at = edge_at[nx, ny, nz]
                ends.append(blocks[ref][at + C_TWO : at + EDGE].astype(f32))
            at = 2 * (x * BY + y)
            to = (px * (BY + 2) + py) * BZ
            before = jnp.where(lane == 0, ends[0][:, at + 1 : at + 2], pltpu.roll(row, 1, 1))
            after = jnp.where(lane == BZ - 1, ends[1][:, at : at + 1], pltpu.roll(row, BZ - 1, 1))
            for i, piece in enumerate((before, row, after)):
                ahead[i * PACK : (i + 1) * PACK, to : to + BZ] = piece.astype(bf16)
    table = doubling()
    line = HY * HZ
    for x in range(HX):
        for y in range(HY):
            at = x * line + y * LANES
            wide = jnp.dot(grad[:, at : at + LANES], table, preferred_element_type=f32).astype(bf16)
            for dx in range(2):
                for dy in range(2):
                    to = ((2 * x + dx) * BY + 2 * y + dy) * BZ
                    conv_one[:, to : to + BZ] = wide * chosen[:, to : to + BZ]
    rows = samples * C_ONE
    count = 27 * PACK
    product = jnp.zeros((rows, count), f32)
    for x in range(BX):
        pieces = []
        for ox in OFFS:
            for oy in OFFS:
                at = ((x + 1 + ox) * (BY + 2) + 1 + oy) * BZ
                pieces.append(ahead[:, at : at + plane])
        product = product + lax.dot_general(
            conv_one[:, x * plane : (x + 1) * plane],
            jnp.concatenate(pieces, axis=0),
            NT,
            preferred_element_type=f32,
        )
    sample_of = (iota((C_ONE, count), 1) % PACK) // C_IN
    folded = jnp.zeros((C_ONE, count), f32)
    for s in range(samples):
        folded = folded + jnp.where(sample_of == s, product[s * C_ONE : (s + 1) * C_ONE], 0.0)
    k = iota((count, LANES), 0)
    fold = ((k % C_IN) * STRIDE_ONE + k // PACK == iota((count, LANES), 1)).astype(f32)
    sums[:, ONE_AT:] = (
        jnp.dot(folded, fold, preferred_element_type=f32, precision=lax.Precision.HIGHEST) * scale
    )


def finish(mine, theirs, grad_one, grad_two):
    total = mine[...] + theirs[...]
    for o in range(27):
        grad_two[o] = total[:, o * C_TWO : (o + 1) * C_TWO]
    for c in range(C_IN):
        at = ONE_AT + c * STRIDE_ONE
        grad_one[c] = total[:, at : at + 27]


def call(body, shapes, operands, far=False, scratch=(), flops=0, moved=0):
    space = pltpu.HBM if far else pltpu.VMEM
    if far:
        scratch = [pltpu.VMEM(a.shape, a.dtype) for a in operands]
        scratch.append(pltpu.SemaphoreType.DMA((len(operands),)))
        operands = [pltpu.with_memory_space_constraint(a, pltpu.HBM) for a in operands]
    return pl.pallas_call(
        body,
        out_shape=shapes,
        in_specs=[pl.BlockSpec(memory_space=space)] * len(operands),
        out_specs=jax.tree.map(lambda _: pl.BlockSpec(memory_space=pltpu.VMEM), shapes),
        scratch_shapes=list(scratch),
        compiler_params=pltpu.CompilerParams(vmem_limit_bytes=32 * 2**20),
        cost_estimate=pl.CostEstimate(flops=flops, bytes_accessed=moved, transcendentals=0),
    )(*operands)


def block_side(blocks):
    return min(k for k in range(1, blocks + 1) if k * k * k >= blocks)


def neighbour(array, side, stride, of):
    blocks = lax.axis_size("space")
    pairs = []
    for i in range(blocks):
        c = i // stride % side
        pairs.append((i + ((c + of) % side - c) * stride, i))
    return lax.ppermute(array, "space", pairs)


def both_sides(array, side, stride):
    below = neighbour(array, side, stride, -1)
    return {-1: below, 1: below if side == 2 else neighbour(array, side, stride, 1)}


def swapped(array, axis, bit):
    size = lax.axis_size(axis)
    return lax.ppermute(array, axis, [(i, i ^ bit) for i in range(size)])


def stacked(parts):
    kept, starts, places = [], [], []
    rows = 0
    for part in parts:
        found = [i for i, a in enumerate(kept) if a is part]
        if not found:
            found = [len(kept)]
            kept.append(part)
            starts.append(rows)
            rows += part.shape[0]
        places.append(starts[found[0]])
    return jnp.concatenate(kept, axis=0), places


def operands_of(*tables):
    arrays, numbered = [], []
    for table in tables:
        new = {}
        for key, (array, row) in table.items():
            found = [i for i, a in enumerate(arrays) if a is array]
            if not found:
                found = [len(arrays)]
                arrays.append(array)
            new[key] = (found[0], row)
        numbered.append(new)
    return arrays, numbered


def local(inputs, mask_one, place_one, pooled_one, w_two, mask_two, place_two, grad_two):
    blocks = lax.axis_size("space")
    side = block_side(blocks)
    samples = inputs.shape[0]
    cells = inputs.shape[3]
    half_cells = HX * HY * HZ
    shape = jax.ShapeDtypeStruct
    vp_rows = 2 * samples * C_TWO
    four = 4 * samples * C_IN
    vp_row = BY * four
    to_x, to_y, own = call(
        functools.partial(prepare, samples),
        (
            shape((BY * four + vp_rows, LANES), bf16),
            shape((4 * four + vp_rows, LANES), bf16),
            shape((PACK, cells), bf16),
        ),
        (grad_two, place_two, mask_two, inputs),
        far=True,
        flops=2 * 10**7,
        moved=2**20,
    )
    edge = call(
        functools.partial(ends, samples, vp_row),
        shape((EDGE, LANES), bf16),
        (to_x, own),
        flops=10**7,
        moved=2**19,
    )
    chosen, flat_weights, expand = call(
        functools.partial(select_one, samples),
        (
            shape((samples * C_ONE, cells), bf16),
            shape((C_ONE, 27 * C_TWO), bf16),
            shape((2 * LANES, TABLE), bf16),
        ),
        (place_one, mask_one, w_two),
        far=True,
        flops=2 * 10**7,
        moved=3 * 2**20,
    )
    vp_at, edge_at, face_at, line_at = {(0, 0): (to_x, vp_row)}, {}, {}, {}
    from_x = both_sides(to_x, side, side * side)
    edge_z = both_sides(edge, side, 1)
    edge_x = {-1: both_sides(edge_z[-1], side, side * side)}
    edge_x[1] = edge_x[-1] if side == 2 else both_sides(edge_z[1], side, side * side)
    first = both_sides(to_y, side, side)
    parts = []
    for n in (-1, 1):
        again = n == 1 and side == 2
        parts += parts[:2] if again else [from_x[n][vp_row:], from_x[n][: 2 * four]]
    parts += [edge_z[-1], edge_z[1]] + [edge_x[nz][nx] for nz in (-1, 1) for nx in (-1, 1)]
    second, starts = stacked(parts)
    second = both_sides(second, side, side)
    for n in (-1, 1):
        vp_at[n, 0] = (from_x[n], vp_row)
        face_at[n] = (from_x[n], 0)
        vp_at[0, n] = (first[n], 4 * four)
        line_at[0, n] = (first[n], 0)
        edge_at[0, 0, n] = (edge_z[n], 0)
        for i, nx in enumerate((-1, 1)):
            edge_at[nx, 0, n] = (edge_x[n][nx], 0)
            vp_at[nx, n] = (second[n], starts[2 * i])
            line_at[nx, n] = (second[n], starts[2 * i + 1])
        for i, nz in enumerate((-1, 1)):
            edge_at[0, n, nz] = (second[n], starts[4 + i])
            for j, nx in enumerate((-1, 1)):
                edge_at[nx, n, nz] = (second[n], starts[6 + 2 * i + j])
    total = lax.axis_size("dp") * samples * blocks * cells
    arrays, tables = operands_of(vp_at, edge_at)
    grad_pooled, kept, sums = call(
        functools.partial(layer_two, samples, float(total // 8) ** -0.5, *tables),
        (
            shape((samples, 1, C_ONE, half_cells), bf16),
            shape((samples * C_ONE, half_cells), bf16),
            shape((C_ONE, ONE_AT), f32),
        ),
        (*arrays, pooled_one, flat_weights, expand),
        scratch=(pltpu.VMEM((samples, 3 * C_TWO, (HX + 2) * (HY + 2) * HZ), bf16),),
        flops=5 * 10**8,
        moved=2**20,
    )
    arrays, tables = operands_of(face_at, line_at, edge_at)
    sums = call(
        functools.partial(layer_one, samples, float(total) ** -0.5, *tables),
        shape((C_ONE, WIDTH), f32),
        (*arrays, own, kept, chosen, sums),
        scratch=(
            pltpu.VMEM((samples * C_ONE, cells), bf16),
            pltpu.VMEM((3 * PACK, (BX + 2) * (BY + 2) * BZ), bf16),
        ),
        flops=5 * 10**8,
        moved=2**20,
    )
    steps = []
    for axis in ("dp", "space"):
        bit = 1
        while bit < lax.axis_size(axis):
            steps.append((axis, bit))
            bit *= 2
    for axis, bit in steps[:-1]:
        sums = sums + swapped(sums, axis, bit)
    grad_w_one, grad_w_two = call(
        finish,
        (shape((C_IN, C_ONE, 27), f32), shape((27, C_ONE, C_TWO), f32)),
        (sums, swapped(sums, *steps[-1])),
    )
    return grad_pooled, jnp.transpose(grad_w_one, (2, 0, 1)), grad_w_two


def solution(mesh):
    split = P("dp", "space", None, None)
    return jax.shard_map(
        local,
        mesh=mesh,
        in_specs=(split, split, split, split, P(), split, split, split),
        out_specs=(split, P(), P()),
        check_vma=False,
    )
```

```python
import functools

import jax
import jax.numpy as jnp
from jax import lax
from jax.experimental import pallas as pl
from jax.experimental.pallas import tpu as pltpu
from jax.sharding import PartitionSpec as P

C_IN = 4
C_ONE = 16
C_TWO = 32
BX = 4
BY = 8
BZ = 256
HX, HY, HZ = BX // 2, BY // 2, BZ // 2
QY, QZ = HY // 2, HZ // 2
LANES = 128
PACK = 16
EDGE = C_TWO + PACK
OFFS = (-1, 0, 1)
GRAD_W_TWO = 27 * C_TWO
WIDTH = 1024
ONE_AT = WIDTH - LANES
STRIDE_ONE = LANES // C_IN
TABLE = 3 * QY * LANES
NT = (((1,), (1,)), ((), ()))
f32, bf16, i32 = jnp.float32, jnp.bfloat16, jnp.int32


def iota(shape, dim):
    return lax.broadcasted_iota(i32, shape, dim)


def doubling():
    return (iota((LANES, 2 * LANES), 0) == iota((LANES, 2 * LANES), 1) // 2).astype(bf16)


def fetch(pairs, sems):
    copies = [pltpu.make_async_copy(a, b, sems.at[i]) for i, (a, b) in enumerate(pairs)]
    for copy in copies:
        copy.start()
    return copies


def prepare(samples, *refs):
    far, (to_x, own), near, sems = refs[:4], refs[4:6], refs[6:10], refs[10]
    grad, place, mask, source = near
    copies = fetch(tuple(zip(far, near)), sems)
    rows = samples * C_TWO
    table = doubling()
    copies[0].wait()
    copies[1].wait()
    values = jnp.dot(grad[...].reshape(rows, LANES), table, preferred_element_type=f32)
    spots = place[...].reshape(rows, LANES).astype(f32).astype(bf16)
    wide = jnp.dot(spots, table, preferred_element_type=f32)
    parity = (iota((rows, LANES), 1) % 2).astype(f32)
    copies[2].wait()
    halves = []
    for qy in range(QY):
        v = values[:, qy * LANES : (qy + 1) * LANES]
        p = wide[:, qy * LANES : (qy + 1) * LANES] - parity
        total = jnp.zeros((rows, LANES), f32)
        for x in range(HX):
            for dy in range(2):
                at = (x * HY + 2 * qy + dy) * LANES
                on = mask[:, 0, :, at : at + LANES].reshape(rows, LANES) == 1
                total = total + jnp.where(on & (p == 4.0 * x + 2.0 * dy), v, 0.0)
        halves.append(total)
    kept = jnp.concatenate(halves, axis=1).astype(bf16)
    v = lax.dot_general(kept, table, NT, preferred_element_type=f32).astype(bf16)
    used = samples * C_IN
    at = BY * 4 * used
    to_x[at : at + rows] = v
    to_x[at + rows : at + 2 * rows] = spots
    copies[3].wait()
    pieces = [source[s, 0].astype(f32) for s in range(samples)]
    if used < PACK:
        pieces.append(jnp.zeros((PACK - used, BX * BY * BZ), f32))
    cells = jnp.concatenate(pieces, axis=0)
    own[...] = cells.astype(bf16)
    for t in range(BY):
        group = []
        for x in (0, BX - 1):
            for y in (t // 2, BY - 1 - t // 2):
                at = (x * BY + y) * BZ + (t % 2) * LANES
                group.append(cells[0:used, at : at + LANES])
        to_x[4 * used * t : 4 * used * (t + 1)] = jnp.concatenate(group, axis=0).astype(bf16)


def ends(samples, vp_row, to_x, own, edge):
    rows = samples * C_TWO
    lane = iota((LANES, LANES), 0)
    spot = (lane // QZ) * 2 + (lane % QZ == QZ - 1).astype(i32)
    spot = jnp.where((lane % QZ == 0) | (lane % QZ == QZ - 1), spot, -LANES)
    column = iota((LANES, LANES), 1)
    packed = jnp.zeros((C_TWO, LANES), f32)
    for s in range(samples):
        for t in range(2):
            pick = (spot + (8 * s + 4 * t) == column).astype(bf16)
            at = vp_row + t * rows + s * C_TWO
            packed = packed + jnp.dot(to_x[at : at + C_TWO], pick, preferred_element_type=f32)
    edge[0:C_TWO] = packed.astype(bf16)
    lane = iota((PACK, LANES), 1)
    packed = jnp.zeros((PACK, LANES), f32)
    for row in range(BX * BY):
        left = own[:, row * BZ : row * BZ + LANES].astype(f32)
        right = own[:, (row + 1) * BZ - LANES : (row + 1) * BZ].astype(f32)
        packed = jnp.where(lane == 2 * row, left[:, 0:1], packed)
        packed = jnp.where(lane == 2 * row + 1, right[:, LANES - 1 :], packed)
    edge[C_TWO:EDGE] = packed.astype(bf16)


def select_one(samples, vp_row, *refs):
    far, (to_x, own), (chosen, folded_weights, expand, to_y), near, sems = (
        refs[:3], refs[3:5], refs[5:9], refs[9:12], refs[12],
    )
    place, mask, weights = near
    copies = fetch(tuple(zip(far, near)), sems)
    used = samples * C_IN
    to_y[4 * 4 * used :] = to_x[vp_row:]
    for t in range(4):
        group = []
        for x in range(BX):
            at = (x * BY + (BY - 1) * (t // 2)) * BZ + (t % 2) * LANES
            group.append(own[:, at : at + LANES].astype(f32)[0:used])
        to_y[4 * used * t : 4 * used * (t + 1)] = jnp.concatenate(group, axis=0).astype(bf16)
    k = iota((2 * LANES, TABLE), 0)
    j = iota((1, TABLE), 1)
    shift = j // (QY * LANES) - 1
    qy = (j // LANES) % QY
    z = j % LANES - shift
    beyond = LANES + qy * 2 + (z < 0).astype(i32)
    expand[...] = (k == jnp.where((z >= 0) & (z < LANES), qy * QZ + z // 2, beyond)).astype(bf16)
    rows = samples * C_ONE
    table = doubling()
    parity = (iota((rows, BZ), 1) % 2).astype(f32)
    copies[2].wait()
    folded_weights[...] = jnp.concatenate(
        [jnp.concatenate([weights[3 * o + i] for i in range(3)], axis=1) for o in range(9)], axis=0
    )
    copies[0].wait()
    copies[1].wait()
    for x in range(HX):
        for y in range(HY):
            at = (x * HY + y) * LANES
            spots = place[:, 0, :, at : at + LANES].reshape(rows, LANES).astype(f32).astype(bf16)
            wide = jnp.dot(spots, table, preferred_element_type=f32) - parity
            for dx in range(2):
                for dy in range(2):
                    to = ((2 * x + dx) * BY + 2 * y + dy) * BZ
                    on = mask[:, 0, :, to : to + BZ].reshape(rows, BZ) == 1
                    hit = on & (wide == 4.0 * dx + 2.0 * dy)
                    chosen[:, to : to + BZ] = jnp.where(hit, 1.0, 0.0).astype(bf16)


def expand_windows(samples, vp_at, edge_at, ys, tile_of, blocks, expand, fields):
    rows = samples * C_TWO
    lane = iota((rows, LANES), 1)
    odd = iota((C_TWO, LANES), 1) % 2 == 1
    groups = {}
    for nx in OFFS:
        for ny in ys:
            key = (vp_at[nx, ny], edge_at[nx, ny, -1], edge_at[nx, ny, 1])
            groups.setdefault(key, []).append((nx, ny))
    for ((ref, at), low, high), places in groups.items():
        edge = blocks[low[0]][low[1] : low[1] + C_TWO].astype(f32)
        if low != high:
            other = blocks[high[0]][high[1] : high[1] + C_TWO].astype(f32)
            edge = jnp.where(odd, edge, other)
        parts = []
        for t in range(2):
            for s in range(samples):
                by = 8 * s + 4 * t
                parts.append(pltpu.roll(edge, LANES - by, 1) if by else edge)
        both = jnp.concatenate(
            [blocks[ref][at : at + 2 * rows], jnp.concatenate(parts, axis=0).astype(bf16)], axis=1
        )
        wide = jnp.dot(both, expand[...], preferred_element_type=f32)
        for i, oz in enumerate(OFFS):
            parity = ((lane - oz) & 1).astype(f32)
            for qy in range(QY):
                lanes = slice((i * QY + qy) * LANES, (i * QY + qy + 1) * LANES)
                v = wide[0:rows, lanes].astype(bf16)
                p = (wide[rows : 2 * rows, lanes] - parity).astype(bf16)
                for x in range(HX):
                    for dy in range(2):
                        y = 2 * qy + dy
                        spots = []
                        for nx, ny in places:
                            near_x = nx == 0 or x == (HX - 1 if nx < 0 else 0)
                            near_y = ny == 0 or y == (HY - 1 if ny < 0 else 0)
                            if near_x and near_y:
                                spots.append(tile_of[x + 1 + nx * HX, y + 1 + ny * HY])
                        if not spots:
                            continue
                        cells = jnp.where(p == 4.0 * x + 2.0 * dy, v, jnp.zeros_like(v))
                        for spot in spots:
                            for s in range(samples):
                                fields[s, i * C_TWO : (i + 1) * C_TWO, spot * LANES : (spot + 1) * LANES] = (
                                    cells[s * C_TWO : (s + 1) * C_TWO]
                                )


def tiles_inside():
    return {(px, py): px * HY + py - 1 for px in range(HX + 2) for py in range(1, HY + 1)}


def tiles_ends():
    return {(px, py): 2 * px + (py > 0) for px in range(HX + 2) for py in (0, HY + 1)}


def shift_pooled(samples, tile_of, pooled, moved):
    for (px, py), tile in tile_of.items():
        k = 0
        for ox in OFFS:
            for oy in OFFS:
                x, y = px - 1 + ox, py - 1 + oy
                inside = 0 <= x < HX and 0 <= y < HY
                for s in range(samples):
                    if inside:
                        at = (x * HY + y) * LANES
                        value = pooled[s, 0, :, at : at + LANES]
                    else:
                        value = jnp.zeros((C_ONE, LANES), bf16)
                    moved[s, k * C_ONE : (k + 1) * C_ONE, tile * LANES : (tile + 1) * LANES] = value
                k += 1


def products_two(samples, tile_of, fields, moved, weights, sums, totals):
    for s in range(samples):
        wide = jnp.dot(weights[...], fields[s], preferred_element_type=f32)
        for x in range(HX):
            for y in range(HY):
                k = 0
                for ox in OFFS:
                    for oy in OFFS:
                        tile = tile_of.get((x + 1 - ox, y + 1 - oy))
                        if tile is not None:
                            part = wide[k * C_ONE : (k + 1) * C_ONE, tile * LANES : (tile + 1) * LANES]
                            old = sums[s].get((x, y))
                            sums[s][x, y] = part if old is None else old + part
                        k += 1
        totals = totals + lax.dot_general(moved[s], fields[s], NT, preferred_element_type=f32)
    return totals


def layer_two_inside(samples, vp_at, edge_at, *refs):
    blocks, (pooled, weights, expand, part, total, moved_ends, fields, moved) = refs[:-8], refs[-8:]
    tile_of = tiles_inside()
    expand_windows(samples, vp_at, edge_at, (0,), tile_of, blocks, expand, fields)
    shift_pooled(samples, tile_of, pooled, moved)
    shift_pooled(samples, tiles_ends(), pooled, moved_ends)
    sums = [{} for _ in range(samples)]
    totals = jnp.zeros((9 * C_ONE, 3 * C_TWO), f32)
    total[...] = products_two(samples, tile_of, fields, moved, weights, sums, totals)
    for s in range(samples):
        for (x, y), value in sums[s].items():
            at = (x * HY + y) * LANES
            part[s * C_ONE : (s + 1) * C_ONE, at : at + LANES] = value


def layer_two_ends(samples, scale, vp_at, edge_at, *refs):
    blocks, (weights, expand, part, total, moved, out, kept, message, fields) = refs[:-9], refs[-9:]
    tile_of = tiles_ends()
    expand_windows(samples, vp_at, edge_at, (-1, 1), tile_of, blocks, expand, fields)
    sums = [
        {
            (x, y): part[s * C_ONE : (s + 1) * C_ONE, (x * HY + y) * LANES : (x * HY + y + 1) * LANES]
            for x in range(HX)
            for y in range(HY)
        }
        for s in range(samples)
    ]
    totals = products_two(samples, tile_of, fields, moved, weights, sums, total[...]) * scale
    for s in range(samples):
        for (x, y), value in sums[s].items():
            at = (x * HY + y) * LANES
            got = value.astype(bf16)
            out[s, 0, :, at : at + LANES] = got
            kept[s * C_ONE : (s + 1) * C_ONE, at : at + LANES] = got
    width = 3 * C_TWO
    for k in range(9):
        message[:, k * width : (k + 1) * width] = totals[k * C_ONE : (k + 1) * C_ONE]
    message[:, GRAD_W_TWO:ONE_AT] = jnp.zeros((C_ONE, ONE_AT - GRAD_W_TWO), f32)


def shift_input(samples, rows_of, face_at, line_at, edge_at, blocks, own, ahead):
    used = samples * C_IN
    lane = iota((PACK, BZ), 1)
    for (px, py), line in rows_of.items():
        nx = -1 if px == 0 else 1 if px == BX + 1 else 0
        ny = -1 if py == 0 else 1 if py == BY + 1 else 0
        x, y = (px - 1) % BX, (py - 1) % BY
        if nx == 0 and ny == 0:
            row = own[:, (x * BY + y) * BZ : (x * BY + y + 1) * BZ].astype(f32)
        else:
            if nx != 0:
                ref, at = face_at[nx] if ny == 0 else line_at[nx, ny]
                tile = 2 * min(y, BY - 1 - y)
                chunk = 2 * (0 if x == 0 else 1) + (1 if y >= BY // 2 else 0)
            else:
                ref, at = line_at[nx, ny]
                tile = 2 * (0 if y == 0 else 1)
                chunk = x
            halves = []
            for t in (tile, tile + 1):
                four = blocks[ref][at + 4 * used * t : at + 4 * used * (t + 1)].astype(f32)
                halves.append(four[chunk * used : (chunk + 1) * used])
            row = jnp.concatenate(halves, axis=1)
            if used < PACK:
                row = jnp.concatenate([row, jnp.zeros((PACK - used, BZ), f32)], axis=0)
        ends = []
        for nz in (-1, 1):
            ref, at = edge_at[nx, ny, nz]
            ends.append(blocks[ref][at + C_TWO : at + EDGE].astype(f32))
        at = 2 * (x * BY + y)
        to = line * BZ
        before = jnp.where(lane == 0, ends[0][:, at + 1 : at + 2], pltpu.roll(row, 1, 1))
        after = jnp.where(lane == BZ - 1, ends[1][:, at : at + 1], pltpu.roll(row, BZ - 1, 1))
        for i, piece in enumerate((before, row, after)):
            ahead[i * PACK : (i + 1) * PACK, to : to + BZ] = piece.astype(bf16)


def lines_inside():
    return {(px, py): px * BY + py - 1 for px in range(BX + 2) for py in range(1, BY + 1)}


def lines_ends():
    return {(px, py): 2 * px + (py > 0) for px in range(BX + 2) for py in (0, BY + 1)}


def layer_one_inside(samples, face_at, edge_at, *refs):
    blocks, (own, ahead) = refs[:-2], refs[-2:]
    shift_input(samples, lines_inside(), face_at, {}, edge_at, blocks, own, ahead)


def layer_one(samples, scale, line_at, edge_at, *refs):
    blocks, (own, ahead, grad, chosen, before_sums, sums, ahead_ends, inside, ends) = refs[:-9], refs[-9:]
    sums[:, 0:ONE_AT] = before_sums[...]
    shift_input(samples, lines_ends(), {}, line_at, edge_at, blocks, own, ahead_ends)
    rows = samples * C_ONE
    table = doubling()
    empty = jnp.zeros((rows, BZ), bf16)
    for x in range(BX):
        inside[x, 0:rows, (BY - 1) * BZ :] = empty
        inside[x, 2 * rows :, 0:BZ] = empty
        ends[x, 0:rows, BZ:] = empty
        ends[x, rows : 2 * rows, 0:BZ] = empty
        ends[x, rows : 2 * rows, BZ:] = empty
        ends[x, 2 * rows :, 0:BZ] = empty
    for x in range(HX):
        for y in range(HY):
            at = (x * HY + y) * LANES
            wide = jnp.dot(grad[:, at : at + LANES], table, preferred_element_type=f32).astype(bf16)
            for dx in range(2):
                for dy in range(2):
                    cx, cy = 2 * x + dx, 2 * y + dy
                    value = wide * chosen[:, (cx * BY + cy) * BZ : (cx * BY + cy + 1) * BZ]
                    for j, oy in enumerate(OFFS):
                        to = cy + oy
                        here = slice(j * rows, (j + 1) * rows)
                        if to < 0:
                            ends[cx, here, 0:BZ] = value
                        elif to >= BY:
                            ends[cx, here, BZ:] = value
                        else:
                            inside[cx, here, to * BZ : (to + 1) * BZ] = value
    width = 3 * 3 * PACK
    product = jnp.zeros((3 * rows, width), f32)
    for x in range(BX):
        for left, right, size in ((inside, ahead, BY * BZ), (ends, ahead_ends, 2 * BZ)):
            pieces = [right[:, (x + 1 + ox) * size : (x + 2 + ox) * size] for ox in OFFS]
            product = product + lax.dot_general(
                left[x], jnp.concatenate(pieces, axis=0), NT, preferred_element_type=f32
            )
    sample_of = (iota((C_ONE, width), 1) % PACK) // C_IN
    k = iota((width, LANES), 0)
    to = (k % C_IN) * STRIDE_ONE + (k // (3 * PACK)) * 9 + (k // PACK) % 3
    total = jnp.zeros((C_ONE, LANES), f32)
    for j in range(3):
        folded = jnp.zeros((C_ONE, width), f32)
        for s in range(samples):
            at = j * rows + s * C_ONE
            folded = folded + jnp.where(sample_of == s, product[at : at + C_ONE], 0.0)
        fold = (to + 3 * j == iota((width, LANES), 1)).astype(f32)
        total = total + jnp.dot(
            folded, fold, preferred_element_type=f32, precision=lax.Precision.HIGHEST
        )
    sums[:, ONE_AT:] = total * scale


def finish(mine, theirs, grad_one, grad_two):
    total = mine[...] + theirs[...]
    for o in range(27):
        grad_two[o] = total[:, o * C_TWO : (o + 1) * C_TWO]
    for c in range(C_IN):
        at = ONE_AT + c * STRIDE_ONE
        grad_one[c] = total[:, at : at + 27]


def call(body, shapes, operands, far=0, scratch=(), flops=0, moved=0):
    if far:
        scratch = [pltpu.VMEM(a.shape, a.dtype) for a in operands[:far]]
        scratch.append(pltpu.SemaphoreType.DMA((far,)))
        away = [pltpu.with_memory_space_constraint(a, pltpu.HBM) for a in operands[:far]]
        operands = (*away, *operands[far:])
    spaces = [pltpu.HBM] * far + [pltpu.VMEM] * (len(operands) - far)
    return pl.pallas_call(
        body,
        out_shape=shapes,
        in_specs=[pl.BlockSpec(memory_space=space) for space in spaces],
        out_specs=jax.tree.map(lambda _: pl.BlockSpec(memory_space=pltpu.VMEM), shapes),
        scratch_shapes=list(scratch),
        compiler_params=pltpu.CompilerParams(vmem_limit_bytes=32 * 2**20),
        cost_estimate=pl.CostEstimate(flops=flops, bytes_accessed=moved, transcendentals=0),
    )(*operands)


def block_side(blocks):
    return min(k for k in range(1, blocks + 1) if k * k * k >= blocks)


def from_block(array, side, *offset):
    pairs = []
    for i in range(lax.axis_size("space")):
        at = (i // (side * side), i // side % side, i % side)
        x, y, z = ((c + o) % side for c, o in zip(at, offset))
        pairs.append(((x * side + y) * side + z, i))
    return lax.ppermute(array, "space", pairs)


def both_sides(array, side, axis):
    below = from_block(array, side, *(-1 if a == axis else 0 for a in range(3)))
    if side == 2:
        return {-1: below, 1: below}
    return {-1: below, 1: from_block(array, side, *(1 if a == axis else 0 for a in range(3)))}


def swapped(array, axis, bit):
    size = lax.axis_size(axis)
    return lax.ppermute(array, axis, [(i, i ^ bit) for i in range(size)])


def stacked(parts):
    kept, starts, places = [], [], []
    rows = 0
    for part in parts:
        found = [i for i, a in enumerate(kept) if a is part]
        if not found:
            found = [len(kept)]
            kept.append(part)
            starts.append(rows)
            rows += part.shape[0]
        places.append(starts[found[0]])
    return jnp.concatenate(kept, axis=0), places


def operands_of(*tables):
    arrays, numbered = [], []
    for table in tables:
        new = {}
        for key, (array, row) in table.items():
            found = [i for i, a in enumerate(arrays) if a is array]
            if not found:
                found = [len(arrays)]
                arrays.append(array)
            new[key] = (found[0], row)
        numbered.append(new)
    return arrays, numbered


def local(inputs, mask_one, place_one, pooled_one, w_two, mask_two, place_two, grad_two):
    blocks = lax.axis_size("space")
    side = block_side(blocks)
    samples = inputs.shape[0]
    cells = inputs.shape[3]
    half_cells = HX * HY * HZ
    shape = jax.ShapeDtypeStruct
    vp_rows = 2 * samples * C_TWO
    four = 4 * samples * C_IN
    vp_row = BY * four
    to_x, own = call(
        functools.partial(prepare, samples),
        (shape((BY * four + vp_rows, LANES), bf16), shape((PACK, cells), bf16)),
        (grad_two, place_two, mask_two, inputs),
        far=4,
        flops=2 * 10**7,
        moved=2**20,
    )
    edge = call(
        functools.partial(ends, samples, vp_row),
        shape((EDGE, LANES), bf16),
        (to_x, own),
        flops=10**7,
        moved=2**19,
    )
    chosen, folded_weights, expand, to_y = call(
        functools.partial(select_one, samples, vp_row),
        (
            shape((samples * C_ONE, cells), bf16),
            shape((9 * C_ONE, 3 * C_TWO), bf16),
            shape((2 * LANES, TABLE), bf16),
            shape((4 * four + vp_rows, LANES), bf16),
        ),
        (place_one, mask_one, w_two, to_x, own),
        far=3,
        flops=2 * 10**7,
        moved=3 * 2**20,
    )
    vp_at, edge_at, face_at, line_at = {(0, 0): (to_x, vp_row)}, {}, {}, {}
    from_x = both_sides(to_x, side, 0)
    edge_z = both_sides(edge, side, 2)
    if side == 2:
        diagonal = from_block(edge, side, 1, 0, 1)
        edge_x = {nz: {nx: diagonal for nx in (-1, 1)} for nz in (-1, 1)}
    else:
        edge_x = {nz: {nx: from_block(edge, side, nx, 0, nz) for nx in (-1, 1)} for nz in (-1, 1)}
    first = both_sides(to_y, side, 1)
    parts = []
    for n in (-1, 1):
        again = n == 1 and side == 2
        parts += parts[:2] if again else [from_x[n][vp_row:], from_x[n][: 2 * four]]
    second, starts = stacked(parts)
    second = both_sides(second, side, 1)
    parts = [edge_z[-1], edge_z[1]] + [edge_x[nz][nx] for nz in (-1, 1) for nx in (-1, 1)]
    third, edge_starts = stacked(parts)
    third = both_sides(third, side, 1)
    for n in (-1, 1):
        vp_at[n, 0] = (from_x[n], vp_row)
        face_at[n] = (from_x[n], 0)
        vp_at[0, n] = (first[n], 4 * four)
        line_at[0, n] = (first[n], 0)
        edge_at[0, 0, n] = (edge_z[n], 0)
        for i, nx in enumerate((-1, 1)):
            edge_at[nx, 0, n] = (edge_x[n][nx], 0)
            vp_at[nx, n] = (second[n], starts[2 * i])
            line_at[nx, n] = (second[n], starts[2 * i + 1])
        for i, nz in enumerate((-1, 1)):
            edge_at[0, n, nz] = (third[n], edge_starts[i])
            for j, nx in enumerate((-1, 1)):
                edge_at[nx, n, nz] = (third[n], edge_starts[2 + 2 * i + j])
    total = lax.axis_size("dp") * samples * blocks * cells

    def near(table, y):
        return {key: value for key, value in table.items() if key[1] in y}

    arrays, tables = operands_of(near(vp_at, (0,)), near(edge_at, (0,)))
    tiles, end_tiles = (HX + 2) * HY, (HX + 2) * 2
    part, total_two, moved_ends = call(
        functools.partial(layer_two_inside, samples, *tables),
        (
            shape((samples * C_ONE, half_cells), f32),
            shape((9 * C_ONE, 3 * C_TWO), f32),
            shape((samples, 9 * C_ONE, end_tiles * LANES), bf16),
        ),
        (*arrays, pooled_one, folded_weights, expand),
        scratch=(
            pltpu.VMEM((samples, 3 * C_TWO, tiles * LANES), bf16),
            pltpu.VMEM((samples, 9 * C_ONE, tiles * LANES), bf16),
        ),
        flops=5 * 10**8,
        moved=2**20,
    )
    arrays, tables = operands_of(face_at, near(edge_at, (0,)))
    ahead = call(
        functools.partial(layer_one_inside, samples, *tables),
        shape((3 * PACK, (BX + 2) * BY * BZ), bf16),
        (*arrays, own),
        flops=10**8,
        moved=2**20,
    )
    arrays, tables = operands_of(near(vp_at, (-1, 1)), near(edge_at, (-1, 1)))
    grad_pooled, kept, sums = call(
        functools.partial(layer_two_ends, samples, float(total // 8) ** -0.5, *tables),
        (
            shape((samples, 1, C_ONE, half_cells), bf16),
            shape((samples * C_ONE, half_cells), bf16),
            shape((C_ONE, ONE_AT), f32),
        ),
        (*arrays, folded_weights, expand, part, total_two, moved_ends),
        scratch=(pltpu.VMEM((samples, 3 * C_TWO, end_tiles * LANES), bf16),),
        flops=5 * 10**8,
        moved=2**20,
    )
    arrays, tables = operands_of(line_at, near(edge_at, (-1, 1)))
    sums = call(
        functools.partial(layer_one, samples, float(total) ** -0.5, *tables),
        shape((C_ONE, WIDTH), f32),
        (*arrays, own, ahead, kept, chosen, sums),
        scratch=(
            pltpu.VMEM((3 * PACK, (BX + 2) * 2 * BZ), bf16),
            pltpu.VMEM((BX, 3 * samples * C_ONE, BY * BZ), bf16),
            pltpu.VMEM((BX, 3 * samples * C_ONE, 2 * BZ), bf16),
        ),
        flops=5 * 10**8,
        moved=2**20,
    )
    steps = []
    for axis in ("dp", "space"):
        bit = 1
        while bit < lax.axis_size(axis):
            steps.append((axis, bit))
            bit *= 2
    for axis, bit in steps[:-1]:
        sums = sums + swapped(sums, axis, bit)
    grad_w_one, grad_w_two = call(
        finish,
        (shape((C_IN, C_ONE, 27), f32), shape((27, C_ONE, C_TWO), f32)),
        (sums, swapped(sums, *steps[-1])),
    )
    return grad_pooled, jnp.transpose(grad_w_one, (2, 0, 1)), grad_w_two


def solution(mesh):
    split = P("dp", "space", None, None)
    return jax.shard_map(
        local,
        mesh=mesh,
        in_specs=(split, split, split, split, P(), split, split, split),
        out_specs=(split, P(), P()),
        check_vma=False,
    )
```

```python
import functools

import jax
import jax.numpy as jnp
from jax import lax
from jax.experimental import pallas as pl
from jax.experimental.pallas import tpu as pltpu
from jax.sharding import PartitionSpec as P

C_IN = 4
C_ONE = 16
C_TWO = 32
BX = 4
BY = 8
BZ = 256
HX, HY, HZ = BX // 2, BY // 2, BZ // 2
QY, QZ = HY // 2, HZ // 2
LANES = 128
PACK = 16
EDGE = C_TWO + PACK
OFFS = (-1, 0, 1)
GRAD_W_TWO = 27 * C_TWO
WIDTH = 1024
ONE_AT = WIDTH - LANES
STRIDE_ONE = LANES // C_IN
HALF = C_ONE // 2
TABLE = 3 * QY * LANES
NT = (((1,), (1,)), ((), ()))
f32, bf16, i32 = jnp.float32, jnp.bfloat16, jnp.int32


def iota(shape, dim):
    return lax.broadcasted_iota(i32, shape, dim)


def doubling():
    return (iota((LANES, 2 * LANES), 0) == iota((LANES, 2 * LANES), 1) // 2).astype(bf16)


def fetch(pairs, sems):
    copies = [pltpu.make_async_copy(a, b, sems.at[i]) for i, (a, b) in enumerate(pairs)]
    for copy in copies:
        copy.start()
    return copies


def prepare(samples, *refs):
    far, (to_x, own), near, sems = refs[:4], refs[4:6], refs[6:10], refs[10]
    grad, place, mask, source = near
    copies = fetch(tuple(zip(far, near)), sems)
    rows = samples * C_TWO
    table = doubling()
    copies[0].wait()
    copies[1].wait()
    values = jnp.dot(grad[...].reshape(rows, LANES), table, preferred_element_type=f32)
    spots = place[...].reshape(rows, LANES).astype(f32).astype(bf16)
    wide = jnp.dot(spots, table, preferred_element_type=f32)
    parity = (iota((rows, LANES), 1) % 2).astype(f32)
    copies[2].wait()
    halves = []
    for qy in range(QY):
        v = values[:, qy * LANES : (qy + 1) * LANES]
        p = wide[:, qy * LANES : (qy + 1) * LANES] - parity
        total = jnp.zeros((rows, LANES), f32)
        for x in range(HX):
            for dy in range(2):
                at = (x * HY + 2 * qy + dy) * LANES
                on = mask[:, 0, :, at : at + LANES].reshape(rows, LANES) == 1
                total = total + jnp.where(on & (p == 4.0 * x + 2.0 * dy), v, 0.0)
        halves.append(total)
    kept = jnp.concatenate(halves, axis=1).astype(bf16)
    v = lax.dot_general(kept, table, NT, preferred_element_type=f32).astype(bf16)
    used = samples * C_IN
    at = BY * 4 * used
    to_x[at : at + rows] = v
    to_x[at + rows : at + 2 * rows] = spots
    copies[3].wait()
    pieces = [source[s, 0].astype(f32) for s in range(samples)]
    if used < PACK:
        pieces.append(jnp.zeros((PACK - used, BX * BY * BZ), f32))
    cells = jnp.concatenate(pieces, axis=0)
    own[...] = cells.astype(bf16)
    for t in range(BY):
        group = []
        for x in (0, BX - 1):
            for y in (t // 2, BY - 1 - t // 2):
                at = (x * BY + y) * BZ + (t % 2) * LANES
                group.append(cells[0:used, at : at + LANES])
        to_x[4 * used * t : 4 * used * (t + 1)] = jnp.concatenate(group, axis=0).astype(bf16)


def ends(samples, vp_row, to_x, own, edge):
    rows = samples * C_TWO
    lane = iota((LANES, LANES), 0)
    spot = (lane // QZ) * 2 + (lane % QZ == QZ - 1).astype(i32)
    spot = jnp.where((lane % QZ == 0) | (lane % QZ == QZ - 1), spot, -LANES)
    column = iota((LANES, LANES), 1)
    packed = jnp.zeros((C_TWO, LANES), f32)
    for s in range(samples):
        for t in range(2):
            pick = (spot + (8 * s + 4 * t) == column).astype(bf16)
            at = vp_row + t * rows + s * C_TWO
            packed = packed + jnp.dot(to_x[at : at + C_TWO], pick, preferred_element_type=f32)
    edge[0:C_TWO] = packed.astype(bf16)
    lane = iota((PACK, LANES), 1)
    packed = jnp.zeros((PACK, LANES), f32)
    for row in range(BX * BY):
        left = own[:, row * BZ : row * BZ + LANES].astype(f32)
        right = own[:, (row + 1) * BZ - LANES : (row + 1) * BZ].astype(f32)
        packed = jnp.where(lane == 2 * row, left[:, 0:1], packed)
        packed = jnp.where(lane == 2 * row + 1, right[:, LANES - 1 :], packed)
    edge[C_TWO:EDGE] = packed.astype(bf16)


def select_one(samples, vp_row, *refs):
    far, (to_x, own), (chosen, folded_weights, expand, to_y), near, sems = (
        refs[:3], refs[3:5], refs[5:9], refs[9:12], refs[12],
    )
    place, mask, weights = near
    copies = fetch(tuple(zip(far, near)), sems)
    used = samples * C_IN
    to_y[4 * 4 * used :] = to_x[vp_row:]
    for t in range(4):
        group = []
        for x in range(BX):
            at = (x * BY + (BY - 1) * (t // 2)) * BZ + (t % 2) * LANES
            group.append(own[:, at : at + LANES].astype(f32)[0:used])
        to_y[4 * used * t : 4 * used * (t + 1)] = jnp.concatenate(group, axis=0).astype(bf16)
    k = iota((2 * LANES, TABLE), 0)
    j = iota((1, TABLE), 1)
    shift = j // (QY * LANES) - 1
    qy = (j // LANES) % QY
    z = j % LANES - shift
    beyond = LANES + qy * 2 + (z < 0).astype(i32)
    expand[...] = (k == jnp.where((z >= 0) & (z < LANES), qy * QZ + z // 2, beyond)).astype(bf16)
    rows = samples * C_ONE
    table = doubling()
    parity = (iota((rows, BZ), 1) % 2).astype(f32)
    copies[2].wait()
    folded_weights[...] = jnp.concatenate(
        [jnp.concatenate([weights[3 * o + i] for i in range(3)], axis=1) for o in range(9)], axis=0
    )
    copies[0].wait()
    copies[1].wait()
    for x in range(HX):
        for y in range(HY):
            at = (x * HY + y) * LANES
            spots = place[:, 0, :, at : at + LANES].reshape(rows, LANES).astype(f32).astype(bf16)
            wide = jnp.dot(spots, table, preferred_element_type=f32) - parity
            for dx in range(2):
                for dy in range(2):
                    to = ((2 * x + dx) * BY + 2 * y + dy) * BZ
                    on = mask[:, 0, :, to : to + BZ].reshape(rows, BZ) == 1
                    hit = on & (wide == 4.0 * dx + 2.0 * dy)
                    chosen[:, to : to + BZ] = jnp.where(hit, 1.0, 0.0).astype(bf16)


def expand_windows(samples, vp_at, edge_at, ys, tile_of, blocks, expand, fields):
    rows = samples * C_TWO
    lane = iota((rows, LANES), 1)
    odd = iota((C_TWO, LANES), 1) % 2 == 1
    groups = {}
    for nx in OFFS:
        for ny in ys:
            key = (vp_at[nx, ny], edge_at[nx, ny, -1], edge_at[nx, ny, 1])
            groups.setdefault(key, []).append((nx, ny))
    for ((ref, at), low, high), places in groups.items():
        edge = blocks[low[0]][low[1] : low[1] + C_TWO].astype(f32)
        if low != high:
            other = blocks[high[0]][high[1] : high[1] + C_TWO].astype(f32)
            edge = jnp.where(odd, edge, other)
        parts = []
        for t in range(2):
            for s in range(samples):
                by = 8 * s + 4 * t
                parts.append(pltpu.roll(edge, LANES - by, 1) if by else edge)
        both = jnp.concatenate(
            [blocks[ref][at : at + 2 * rows], jnp.concatenate(parts, axis=0).astype(bf16)], axis=1
        )
        wide = jnp.dot(both, expand[...], preferred_element_type=f32)
        for i, oz in enumerate(OFFS):
            parity = ((lane - oz) & 1).astype(f32)
            for qy in range(QY):
                lanes = slice((i * QY + qy) * LANES, (i * QY + qy + 1) * LANES)
                v = wide[0:rows, lanes].astype(bf16)
                p = (wide[rows : 2 * rows, lanes] - parity).astype(bf16)
                for x in range(HX):
                    for dy in range(2):
                        y = 2 * qy + dy
                        spots = []
                        for nx, ny in places:
                            near_x = nx == 0 or x == (HX - 1 if nx < 0 else 0)
                            near_y = ny == 0 or y == (HY - 1 if ny < 0 else 0)
                            if near_x and near_y:
                                spots.append(tile_of[x + 1 + nx * HX, y + 1 + ny * HY])
                        if not spots:
                            continue
                        cells = jnp.where(p == 4.0 * x + 2.0 * dy, v, jnp.zeros_like(v))
                        for spot in spots:
                            for s in range(samples):
                                fields[s, i * C_TWO : (i + 1) * C_TWO, spot * LANES : (spot + 1) * LANES] = (
                                    cells[s * C_TWO : (s + 1) * C_TWO]
                                )


def tiles_inside():
    return {(px, py): px * HY + py - 1 for px in range(HX + 2) for py in range(1, HY + 1)}


def tiles_ends():
    return {(px, py): 2 * px + (py > 0) for px in range(HX + 2) for py in (0, HY + 1)}


def shift_pooled(samples, tile_of, pooled, moved):
    for (px, py), tile in tile_of.items():
        k = 0
        for ox in OFFS:
            for oy in OFFS:
                x, y = px - 1 + ox, py - 1 + oy
                inside = 0 <= x < HX and 0 <= y < HY
                for s in range(samples):
                    if inside:
                        at = (x * HY + y) * LANES
                        value = pooled[s, 0, :, at : at + LANES]
                    else:
                        value = jnp.zeros((C_ONE, LANES), bf16)
                    moved[s, k * C_ONE : (k + 1) * C_ONE, tile * LANES : (tile + 1) * LANES] = value
                k += 1


def products_two(samples, tile_of, fields, moved, weights, sums, totals):
    for s in range(samples):
        wide = jnp.dot(weights[...], fields[s], preferred_element_type=f32)
        for x in range(HX):
            for y in range(HY):
                k = 0
                for ox in OFFS:
                    for oy in OFFS:
                        tile = tile_of.get((x + 1 - ox, y + 1 - oy))
                        if tile is not None:
                            part = wide[k * C_ONE : (k + 1) * C_ONE, tile * LANES : (tile + 1) * LANES]
                            old = sums[s].get((x, y))
                            sums[s][x, y] = part if old is None else old + part
                        k += 1
        totals = totals + lax.dot_general(moved[s], fields[s], NT, preferred_element_type=f32)
    return totals


def layer_two_inside(samples, vp_at, edge_at, *refs):
    blocks, (pooled, weights, expand, part, total, moved_ends, fields, moved) = refs[:-8], refs[-8:]
    tile_of = tiles_inside()
    expand_windows(samples, vp_at, edge_at, (0,), tile_of, blocks, expand, fields)
    shift_pooled(samples, tile_of, pooled, moved)
    shift_pooled(samples, tiles_ends(), pooled, moved_ends)
    sums = [{} for _ in range(samples)]
    totals = jnp.zeros((9 * C_ONE, 3 * C_TWO), f32)
    total[...] = products_two(samples, tile_of, fields, moved, weights, sums, totals)
    for s in range(samples):
        for (x, y), value in sums[s].items():
            at = (x * HY + y) * LANES
            part[s * C_ONE : (s + 1) * C_ONE, at : at + LANES] = value


def layer_two_ends(samples, scale, vp_at, edge_at, *refs):
    blocks, (weights, expand, part, total, moved, kept, message, fields) = refs[:-8], refs[-8:]
    tile_of = tiles_ends()
    expand_windows(samples, vp_at, edge_at, (-1, 1), tile_of, blocks, expand, fields)
    sums = [
        {
            (x, y): part[s * C_ONE : (s + 1) * C_ONE, (x * HY + y) * LANES : (x * HY + y + 1) * LANES]
            for x in range(HX)
            for y in range(HY)
        }
        for s in range(samples)
    ]
    totals = products_two(samples, tile_of, fields, moved, weights, sums, total[...]) * scale
    for s in range(samples):
        for (x, y), value in sums[s].items():
            at = (x * HY + y) * LANES
            kept[s * C_ONE : (s + 1) * C_ONE, at : at + LANES] = value.astype(bf16)
    width = 3 * C_TWO
    for k in range(9):
        message[:, k * width : (k + 1) * width] = totals[k * C_ONE : (k + 1) * C_ONE]
    message[:, GRAD_W_TWO:ONE_AT] = jnp.zeros((C_ONE, ONE_AT - GRAD_W_TWO), f32)


def shift_input(samples, rows_of, face_at, line_at, edge_at, blocks, own, ahead):
    used = samples * C_IN
    lane = iota((PACK, BZ), 1)
    for (px, py), line in rows_of.items():
        nx = -1 if px == 0 else 1 if px == BX + 1 else 0
        ny = -1 if py == 0 else 1 if py == BY + 1 else 0
        x, y = (px - 1) % BX, (py - 1) % BY
        if nx == 0 and ny == 0:
            row = own[:, (x * BY + y) * BZ : (x * BY + y + 1) * BZ].astype(f32)
        else:
            if nx != 0:
                ref, at = face_at[nx] if ny == 0 else line_at[nx, ny]
                tile = 2 * min(y, BY - 1 - y)
                chunk = 2 * (0 if x == 0 else 1) + (1 if y >= BY // 2 else 0)
            else:
                ref, at = line_at[nx, ny]
                tile = 2 * (0 if y == 0 else 1)
                chunk = x
            halves = []
            for t in (tile, tile + 1):
                four = blocks[ref][at + 4 * used * t : at + 4 * used * (t + 1)].astype(f32)
                halves.append(four[chunk * used : (chunk + 1) * used])
            row = jnp.concatenate(halves, axis=1)
            if used < PACK:
                row = jnp.concatenate([row, jnp.zeros((PACK - used, BZ), f32)], axis=0)
        ends = []
        for nz in (-1, 1):
            ref, at = edge_at[nx, ny, nz]
            ends.append(blocks[ref][at + C_TWO : at + EDGE].astype(f32))
        at = 2 * (x * BY + y)
        to = line * BZ
        before = jnp.where(lane == 0, ends[0][:, at + 1 : at + 2], pltpu.roll(row, 1, 1))
        after = jnp.where(lane == BZ - 1, ends[1][:, at : at + 1], pltpu.roll(row, BZ - 1, 1))
        for i, piece in enumerate((before, row, after)):
            ahead[i * PACK : (i + 1) * PACK, to : to + BZ] = piece.astype(bf16)


def lines_inside():
    return {(px, py): px * BY + py - 1 for px in range(BX + 2) for py in range(1, BY + 1)}


def lines_ends():
    return {(px, py): 2 * px + (py > 0) for px in range(BX + 2) for py in (0, BY + 1)}


def emit(samples, kept, out):
    for s in range(samples):
        out[s, 0] = kept[s * C_ONE : (s + 1) * C_ONE]


def layer_one_inside(samples, face_at, edge_at, *refs):
    blocks, (own, ahead) = refs[:-2], refs[-2:]
    shift_input(samples, lines_inside(), face_at, {}, edge_at, blocks, own, ahead)


def layer_one(samples, scale, line_at, edge_at, *refs):
    blocks, (own, ahead, grad, chosen, before_sums, half, mine, other, ahead_ends, inside, ends) = refs[:-11], refs[-11:]
    shift_input(samples, lines_ends(), {}, line_at, edge_at, blocks, own, ahead_ends)
    rows = samples * C_ONE
    table = doubling()
    empty = jnp.zeros((rows, BZ), bf16)
    for x in range(BX):
        inside[x, 0:rows, (BY - 1) * BZ :] = empty
        inside[x, 2 * rows :, 0:BZ] = empty
        ends[x, 0:rows, BZ:] = empty
        ends[x, rows : 2 * rows, 0:BZ] = empty
        ends[x, rows : 2 * rows, BZ:] = empty
        ends[x, 2 * rows :, 0:BZ] = empty
    for x in range(HX):
        for y in range(HY):
            at = (x * HY + y) * LANES
            wide = jnp.dot(grad[:, at : at + LANES], table, preferred_element_type=f32).astype(bf16)
            for dx in range(2):
                for dy in range(2):
                    cx, cy = 2 * x + dx, 2 * y + dy
                    value = wide * chosen[:, (cx * BY + cy) * BZ : (cx * BY + cy + 1) * BZ]
                    for j, oy in enumerate(OFFS):
                        to = cy + oy
                        here = slice(j * rows, (j + 1) * rows)
                        if to < 0:
                            ends[cx, here, 0:BZ] = value
                        elif to >= BY:
                            ends[cx, here, BZ:] = value
                        else:
                            inside[cx, here, to * BZ : (to + 1) * BZ] = value
    width = 3 * 3 * PACK
    product = jnp.zeros((3 * rows, width), f32)
    for x in range(BX):
        for left, right, size in ((inside, ahead, BY * BZ), (ends, ahead_ends, 2 * BZ)):
            pieces = [right[:, (x + 1 + ox) * size : (x + 2 + ox) * size] for ox in OFFS]
            product = product + lax.dot_general(
                left[x], jnp.concatenate(pieces, axis=0), NT, preferred_element_type=f32
            )
    sample_of = (iota((C_ONE, width), 1) % PACK) // C_IN
    k = iota((width, LANES), 0)
    to = (k % C_IN) * STRIDE_ONE + (k // (3 * PACK)) * 9 + (k // PACK) % 3
    total = jnp.zeros((C_ONE, LANES), f32)
    for j in range(3):
        folded = jnp.zeros((C_ONE, width), f32)
        for s in range(samples):
            at = j * rows + s * C_ONE
            folded = folded + jnp.where(sample_of == s, product[at : at + C_ONE], 0.0)
        fold = (to + 3 * j == iota((width, LANES), 1)).astype(f32)
        total = total + jnp.dot(
            folded, fold, preferred_element_type=f32, precision=lax.Precision.HIGHEST
        )
    sums = jnp.concatenate([before_sums[...], total * scale], axis=1)
    top, bottom = sums[0:HALF], sums[HALF:]
    first = half[0] == 0
    mine[...] = jnp.where(first, top, bottom)
    other[...] = jnp.where(first, bottom, top)


def finish(half, mine, theirs, grad_one, grad_two):
    first = half[0] == 0
    top = jnp.where(first, mine[...], theirs[...])
    bottom = jnp.where(first, theirs[...], mine[...])
    for rows, part in ((slice(0, HALF), top), (slice(HALF, C_ONE), bottom)):
        for o in range(27):
            grad_two[o, rows] = part[:, o * C_TWO : (o + 1) * C_TWO]
        for c in range(C_IN):
            at = ONE_AT + c * STRIDE_ONE
            grad_one[c, rows] = part[:, at : at + 27]


def call(body, shapes, operands, far=0, scratch=(), flops=0, moved=0, scalars=()):
    if far:
        scratch = [pltpu.VMEM(a.shape, a.dtype) for a in operands[:far]]
        scratch.append(pltpu.SemaphoreType.DMA((far,)))
        away = [pltpu.with_memory_space_constraint(a, pltpu.HBM) for a in operands[:far]]
        operands = (*away, *operands[far:])
    spaces = [pltpu.HBM] * far + [pltpu.VMEM] * (len(operands) - far)
    for i in scalars:
        spaces[i] = pltpu.SMEM
    return pl.pallas_call(
        body,
        out_shape=shapes,
        in_specs=[pl.BlockSpec(memory_space=space) for space in spaces],
        out_specs=jax.tree.map(lambda _: pl.BlockSpec(memory_space=pltpu.VMEM), shapes),
        scratch_shapes=list(scratch),
        compiler_params=pltpu.CompilerParams(vmem_limit_bytes=32 * 2**20),
        cost_estimate=pl.CostEstimate(flops=flops, bytes_accessed=moved, transcendentals=0),
    )(*operands)


def block_side(blocks):
    return min(k for k in range(1, blocks + 1) if k * k * k >= blocks)


def from_block(array, side, *offset):
    pairs = []
    for i in range(lax.axis_size("space")):
        at = (i // (side * side), i // side % side, i % side)
        x, y, z = ((c + o) % side for c, o in zip(at, offset))
        pairs.append(((x * side + y) * side + z, i))
    return lax.ppermute(array, "space", pairs)


def both_sides(array, side, axis):
    below = from_block(array, side, *(-1 if a == axis else 0 for a in range(3)))
    if side == 2:
        return {-1: below, 1: below}
    return {-1: below, 1: from_block(array, side, *(1 if a == axis else 0 for a in range(3)))}


def swapped(array, axis, bit):
    size = lax.axis_size(axis)
    return lax.ppermute(array, axis, [(i, i ^ bit) for i in range(size)])


def stacked(parts):
    kept, starts, places = [], [], []
    rows = 0
    for part in parts:
        found = [i for i, a in enumerate(kept) if a is part]
        if not found:
            found = [len(kept)]
            kept.append(part)
            starts.append(rows)
            rows += part.shape[0]
        places.append(starts[found[0]])
    return jnp.concatenate(kept, axis=0), places


def operands_of(*tables):
    arrays, numbered = [], []
    for table in tables:
        new = {}
        for key, (array, row) in table.items():
            found = [i for i, a in enumerate(arrays) if a is array]
            if not found:
                found = [len(arrays)]
                arrays.append(array)
            new[key] = (found[0], row)
        numbered.append(new)
    return arrays, numbered


def local(inputs, mask_one, place_one, pooled_one, w_two, mask_two, place_two, grad_two):
    blocks = lax.axis_size("space")
    side = block_side(blocks)
    samples = inputs.shape[0]
    cells = inputs.shape[3]
    half_cells = HX * HY * HZ
    shape = jax.ShapeDtypeStruct
    vp_rows = 2 * samples * C_TWO
    four = 4 * samples * C_IN
    vp_row = BY * four
    to_x, own = call(
        functools.partial(prepare, samples),
        (shape((BY * four + vp_rows, LANES), bf16), shape((PACK, cells), bf16)),
        (grad_two, place_two, mask_two, inputs),
        far=4,
        flops=2 * 10**7,
        moved=2**20,
    )
    edge = call(
        functools.partial(ends, samples, vp_row),
        shape((EDGE, LANES), bf16),
        (to_x, own),
        flops=10**7,
        moved=2**19,
    )
    chosen, folded_weights, expand, to_y = call(
        functools.partial(select_one, samples, vp_row),
        (
            shape((samples * C_ONE, cells), bf16),
            shape((9 * C_ONE, 3 * C_TWO), bf16),
            shape((2 * LANES, TABLE), bf16),
            shape((4 * four + vp_rows, LANES), bf16),
        ),
        (place_one, mask_one, w_two, to_x, own),
        far=3,
        flops=2 * 10**7,
        moved=3 * 2**20,
    )
    vp_at, edge_at, face_at, line_at = {(0, 0): (to_x, vp_row)}, {}, {}, {}
    from_x = both_sides(to_x, side, 0)
    edge_z = both_sides(edge, side, 2)
    if side == 2:
        diagonal = from_block(edge, side, 1, 0, 1)
        edge_x = {nz: {nx: diagonal for nx in (-1, 1)} for nz in (-1, 1)}
    else:
        edge_x = {nz: {nx: from_block(edge, side, nx, 0, nz) for nx in (-1, 1)} for nz in (-1, 1)}
    first = both_sides(to_y, side, 1)
    parts = []
    for n in (-1, 1):
        again = n == 1 and side == 2
        parts += parts[:2] if again else [from_x[n][vp_row:], from_x[n][: 2 * four]]
    second, starts = stacked(parts)
    second = both_sides(second, side, 1)
    parts = [edge_z[-1], edge_z[1]] + [edge_x[nz][nx] for nz in (-1, 1) for nx in (-1, 1)]
    third, edge_starts = stacked(parts)
    third = both_sides(third, side, 1)
    for n in (-1, 1):
        vp_at[n, 0] = (from_x[n], vp_row)
        face_at[n] = (from_x[n], 0)
        vp_at[0, n] = (first[n], 4 * four)
        line_at[0, n] = (first[n], 0)
        edge_at[0, 0, n] = (edge_z[n], 0)
        for i, nx in enumerate((-1, 1)):
            edge_at[nx, 0, n] = (edge_x[n][nx], 0)
            vp_at[nx, n] = (second[n], starts[2 * i])
            line_at[nx, n] = (second[n], starts[2 * i + 1])
        for i, nz in enumerate((-1, 1)):
            edge_at[0, n, nz] = (third[n], edge_starts[i])
            for j, nx in enumerate((-1, 1)):
                edge_at[nx, n, nz] = (third[n], edge_starts[2 + 2 * i + j])
    total = lax.axis_size("dp") * samples * blocks * cells

    def near(table, y):
        return {key: value for key, value in table.items() if key[1] in y}

    arrays, tables = operands_of(near(vp_at, (0,)), near(edge_at, (0,)))
    tiles, end_tiles = (HX + 2) * HY, (HX + 2) * 2
    part, total_two, moved_ends = call(
        functools.partial(layer_two_inside, samples, *tables),
        (
            shape((samples * C_ONE, half_cells), f32),
            shape((9 * C_ONE, 3 * C_TWO), f32),
            shape((samples, 9 * C_ONE, end_tiles * LANES), bf16),
        ),
        (*arrays, pooled_one, folded_weights, expand),
        scratch=(
            pltpu.VMEM((samples, 3 * C_TWO, tiles * LANES), bf16),
            pltpu.VMEM((samples, 9 * C_ONE, tiles * LANES), bf16),
        ),
        flops=5 * 10**8,
        moved=2**20,
    )
    arrays, tables = operands_of(face_at, near(edge_at, (0,)))
    ahead = call(
        functools.partial(layer_one_inside, samples, *tables),
        shape((3 * PACK, (BX + 2) * BY * BZ), bf16),
        (*arrays, own),
        flops=10**8,
        moved=2**20,
    )
    arrays, tables = operands_of(near(vp_at, (-1, 1)), near(edge_at, (-1, 1)))
    kept, sums = call(
        functools.partial(layer_two_ends, samples, float(total // 8) ** -0.5, *tables),
        (
            shape((samples * C_ONE, half_cells), bf16),
            shape((C_ONE, ONE_AT), f32),
        ),
        (*arrays, folded_weights, expand, part, total_two, moved_ends),
        scratch=(pltpu.VMEM((samples, 3 * C_TWO, end_tiles * LANES), bf16),),
        flops=5 * 10**8,
        moved=2**20,
    )
    arrays, tables = operands_of(line_at, near(edge_at, (-1, 1)))
    half = (lax.axis_index("dp") % 2).astype(i32).reshape(1)
    operands = (*arrays, own, ahead, kept, chosen, sums, half)
    half_sums = shape((HALF, WIDTH), f32)
    mine, other = call(
        functools.partial(layer_one, samples, float(total) ** -0.5, *tables),
        (half_sums, half_sums),
        operands,
        scratch=(
            pltpu.VMEM((3 * PACK, (BX + 2) * 2 * BZ), bf16),
            pltpu.VMEM((BX, 3 * samples * C_ONE, BY * BZ), bf16),
            pltpu.VMEM((BX, 3 * samples * C_ONE, 2 * BZ), bf16),
        ),
        flops=5 * 10**8,
        moved=2**20,
        scalars=(len(operands) - 1,),
    )
    grad_pooled = call(
        functools.partial(emit, samples),
        shape((samples, 1, C_ONE, half_cells), bf16),
        (kept,),
        flops=10**6,
        moved=2**18,
    )
    mine = mine + swapped(other, "dp", 1)
    for axis in ("dp", "space"):
        bit = 2 if axis == "dp" else 1
        while bit < lax.axis_size(axis):
            mine = mine + swapped(mine, axis, bit)
            bit *= 2
    grad_w_one, grad_w_two = call(
        finish,
        (shape((C_IN, C_ONE, 27), f32), shape((27, C_ONE, C_TWO), f32)),
        (half, mine, swapped(mine, "dp", 1)),
        scalars=(0,),
    )
    return grad_pooled, jnp.transpose(grad_w_one, (2, 0, 1)), grad_w_two


def solution(mesh):
    split = P("dp", "space", None, None)
    return jax.shard_map(
        local,
        mesh=mesh,
        in_specs=(split, split, split, split, P(), split, split, split),
        out_specs=(split, P(), P()),
        check_vma=False,
    )
```

```python
import functools

import jax
import jax.numpy as jnp
from jax import lax
from jax.experimental import pallas as pl
from jax.experimental.pallas import tpu as pltpu
from jax.sharding import PartitionSpec as P

C_IN = 4
C_ONE = 16
C_TWO = 32
BX = 4
BY = 8
BZ = 256
HX, HY, HZ = BX // 2, BY // 2, BZ // 2
QY, QZ = HY // 2, HZ // 2
LANES = 128
PACK = 16
ENDS_AT = LANES - 2 * BX * BY
OFFS = (-1, 0, 1)
GRAD_W_TWO = 27 * C_TWO
WIDTH = 1024
ONE_AT = WIDTH - LANES
STRIDE_ONE = LANES // C_IN
HALF = C_ONE // 2
TABLE = 3 * QY * LANES
NT = (((1,), (1,)), ((), ()))
f32, bf16, i32 = jnp.float32, jnp.bfloat16, jnp.int32


def iota(shape, dim):
    return lax.broadcasted_iota(i32, shape, dim)


def doubling():
    return (iota((LANES, 2 * LANES), 0) == iota((LANES, 2 * LANES), 1) // 2).astype(bf16)


def fetch(pairs, sems):
    copies = [pltpu.make_async_copy(a, b, sems.at[i]) for i, (a, b) in enumerate(pairs)]
    for copy in copies:
        copy.start()
    return copies


def prepare(samples, *refs):
    far, (to_x, own), near, sems = refs[:4], refs[4:6], refs[6:10], refs[10]
    grad, place, mask, source = near
    copies = fetch(tuple(zip(far, near)), sems)
    rows = samples * C_TWO
    table = doubling()
    copies[0].wait()
    copies[1].wait()
    values = jnp.dot(grad[...].reshape(rows, LANES), table, preferred_element_type=f32)
    spots = place[...].reshape(rows, LANES).astype(f32).astype(bf16)
    wide = jnp.dot(spots, table, preferred_element_type=f32)
    parity = (iota((rows, LANES), 1) % 2).astype(f32)
    copies[2].wait()
    halves = []
    for qy in range(QY):
        v = values[:, qy * LANES : (qy + 1) * LANES]
        p = wide[:, qy * LANES : (qy + 1) * LANES] - parity
        total = jnp.zeros((rows, LANES), f32)
        for x in range(HX):
            for dy in range(2):
                at = (x * HY + 2 * qy + dy) * LANES
                on = mask[:, 0, :, at : at + LANES].reshape(rows, LANES) == 1
                total = total + jnp.where(on & (p == 4.0 * x + 2.0 * dy), v, 0.0)
        halves.append(total)
    kept = jnp.concatenate(halves, axis=1).astype(bf16)
    v = lax.dot_general(kept, table, NT, preferred_element_type=f32).astype(bf16)
    used = samples * C_IN
    at = BY * 4 * used
    to_x[at : at + rows] = v
    to_x[at + rows : at + 2 * rows] = spots
    copies[3].wait()
    pieces = [source[s, 0].astype(f32) for s in range(samples)]
    if used < PACK:
        pieces.append(jnp.zeros((PACK - used, BX * BY * BZ), f32))
    cells = jnp.concatenate(pieces, axis=0)
    own[...] = cells.astype(bf16)
    for t in range(BY):
        group = []
        for x in (0, BX - 1):
            for y in (t // 2, BY - 1 - t // 2):
                at = (x * BY + y) * BZ + (t % 2) * LANES
                group.append(cells[0:used, at : at + LANES])
        to_x[4 * used * t : 4 * used * (t + 1)] = jnp.concatenate(group, axis=0).astype(bf16)


def ends(samples, vp_row, to_x, own, edge):
    rows = samples * C_TWO
    lane = iota((LANES, LANES), 0)
    spot = (lane // QZ) * 2 + (lane % QZ == QZ - 1).astype(i32)
    spot = jnp.where((lane % QZ == 0) | (lane % QZ == QZ - 1), spot, -LANES)
    column = iota((LANES, LANES), 1)
    packed = jnp.zeros((C_TWO, LANES), f32)
    for s in range(samples):
        for t in range(2):
            pick = (spot + (8 * s + 4 * t) == column).astype(bf16)
            at = vp_row + t * rows + s * C_TWO
            packed = packed + jnp.dot(to_x[at : at + C_TWO], pick, preferred_element_type=f32)
    lane = iota((PACK, LANES), 1)
    cells = packed[0:PACK]
    for row in range(BX * BY):
        left = own[:, row * BZ : row * BZ + LANES].astype(f32)
        right = own[:, (row + 1) * BZ - LANES : (row + 1) * BZ].astype(f32)
        cells = jnp.where(lane == ENDS_AT + 2 * row, left[:, 0:1], cells)
        cells = jnp.where(lane == ENDS_AT + 2 * row + 1, right[:, LANES - 1 :], cells)
    edge[0:PACK] = cells.astype(bf16)
    edge[PACK:] = packed[PACK:].astype(bf16)


def select_one(samples, vp_row, *refs):
    far, (to_x, own), (chosen, folded_weights, expand, to_y), near, sems = (
        refs[:3], refs[3:5], refs[5:9], refs[9:12], refs[12],
    )
    place, mask, weights = near
    copies = fetch(tuple(zip(far, near)), sems)
    used = samples * C_IN
    to_y[4 * 4 * used :] = to_x[vp_row:]
    for t in range(4):
        group = []
        for x in range(BX):
            at = (x * BY + (BY - 1) * (t // 2)) * BZ + (t % 2) * LANES
            group.append(own[:, at : at + LANES].astype(f32)[0:used])
        to_y[4 * used * t : 4 * used * (t + 1)] = jnp.concatenate(group, axis=0).astype(bf16)
    k = iota((2 * LANES, TABLE), 0)
    j = iota((1, TABLE), 1)
    shift = j // (QY * LANES) - 1
    qy = (j // LANES) % QY
    z = j % LANES - shift
    beyond = LANES + qy * 2 + (z < 0).astype(i32)
    expand[...] = (k == jnp.where((z >= 0) & (z < LANES), qy * QZ + z // 2, beyond)).astype(bf16)
    rows = samples * C_ONE
    table = doubling()
    parity = (iota((rows, BZ), 1) % 2).astype(f32)
    copies[2].wait()
    folded_weights[...] = jnp.concatenate(
        [jnp.concatenate([weights[3 * o + i] for i in range(3)], axis=1) for o in range(9)], axis=0
    )
    copies[0].wait()
    copies[1].wait()
    for x in range(HX):
        for y in range(HY):
            at = (x * HY + y) * LANES
            spots = place[:, 0, :, at : at + LANES].reshape(rows, LANES).astype(f32).astype(bf16)
            wide = jnp.dot(spots, table, preferred_element_type=f32) - parity
            for dx in range(2):
                for dy in range(2):
                    to = ((2 * x + dx) * BY + 2 * y + dy) * BZ
                    on = mask[:, 0, :, to : to + BZ].reshape(rows, BZ) == 1
                    hit = on & (wide == 4.0 * dx + 2.0 * dy)
                    chosen[:, to : to + BZ] = jnp.where(hit, 1.0, 0.0).astype(bf16)


def expand_windows(samples, vp_at, edge_at, ys, tile_of, blocks, expand, fields):
    rows = samples * C_TWO
    lane = iota((rows, LANES), 1)
    odd = iota((C_TWO, LANES), 1) % 2 == 1
    groups = {}
    for nx in OFFS:
        for ny in ys:
            key = (vp_at[nx, ny], edge_at[nx, ny, -1], edge_at[nx, ny, 1])
            groups.setdefault(key, []).append((nx, ny))
    for ((ref, at), low, high), places in groups.items():
        edge = blocks[low[0]][low[1] : low[1] + C_TWO].astype(f32)
        if low != high:
            other = blocks[high[0]][high[1] : high[1] + C_TWO].astype(f32)
            edge = jnp.where(odd, edge, other)
        parts = []
        for t in range(2):
            for s in range(samples):
                by = 8 * s + 4 * t
                parts.append(pltpu.roll(edge, LANES - by, 1) if by else edge)
        both = jnp.concatenate(
            [blocks[ref][at : at + 2 * rows], jnp.concatenate(parts, axis=0).astype(bf16)], axis=1
        )
        wide = jnp.dot(both, expand[...], preferred_element_type=f32)
        for i, oz in enumerate(OFFS):
            parity = ((lane - oz) & 1).astype(f32)
            for qy in range(QY):
                lanes = slice((i * QY + qy) * LANES, (i * QY + qy + 1) * LANES)
                v = wide[0:rows, lanes].astype(bf16)
                p = (wide[rows : 2 * rows, lanes] - parity).astype(bf16)
                for x in range(HX):
                    for dy in range(2):
                        y = 2 * qy + dy
                        spots = []
                        for nx, ny in places:
                            near_x = nx == 0 or x == (HX - 1 if nx < 0 else 0)
                            near_y = ny == 0 or y == (HY - 1 if ny < 0 else 0)
                            if near_x and near_y:
                                spots.append(tile_of[x + 1 + nx * HX, y + 1 + ny * HY])
                        if not spots:
                            continue
                        cells = jnp.where(p == 4.0 * x + 2.0 * dy, v, jnp.zeros_like(v))
                        for spot in spots:
                            for s in range(samples):
                                fields[s, i * C_TWO : (i + 1) * C_TWO, spot * LANES : (spot + 1) * LANES] = (
                                    cells[s * C_TWO : (s + 1) * C_TWO]
                                )


def tiles_inside():
    return {(px, py): px * HY + py - 1 for px in range(HX + 2) for py in range(1, HY + 1)}


def tiles_ends():
    return {(px, py): 2 * px + (py > 0) for px in range(HX + 2) for py in (0, HY + 1)}


def shift_pooled(samples, tile_of, pooled, moved):
    for (px, py), tile in tile_of.items():
        k = 0
        for ox in OFFS:
            for oy in OFFS:
                x, y = px - 1 + ox, py - 1 + oy
                inside = 0 <= x < HX and 0 <= y < HY
                for s in range(samples):
                    if inside:
                        at = (x * HY + y) * LANES
                        value = pooled[s, 0, :, at : at + LANES]
                    else:
                        value = jnp.zeros((C_ONE, LANES), bf16)
                    moved[s, k * C_ONE : (k + 1) * C_ONE, tile * LANES : (tile + 1) * LANES] = value
                k += 1


def products_two(samples, tile_of, fields, moved, weights, sums, totals):
    for s in range(samples):
        wide = jnp.dot(weights[...], fields[s], preferred_element_type=f32)
        for x in range(HX):
            for y in range(HY):
                k = 0
                for ox in OFFS:
                    for oy in OFFS:
                        tile = tile_of.get((x + 1 - ox, y + 1 - oy))
                        if tile is not None:
                            part = wide[k * C_ONE : (k + 1) * C_ONE, tile * LANES : (tile + 1) * LANES]
                            old = sums[s].get((x, y))
                            sums[s][x, y] = part if old is None else old + part
                        k += 1
        totals = totals + lax.dot_general(moved[s], fields[s], NT, preferred_element_type=f32)
    return totals


def layer_two_inside(samples, vp_at, edge_at, *refs):
    blocks, (pooled, weights, expand, part, total, moved_ends, fields, moved) = refs[:-8], refs[-8:]
    tile_of = tiles_inside()
    expand_windows(samples, vp_at, edge_at, (0,), tile_of, blocks, expand, fields)
    shift_pooled(samples, tile_of, pooled, moved)
    shift_pooled(samples, tiles_ends(), pooled, moved_ends)
    sums = [{} for _ in range(samples)]
    totals = jnp.zeros((9 * C_ONE, 3 * C_TWO), f32)
    total[...] = products_two(samples, tile_of, fields, moved, weights, sums, totals)
    for s in range(samples):
        for (x, y), value in sums[s].items():
            at = (x * HY + y) * LANES
            part[s * C_ONE : (s + 1) * C_ONE, at : at + LANES] = value


def layer_two_ends(samples, scale, vp_at, edge_at, *refs):
    blocks, (weights, expand, part, total, moved, kept, message, fields) = refs[:-8], refs[-8:]
    tile_of = tiles_ends()
    expand_windows(samples, vp_at, edge_at, (-1, 1), tile_of, blocks, expand, fields)
    sums = [
        {
            (x, y): part[s * C_ONE : (s + 1) * C_ONE, (x * HY + y) * LANES : (x * HY + y + 1) * LANES]
            for x in range(HX)
            for y in range(HY)
        }
        for s in range(samples)
    ]
    totals = products_two(samples, tile_of, fields, moved, weights, sums, total[...]) * scale
    for s in range(samples):
        for (x, y), value in sums[s].items():
            at = (x * HY + y) * LANES
            kept[s * C_ONE : (s + 1) * C_ONE, at : at + LANES] = value.astype(bf16)
    width = 3 * C_TWO
    for k in range(9):
        message[:, k * width : (k + 1) * width] = totals[k * C_ONE : (k + 1) * C_ONE]
    message[:, GRAD_W_TWO:ONE_AT] = jnp.zeros((C_ONE, ONE_AT - GRAD_W_TWO), f32)


def shift_input(samples, rows_of, face_at, line_at, edge_at, blocks, own, ahead):
    used = samples * C_IN
    lane = iota((PACK, BZ), 1)
    for (px, py), line in rows_of.items():
        nx = -1 if px == 0 else 1 if px == BX + 1 else 0
        ny = -1 if py == 0 else 1 if py == BY + 1 else 0
        x, y = (px - 1) % BX, (py - 1) % BY
        if nx == 0 and ny == 0:
            row = own[:, (x * BY + y) * BZ : (x * BY + y + 1) * BZ].astype(f32)
        else:
            if nx != 0:
                ref, at = face_at[nx] if ny == 0 else line_at[nx, ny]
                tile = 2 * min(y, BY - 1 - y)
                chunk = 2 * (0 if x == 0 else 1) + (1 if y >= BY // 2 else 0)
            else:
                ref, at = line_at[nx, ny]
                tile = 2 * (0 if y == 0 else 1)
                chunk = x
            halves = []
            for t in (tile, tile + 1):
                four = blocks[ref][at + 4 * used * t : at + 4 * used * (t + 1)].astype(f32)
                halves.append(four[chunk * used : (chunk + 1) * used])
            row = jnp.concatenate(halves, axis=1)
            if used < PACK:
                row = jnp.concatenate([row, jnp.zeros((PACK - used, BZ), f32)], axis=0)
        ends = []
        for nz in (-1, 1):
            ref, at = edge_at[nx, ny, nz]
            ends.append(blocks[ref][at : at + PACK].astype(f32))
        at = ENDS_AT + 2 * (x * BY + y)
        to = line * BZ
        before = jnp.where(lane == 0, ends[0][:, at + 1 : at + 2], pltpu.roll(row, 1, 1))
        after = jnp.where(lane == BZ - 1, ends[1][:, at : at + 1], pltpu.roll(row, BZ - 1, 1))
        for i, piece in enumerate((before, row, after)):
            ahead[i * PACK : (i + 1) * PACK, to : to + BZ] = piece.astype(bf16)


def lines_inside():
    return {(px, py): px * BY + py - 1 for px in range(BX + 2) for py in range(1, BY + 1)}


def lines_ends():
    return {(px, py): 2 * px + (py > 0) for px in range(BX + 2) for py in (0, BY + 1)}


def emit(samples, kept, out):
    for s in range(samples):
        out[s, 0] = kept[s * C_ONE : (s + 1) * C_ONE]


def layer_one_inside(samples, face_at, edge_at, *refs):
    blocks, (own, ahead) = refs[:-2], refs[-2:]
    shift_input(samples, lines_inside(), face_at, {}, edge_at, blocks, own, ahead)


def layer_one(samples, scale, line_at, edge_at, *refs):
    blocks, (own, ahead, grad, chosen, before_sums, half, mine, other, ahead_ends, inside, ends) = refs[:-11], refs[-11:]
    shift_input(samples, lines_ends(), {}, line_at, edge_at, blocks, own, ahead_ends)
    rows = samples * C_ONE
    table = doubling()
    empty = jnp.zeros((rows, BZ), bf16)
    for x in range(BX):
        inside[x, 0:rows, (BY - 1) * BZ :] = empty
        inside[x, 2 * rows :, 0:BZ] = empty
        ends[x, 0:rows, BZ:] = empty
        ends[x, rows : 2 * rows, 0:BZ] = empty
        ends[x, rows : 2 * rows, BZ:] = empty
        ends[x, 2 * rows :, 0:BZ] = empty
    for x in range(HX):
        for y in range(HY):
            at = (x * HY + y) * LANES
            wide = jnp.dot(grad[:, at : at + LANES], table, preferred_element_type=f32).astype(bf16)
            for dx in range(2):
                for dy in range(2):
                    cx, cy = 2 * x + dx, 2 * y + dy
                    value = wide * chosen[:, (cx * BY + cy) * BZ : (cx * BY + cy + 1) * BZ]
                    for j, oy in enumerate(OFFS):
                        to = cy + oy
                        here = slice(j * rows, (j + 1) * rows)
                        if to < 0:
                            ends[cx, here, 0:BZ] = value
                        elif to >= BY:
                            ends[cx, here, BZ:] = value
                        else:
                            inside[cx, here, to * BZ : (to + 1) * BZ] = value
    width = 3 * 3 * PACK
    product = jnp.zeros((3 * rows, width), f32)
    for x in range(BX):
        for left, right, size in ((inside, ahead, BY * BZ), (ends, ahead_ends, 2 * BZ)):
            pieces = [right[:, (x + 1 + ox) * size : (x + 2 + ox) * size] for ox in OFFS]
            product = product + lax.dot_general(
                left[x], jnp.concatenate(pieces, axis=0), NT, preferred_element_type=f32
            )
    sample_of = (iota((C_ONE, width), 1) % PACK) // C_IN
    k = iota((width, LANES), 0)
    to = (k % C_IN) * STRIDE_ONE + (k // (3 * PACK)) * 9 + (k // PACK) % 3
    total = jnp.zeros((C_ONE, LANES), f32)
    for j in range(3):
        folded = jnp.zeros((C_ONE, width), f32)
        for s in range(samples):
            at = j * rows + s * C_ONE
            folded = folded + jnp.where(sample_of == s, product[at : at + C_ONE], 0.0)
        fold = (to + 3 * j == iota((width, LANES), 1)).astype(bf16)
        parts = []
        for _ in range(3):
            parts.append(folded.astype(bf16))
            folded = folded - parts[-1].astype(f32)
        got = jnp.dot(jnp.concatenate(parts, axis=0), fold, preferred_element_type=f32)
        total = total + (got[2 * C_ONE :] + got[C_ONE : 2 * C_ONE] + got[0:C_ONE])
    sums = jnp.concatenate([before_sums[...], total * scale], axis=1)
    top, bottom = sums[0:HALF], sums[HALF:]
    first = half[0] == 0
    mine[...] = jnp.where(first, top, bottom)
    other[...] = jnp.where(first, bottom, top)


def finish(half, mine, theirs, grad_one, grad_two):
    first = half[0] == 0
    top = jnp.where(first, mine[...], theirs[...])
    bottom = jnp.where(first, theirs[...], mine[...])
    for rows, part in ((slice(0, HALF), top), (slice(HALF, C_ONE), bottom)):
        for o in range(27):
            grad_two[o, rows] = part[:, o * C_TWO : (o + 1) * C_TWO]
        for c in range(C_IN):
            at = ONE_AT + c * STRIDE_ONE
            grad_one[c, rows] = part[:, at : at + 27]


def call(body, shapes, operands, far=0, scratch=(), flops=0, moved=0, scalars=()):
    if far:
        scratch = [pltpu.VMEM(a.shape, a.dtype) for a in operands[:far]]
        scratch.append(pltpu.SemaphoreType.DMA((far,)))
        away = [pltpu.with_memory_space_constraint(a, pltpu.HBM) for a in operands[:far]]
        operands = (*away, *operands[far:])
    spaces = [pltpu.HBM] * far + [pltpu.VMEM] * (len(operands) - far)
    for i in scalars:
        spaces[i] = pltpu.SMEM
    return pl.pallas_call(
        body,
        out_shape=shapes,
        in_specs=[pl.BlockSpec(memory_space=space) for space in spaces],
        out_specs=jax.tree.map(lambda _: pl.BlockSpec(memory_space=pltpu.VMEM), shapes),
        scratch_shapes=list(scratch),
        compiler_params=pltpu.CompilerParams(vmem_limit_bytes=32 * 2**20),
        cost_estimate=pl.CostEstimate(flops=flops, bytes_accessed=moved, transcendentals=0),
    )(*operands)


def block_side(blocks):
    return min(k for k in range(1, blocks + 1) if k * k * k >= blocks)


def from_block(array, side, *offset):
    pairs = []
    for i in range(lax.axis_size("space")):
        at = (i // (side * side), i // side % side, i % side)
        x, y, z = ((c + o) % side for c, o in zip(at, offset))
        pairs.append(((x * side + y) * side + z, i))
    return lax.ppermute(array, "space", pairs)


def both_sides(array, side, axis):
    below = from_block(array, side, *(-1 if a == axis else 0 for a in range(3)))
    if side == 2:
        return {-1: below, 1: below}
    return {-1: below, 1: from_block(array, side, *(1 if a == axis else 0 for a in range(3)))}


def swapped(array, axis, bit):
    size = lax.axis_size(axis)
    return lax.ppermute(array, axis, [(i, i ^ bit) for i in range(size)])


def stacked(parts):
    kept, starts, places = [], [], []
    rows = 0
    for part in parts:
        found = [i for i, a in enumerate(kept) if a is part]
        if not found:
            found = [len(kept)]
            kept.append(part)
            starts.append(rows)
            rows += part.shape[0]
        places.append(starts[found[0]])
    return jnp.concatenate(kept, axis=0), places


def operands_of(*tables):
    arrays, numbered = [], []
    for table in tables:
        new = {}
        for key, (array, row) in table.items():
            found = [i for i, a in enumerate(arrays) if a is array]
            if not found:
                found = [len(arrays)]
                arrays.append(array)
            new[key] = (found[0], row)
        numbered.append(new)
    return arrays, numbered


def local(inputs, mask_one, place_one, pooled_one, w_two, mask_two, place_two, grad_two):
    blocks = lax.axis_size("space")
    side = block_side(blocks)
    samples = inputs.shape[0]
    cells = inputs.shape[3]
    half_cells = HX * HY * HZ
    shape = jax.ShapeDtypeStruct
    vp_rows = 2 * samples * C_TWO
    four = 4 * samples * C_IN
    vp_row = BY * four
    to_x, own = call(
        functools.partial(prepare, samples),
        (shape((BY * four + vp_rows, LANES), bf16), shape((PACK, cells), bf16)),
        (grad_two, place_two, mask_two, inputs),
        far=4,
        flops=2 * 10**7,
        moved=2**20,
    )
    edge = call(
        functools.partial(ends, samples, vp_row),
        shape((C_TWO, LANES), bf16),
        (to_x, own),
        flops=10**7,
        moved=2**19,
    )
    chosen, folded_weights, expand, to_y = call(
        functools.partial(select_one, samples, vp_row),
        (
            shape((samples * C_ONE, cells), bf16),
            shape((9 * C_ONE, 3 * C_TWO), bf16),
            shape((2 * LANES, TABLE), bf16),
            shape((4 * four + vp_rows, LANES), bf16),
        ),
        (place_one, mask_one, w_two, to_x, own),
        far=3,
        flops=2 * 10**7,
        moved=3 * 2**20,
    )
    vp_at, edge_at, face_at, line_at = {(0, 0): (to_x, vp_row)}, {}, {}, {}
    from_x = both_sides(to_x, side, 0)
    edge_z = both_sides(edge, side, 2)
    if side == 2:
        diagonal = from_block(edge, side, 1, 0, 1)
        edge_x = {nz: {nx: diagonal for nx in (-1, 1)} for nz in (-1, 1)}
    else:
        edge_x = {nz: {nx: from_block(edge, side, nx, 0, nz) for nx in (-1, 1)} for nz in (-1, 1)}
    first = both_sides(to_y, side, 1)
    parts = []
    for n in (-1, 1):
        again = n == 1 and side == 2
        parts += parts[:2] if again else [from_x[n][vp_row:], from_x[n][: 2 * four]]
    second, starts = stacked(parts)
    second = both_sides(second, side, 1)
    parts = [edge_z[-1], edge_z[1]] + [edge_x[nz][nx] for nz in (-1, 1) for nx in (-1, 1)]
    third, edge_starts = stacked(parts)
    third = both_sides(third, side, 1)
    for n in (-1, 1):
        vp_at[n, 0] = (from_x[n], vp_row)
        face_at[n] = (from_x[n], 0)
        vp_at[0, n] = (first[n], 4 * four)
        line_at[0, n] = (first[n], 0)
        edge_at[0, 0, n] = (edge_z[n], 0)
        for i, nx in enumerate((-1, 1)):
            edge_at[nx, 0, n] = (edge_x[n][nx], 0)
            vp_at[nx, n] = (second[n], starts[2 * i])
            line_at[nx, n] = (second[n], starts[2 * i + 1])
        for i, nz in enumerate((-1, 1)):
            edge_at[0, n, nz] = (third[n], edge_starts[i])
            for j, nx in enumerate((-1, 1)):
                edge_at[nx, n, nz] = (third[n], edge_starts[2 + 2 * i + j])
    total = lax.axis_size("dp") * samples * blocks * cells

    def near(table, y):
        return {key: value for key, value in table.items() if key[1] in y}

    arrays, tables = operands_of(near(vp_at, (0,)), near(edge_at, (0,)))
    tiles, end_tiles = (HX + 2) * HY, (HX + 2) * 2
    part, total_two, moved_ends = call(
        functools.partial(layer_two_inside, samples, *tables),
        (
            shape((samples * C_ONE, half_cells), f32),
            shape((9 * C_ONE, 3 * C_TWO), f32),
            shape((samples, 9 * C_ONE, end_tiles * LANES), bf16),
        ),
        (*arrays, pooled_one, folded_weights, expand),
        scratch=(
            pltpu.VMEM((samples, 3 * C_TWO, tiles * LANES), bf16),
            pltpu.VMEM((samples, 9 * C_ONE, tiles * LANES), bf16),
        ),
        flops=5 * 10**8,
        moved=2**20,
    )
    arrays, tables = operands_of(face_at, near(edge_at, (0,)))
    ahead = call(
        functools.partial(layer_one_inside, samples, *tables),
        shape((3 * PACK, (BX + 2) * BY * BZ), bf16),
        (*arrays, own),
        flops=10**8,
        moved=2**20,
    )
    arrays, tables = operands_of(near(vp_at, (-1, 1)), near(edge_at, (-1, 1)))
    kept, sums = call(
        functools.partial(layer_two_ends, samples, float(total // 8) ** -0.5, *tables),
        (
            shape((samples * C_ONE, half_cells), bf16),
            shape((C_ONE, ONE_AT), f32),
        ),
        (*arrays, folded_weights, expand, part, total_two, moved_ends),
        scratch=(pltpu.VMEM((samples, 3 * C_TWO, end_tiles * LANES), bf16),),
        flops=5 * 10**8,
        moved=2**20,
    )
    arrays, tables = operands_of(line_at, near(edge_at, (-1, 1)))
    half = (lax.axis_index("dp") % 2).astype(i32).reshape(1)
    operands = (*arrays, own, ahead, kept, chosen, sums, half)
    half_sums = shape((HALF, WIDTH), f32)
    mine, other = call(
        functools.partial(layer_one, samples, float(total) ** -0.5, *tables),
        (half_sums, half_sums),
        operands,
        scratch=(
            pltpu.VMEM((3 * PACK, (BX + 2) * 2 * BZ), bf16),
            pltpu.VMEM((BX, 3 * samples * C_ONE, BY * BZ), bf16),
            pltpu.VMEM((BX, 3 * samples * C_ONE, 2 * BZ), bf16),
        ),
        flops=5 * 10**8,
        moved=2**20,
        scalars=(len(operands) - 1,),
    )
    grad_pooled = call(
        functools.partial(emit, samples),
        shape((samples, 1, C_ONE, half_cells), bf16),
        (kept,),
        flops=10**6,
        moved=2**18,
    )
    mine = mine + swapped(other, "dp", 1)
    for axis in ("dp", "space"):
        bit = 2 if axis == "dp" else 1
        while bit < lax.axis_size(axis):
            mine = mine + swapped(mine, axis, bit)
            bit *= 2
    grad_w_one, grad_w_two = call(
        finish,
        (shape((C_IN, C_ONE, 27), f32), shape((27, C_ONE, C_TWO), f32)),
        (half, mine, swapped(mine, "dp", 1)),
        scalars=(0,),
    )
    return grad_pooled, jnp.transpose(grad_w_one, (2, 0, 1)), grad_w_two


def solution(mesh):
    split = P("dp", "space", None, None)
    return jax.shard_map(
        local,
        mesh=mesh,
        in_specs=(split, split, split, split, P(), split, split, split),
        out_specs=(split, P(), P()),
        check_vma=False,
    )
```

```python
import functools

import jax
import jax.numpy as jnp
from jax import lax
from jax.experimental import pallas as pl
from jax.experimental.pallas import tpu as pltpu
from jax.sharding import PartitionSpec as P

C_IN = 4
C_ONE = 16
C_TWO = 32
BX = 4
BY = 8
BZ = 256
HX, HY, HZ = BX // 2, BY // 2, BZ // 2
QY, QZ = HY // 2, HZ // 2
LANES = 128
PACK = 16
ENDS_AT = LANES - 2 * BX * BY
OFFS = (-1, 0, 1)
GRAD_W_TWO = 27 * C_TWO
WIDTH = 1024
ONE_AT = WIDTH - LANES
STRIDE_ONE = LANES // C_IN
HALF = C_ONE // 2
TABLE = 3 * QY * LANES
NT = (((1,), (1,)), ((), ()))
f32, bf16, i32 = jnp.float32, jnp.bfloat16, jnp.int32


def iota(shape, dim):
    return lax.broadcasted_iota(i32, shape, dim)


def doubling():
    return (iota((LANES, 2 * LANES), 0) == iota((LANES, 2 * LANES), 1) // 2).astype(bf16)


def fetch(pairs, sems):
    copies = [pltpu.make_async_copy(a, b, sems.at[i]) for i, (a, b) in enumerate(pairs)]
    for copy in copies:
        copy.start()
    return copies


def prepare(samples, *refs):
    far, (to_x, own), near, sems = refs[:4], refs[4:6], refs[6:10], refs[10]
    grad, place, mask, source = near
    copies = fetch(tuple(zip(far, near)), sems)
    rows = samples * C_TWO
    table = doubling()
    copies[0].wait()
    copies[1].wait()
    values = jnp.dot(grad[...].reshape(rows, LANES), table, preferred_element_type=f32)
    spots = place[...].reshape(rows, LANES).astype(f32).astype(bf16)
    wide = jnp.dot(spots, table, preferred_element_type=f32)
    parity = (iota((rows, LANES), 1) % 2).astype(f32)
    copies[2].wait()
    halves = []
    for qy in range(QY):
        v = values[:, qy * LANES : (qy + 1) * LANES]
        p = wide[:, qy * LANES : (qy + 1) * LANES] - parity
        total = jnp.zeros((rows, LANES), f32)
        for x in range(HX):
            for dy in range(2):
                at = (x * HY + 2 * qy + dy) * LANES
                on = mask[:, 0, :, at : at + LANES].reshape(rows, LANES) == 1
                total = total + jnp.where(on & (p == 4.0 * x + 2.0 * dy), v, 0.0)
        halves.append(total)
    kept = jnp.concatenate(halves, axis=1).astype(bf16)
    v = lax.dot_general(kept, table, NT, preferred_element_type=f32).astype(bf16)
    used = samples * C_IN
    at = BY * 4 * used
    to_x[at : at + rows] = v
    to_x[at + rows : at + 2 * rows] = spots
    copies[3].wait()
    pieces = [source[s, 0].astype(f32) for s in range(samples)]
    if used < PACK:
        pieces.append(jnp.zeros((PACK - used, BX * BY * BZ), f32))
    cells = jnp.concatenate(pieces, axis=0)
    own[...] = cells.astype(bf16)
    for t in range(BY):
        group = []
        for x in (0, BX - 1):
            for y in (t // 2, BY - 1 - t // 2):
                at = (x * BY + y) * BZ + (t % 2) * LANES
                group.append(cells[0:used, at : at + LANES])
        to_x[4 * used * t : 4 * used * (t + 1)] = jnp.concatenate(group, axis=0).astype(bf16)


def ends(samples, vp_row, to_x, own, edge, to_y):
    rows = samples * C_TWO
    lane = iota((LANES, LANES), 0)
    spot = (lane // QZ) * 2 + (lane % QZ == QZ - 1).astype(i32)
    spot = jnp.where((lane % QZ == 0) | (lane % QZ == QZ - 1), spot, -LANES)
    column = iota((LANES, LANES), 1)
    packed = jnp.zeros((C_TWO, LANES), f32)
    for s in range(samples):
        for t in range(2):
            pick = (spot + (8 * s + 4 * t) == column).astype(bf16)
            at = vp_row + t * rows + s * C_TWO
            packed = packed + jnp.dot(to_x[at : at + C_TWO], pick, preferred_element_type=f32)
    lane = iota((PACK, LANES), 1)
    cells = packed[0:PACK]
    for row in range(BX * BY):
        left = own[:, row * BZ : row * BZ + LANES].astype(f32)
        right = own[:, (row + 1) * BZ - LANES : (row + 1) * BZ].astype(f32)
        cells = jnp.where(lane == ENDS_AT + 2 * row, left[:, 0:1], cells)
        cells = jnp.where(lane == ENDS_AT + 2 * row + 1, right[:, LANES - 1 :], cells)
    edge[0:PACK] = cells.astype(bf16)
    edge[PACK:] = packed[PACK:].astype(bf16)
    used = samples * C_IN
    to_y[4 * 4 * used :] = to_x[vp_row:]
    for t in range(4):
        group = []
        for x in range(BX):
            at = (x * BY + (BY - 1) * (t // 2)) * BZ + (t % 2) * LANES
            group.append(own[:, at : at + LANES].astype(f32)[0:used])
        to_y[4 * used * t : 4 * used * (t + 1)] = jnp.concatenate(group, axis=0).astype(bf16)


def select_one(samples, *refs):
    far, (chosen, folded_weights, expand), near, sems = refs[:3], refs[3:6], refs[6:9], refs[9]
    place, mask, weights = near
    copies = fetch(tuple(zip(far, near)), sems)
    k = iota((2 * LANES, TABLE), 0)
    j = iota((1, TABLE), 1)
    shift = j // (QY * LANES) - 1
    qy = (j // LANES) % QY
    z = j % LANES - shift
    beyond = LANES + qy * 2 + (z < 0).astype(i32)
    expand[...] = (k == jnp.where((z >= 0) & (z < LANES), qy * QZ + z // 2, beyond)).astype(bf16)
    rows = samples * C_ONE
    table = doubling()
    parity = (iota((rows, BZ), 1) % 2).astype(f32)
    copies[2].wait()
    folded_weights[...] = jnp.concatenate(
        [jnp.concatenate([weights[3 * o + i] for i in range(3)], axis=1) for o in range(9)], axis=0
    )
    copies[0].wait()
    copies[1].wait()
    for x in range(HX):
        for y in range(HY):
            at = (x * HY + y) * LANES
            spots = place[:, 0, :, at : at + LANES].reshape(rows, LANES).astype(f32).astype(bf16)
            wide = jnp.dot(spots, table, preferred_element_type=f32) - parity
            for dx in range(2):
                for dy in range(2):
                    to = ((2 * x + dx) * BY + 2 * y + dy) * BZ
                    on = mask[:, 0, :, to : to + BZ].reshape(rows, BZ) == 1
                    hit = on & (wide == 4.0 * dx + 2.0 * dy)
                    chosen[:, to : to + BZ] = jnp.where(hit, 1.0, 0.0).astype(bf16)


def expand_windows(samples, vp_at, edge_at, tile_of, blocks, expand, fields):
    rows = samples * C_TWO
    lane = iota((rows, LANES), 1)
    odd = iota((C_TWO, LANES), 1) % 2 == 1
    groups = {}
    for nx, ny in vp_at:
        key = (vp_at[nx, ny], edge_at[nx, ny, -1], edge_at[nx, ny, 1])
        groups.setdefault(key, []).append((nx, ny))
    for ((ref, at), low, high), places in groups.items():
        edge = blocks[low[0]][low[1] : low[1] + C_TWO].astype(f32)
        if low != high:
            other = blocks[high[0]][high[1] : high[1] + C_TWO].astype(f32)
            edge = jnp.where(odd, edge, other)
        parts = []
        for t in range(2):
            for s in range(samples):
                by = 8 * s + 4 * t
                parts.append(pltpu.roll(edge, LANES - by, 1) if by else edge)
        both = jnp.concatenate(
            [blocks[ref][at : at + 2 * rows], jnp.concatenate(parts, axis=0).astype(bf16)], axis=1
        )
        wide = jnp.dot(both, expand[...], preferred_element_type=f32)
        for i, oz in enumerate(OFFS):
            parity = ((lane - oz) & 1).astype(f32)
            for qy in range(QY):
                lanes = slice((i * QY + qy) * LANES, (i * QY + qy + 1) * LANES)
                v = wide[0:rows, lanes].astype(bf16)
                p = (wide[rows : 2 * rows, lanes] - parity).astype(bf16)
                for x in range(HX):
                    for dy in range(2):
                        y = 2 * qy + dy
                        spots = []
                        for nx, ny in places:
                            near_x = nx == 0 or x == (HX - 1 if nx < 0 else 0)
                            near_y = ny == 0 or y == (HY - 1 if ny < 0 else 0)
                            if near_x and near_y:
                                spots.append(tile_of[x + 1 + nx * HX, y + 1 + ny * HY])
                        if not spots:
                            continue
                        cells = jnp.where(p == 4.0 * x + 2.0 * dy, v, jnp.zeros_like(v))
                        for spot in spots:
                            for s in range(samples):
                                fields[s, i * C_TWO : (i + 1) * C_TWO, spot * LANES : (spot + 1) * LANES] = (
                                    cells[s * C_TWO : (s + 1) * C_TWO]
                                )


def tiles_own():
    return {(px, py): (px - 1) * HY + py - 1 for px in range(1, HX + 1) for py in range(1, HY + 1)}


def tiles_x():
    return {(px, py): (px > 0) * HY + py - 1 for px in (0, HX + 1) for py in range(1, HY + 1)}


def tiles_ends():
    return {(px, py): 2 * px + (py > 0) for px in range(HX + 2) for py in (0, HY + 1)}


def shift_pooled(samples, tile_of, pooled, moved):
    for (px, py), tile in tile_of.items():
        k = 0
        for ox in OFFS:
            for oy in OFFS:
                x, y = px - 1 + ox, py - 1 + oy
                inside = 0 <= x < HX and 0 <= y < HY
                for s in range(samples):
                    if inside:
                        at = (x * HY + y) * LANES
                        value = pooled[s, 0, :, at : at + LANES]
                    else:
                        value = jnp.zeros((C_ONE, LANES), bf16)
                    moved[s, k * C_ONE : (k + 1) * C_ONE, tile * LANES : (tile + 1) * LANES] = value
                k += 1


def products_two(samples, tile_of, fields, moved, weights, sums, totals):
    for s in range(samples):
        wide = jnp.dot(weights[...], fields[s], preferred_element_type=f32)
        for x in range(HX):
            for y in range(HY):
                k = 0
                for ox in OFFS:
                    for oy in OFFS:
                        tile = tile_of.get((x + 1 - ox, y + 1 - oy))
                        if tile is not None:
                            part = wide[k * C_ONE : (k + 1) * C_ONE, tile * LANES : (tile + 1) * LANES]
                            old = sums[s].get((x, y))
                            sums[s][x, y] = part if old is None else old + part
                        k += 1
        totals = totals + lax.dot_general(moved[s], fields[s], NT, preferred_element_type=f32)
    return totals


def parts_of(samples, part):
    return [
        {
            (x, y): part[s * C_ONE : (s + 1) * C_ONE, (x * HY + y) * LANES : (x * HY + y + 1) * LANES]
            for x in range(HX)
            for y in range(HY)
        }
        for s in range(samples)
    ]


def store_parts(sums, part):
    for s, tiles in enumerate(sums):
        for (x, y), value in tiles.items():
            at = (x * HY + y) * LANES
            part[s * C_ONE : (s + 1) * C_ONE, at : at + LANES] = value.astype(part.dtype)


def layer_two_own(samples, vp_at, edge_at, *refs):
    blocks, (pooled, weights, expand, part, total, moved_x, moved_ends, fields, moved) = refs[:-9], refs[-9:]
    tile_of = tiles_own()
    expand_windows(samples, vp_at, edge_at, tile_of, blocks, expand, fields)
    shift_pooled(samples, tile_of, pooled, moved)
    shift_pooled(samples, tiles_x(), pooled, moved_x)
    shift_pooled(samples, tiles_ends(), pooled, moved_ends)
    sums = [{} for _ in range(samples)]
    totals = jnp.zeros((9 * C_ONE, 3 * C_TWO), f32)
    total[...] = products_two(samples, tile_of, fields, moved, weights, sums, totals)
    store_parts(sums, part)


def layer_two_x(samples, vp_at, edge_at, *refs):
    blocks, (weights, expand, old, old_total, moved, part, total, fields) = refs[:-8], refs[-8:]
    tile_of = tiles_x()
    expand_windows(samples, vp_at, edge_at, tile_of, blocks, expand, fields)
    sums = parts_of(samples, old)
    total[...] = products_two(samples, tile_of, fields, moved, weights, sums, old_total[...])
    store_parts(sums, part)


def layer_two_ends(samples, scale, vp_at, edge_at, *refs):
    blocks, (weights, expand, part, total, moved, kept, message, fields) = refs[:-8], refs[-8:]
    tile_of = tiles_ends()
    expand_windows(samples, vp_at, edge_at, tile_of, blocks, expand, fields)
    sums = parts_of(samples, part)
    totals = products_two(samples, tile_of, fields, moved, weights, sums, total[...]) * scale
    store_parts(sums, kept)
    width = 3 * C_TWO
    for k in range(9):
        message[:, k * width : (k + 1) * width] = totals[k * C_ONE : (k + 1) * C_ONE]
    message[:, GRAD_W_TWO:ONE_AT] = jnp.zeros((C_ONE, ONE_AT - GRAD_W_TWO), f32)


def shift_input(samples, rows_of, face_at, line_at, edge_at, blocks, own, ahead):
    used = samples * C_IN
    lane = iota((PACK, BZ), 1)
    for (px, py), line in rows_of.items():
        nx = -1 if px == 0 else 1 if px == BX + 1 else 0
        ny = -1 if py == 0 else 1 if py == BY + 1 else 0
        x, y = (px - 1) % BX, (py - 1) % BY
        if nx == 0 and ny == 0:
            row = own[:, (x * BY + y) * BZ : (x * BY + y + 1) * BZ].astype(f32)
        else:
            if nx != 0:
                ref, at = face_at[nx] if ny == 0 else line_at[nx, ny]
                tile = 2 * min(y, BY - 1 - y)
                chunk = 2 * (0 if x == 0 else 1) + (1 if y >= BY // 2 else 0)
            else:
                ref, at = line_at[nx, ny]
                tile = 2 * (0 if y == 0 else 1)
                chunk = x
            halves = []
            for t in (tile, tile + 1):
                four = blocks[ref][at + 4 * used * t : at + 4 * used * (t + 1)].astype(f32)
                halves.append(four[chunk * used : (chunk + 1) * used])
            row = jnp.concatenate(halves, axis=1)
            if used < PACK:
                row = jnp.concatenate([row, jnp.zeros((PACK - used, BZ), f32)], axis=0)
        ends = []
        for nz in (-1, 1):
            ref, at = edge_at[nx, ny, nz]
            ends.append(blocks[ref][at : at + PACK].astype(f32))
        at = ENDS_AT + 2 * (x * BY + y)
        to = line * BZ
        before = jnp.where(lane == 0, ends[0][:, at + 1 : at + 2], pltpu.roll(row, 1, 1))
        after = jnp.where(lane == BZ - 1, ends[1][:, at : at + 1], pltpu.roll(row, BZ - 1, 1))
        for i, piece in enumerate((before, row, after)):
            ahead[i * PACK : (i + 1) * PACK, to : to + BZ] = piece.astype(bf16)


def lines_inside():
    return {(px, py): px * BY + py - 1 for px in range(BX + 2) for py in range(1, BY + 1)}


def lines_ends():
    return {(px, py): 2 * px + (py > 0) for px in range(BX + 2) for py in (0, BY + 1)}


def emit(samples, kept, out):
    for s in range(samples):
        out[s, 0] = kept[s * C_ONE : (s + 1) * C_ONE]


def layer_one_inside(samples, face_at, edge_at, *refs):
    blocks, (own, ahead) = refs[:-2], refs[-2:]
    shift_input(samples, lines_inside(), face_at, {}, edge_at, blocks, own, ahead)


def layer_one(samples, scale, line_at, edge_at, *refs):
    blocks, (own, ahead, grad, chosen, before_sums, half, mine, other, ahead_ends, inside, ends) = refs[:-11], refs[-11:]
    shift_input(samples, lines_ends(), {}, line_at, edge_at, blocks, own, ahead_ends)
    rows = samples * C_ONE
    table = doubling()
    empty = jnp.zeros((rows, BZ), bf16)
    for x in range(BX):
        inside[x, 0:rows, (BY - 1) * BZ :] = empty
        inside[x, 2 * rows :, 0:BZ] = empty
        ends[x, 0:rows, BZ:] = empty
        ends[x, rows : 2 * rows, 0:BZ] = empty
        ends[x, rows : 2 * rows, BZ:] = empty
        ends[x, 2 * rows :, 0:BZ] = empty
    for x in range(HX):
        for y in range(HY):
            at = (x * HY + y) * LANES
            wide = jnp.dot(grad[:, at : at + LANES], table, preferred_element_type=f32).astype(bf16)
            for dx in range(2):
                for dy in range(2):
                    cx, cy = 2 * x + dx, 2 * y + dy
                    value = wide * chosen[:, (cx * BY + cy) * BZ : (cx * BY + cy + 1) * BZ]
                    for j, oy in enumerate(OFFS):
                        to = cy + oy
                        here = slice(j * rows, (j + 1) * rows)
                        if to < 0:
                            ends[cx, here, 0:BZ] = value
                        elif to >= BY:
                            ends[cx, here, BZ:] = value
                        else:
                            inside[cx, here, to * BZ : (to + 1) * BZ] = value
    width = 3 * 3 * PACK
    product = jnp.zeros((3 * rows, width), f32)
    for x in range(BX):
        for left, right, size in ((inside, ahead, BY * BZ), (ends, ahead_ends, 2 * BZ)):
            pieces = [right[:, (x + 1 + ox) * size : (x + 2 + ox) * size] for ox in OFFS]
            product = product + lax.dot_general(
                left[x], jnp.concatenate(pieces, axis=0), NT, preferred_element_type=f32
            )
    sample_of = (iota((C_ONE, width), 1) % PACK) // C_IN
    k = iota((width, LANES), 0)
    to = (k % C_IN) * STRIDE_ONE + (k // (3 * PACK)) * 9 + (k // PACK) % 3
    total = jnp.zeros((C_ONE, LANES), f32)
    for j in range(3):
        folded = jnp.zeros((C_ONE, width), f32)
        for s in range(samples):
            at = j * rows + s * C_ONE
            folded = folded + jnp.where(sample_of == s, product[at : at + C_ONE], 0.0)
        fold = (to + 3 * j == iota((width, LANES), 1)).astype(bf16)
        parts = []
        for _ in range(3):
            parts.append(folded.astype(bf16))
            folded = folded - parts[-1].astype(f32)
        got = jnp.dot(jnp.concatenate(parts, axis=0), fold, preferred_element_type=f32)
        total = total + (got[2 * C_ONE :] + got[C_ONE : 2 * C_ONE] + got[0:C_ONE])
    sums = jnp.concatenate([before_sums[...], total * scale], axis=1)
    top, bottom = sums[0:HALF], sums[HALF:]
    first = half[0] == 0
    mine[...] = jnp.where(first, top, bottom)
    other[...] = jnp.where(first, bottom, top)


def finish(half, mine, theirs, grad_one, grad_two):
    first = half[0] == 0
    top = jnp.where(first, mine[...], theirs[...])
    bottom = jnp.where(first, theirs[...], mine[...])
    for rows, part in ((slice(0, HALF), top), (slice(HALF, C_ONE), bottom)):
        for o in range(27):
            grad_two[o, rows] = part[:, o * C_TWO : (o + 1) * C_TWO]
        for c in range(C_IN):
            at = ONE_AT + c * STRIDE_ONE
            grad_one[c, rows] = part[:, at : at + 27]


def call(body, shapes, operands, far=0, scratch=(), flops=0, moved=0, scalars=()):
    if far:
        scratch = [pltpu.VMEM(a.shape, a.dtype) for a in operands[:far]]
        scratch.append(pltpu.SemaphoreType.DMA((far,)))
        away = [pltpu.with_memory_space_constraint(a, pltpu.HBM) for a in operands[:far]]
        operands = (*away, *operands[far:])
    spaces = [pltpu.HBM] * far + [pltpu.VMEM] * (len(operands) - far)
    for i in scalars:
        spaces[i] = pltpu.SMEM
    return pl.pallas_call(
        body,
        out_shape=shapes,
        in_specs=[pl.BlockSpec(memory_space=space) for space in spaces],
        out_specs=jax.tree.map(lambda _: pl.BlockSpec(memory_space=pltpu.VMEM), shapes),
        scratch_shapes=list(scratch),
        compiler_params=pltpu.CompilerParams(vmem_limit_bytes=32 * 2**20),
        cost_estimate=pl.CostEstimate(flops=flops, bytes_accessed=moved, transcendentals=0),
    )(*operands)


def block_side(blocks):
    return min(k for k in range(1, blocks + 1) if k * k * k >= blocks)


def from_block(array, side, *offset):
    pairs = []
    for i in range(lax.axis_size("space")):
        at = (i // (side * side), i // side % side, i % side)
        x, y, z = ((c + o) % side for c, o in zip(at, offset))
        pairs.append(((x * side + y) * side + z, i))
    return lax.ppermute(array, "space", pairs)


def both_sides(array, side, axis):
    below = from_block(array, side, *(-1 if a == axis else 0 for a in range(3)))
    if side == 2:
        return {-1: below, 1: below}
    return {-1: below, 1: from_block(array, side, *(1 if a == axis else 0 for a in range(3)))}


def swapped(array, bits):
    devices = lax.axis_size("dp") * lax.axis_size("space")
    return lax.ppermute(array, ("dp", "space"), [(i, i ^ bits) for i in range(devices)])


def stacked(parts):
    kept, starts, places = [], [], []
    rows = 0
    for part in parts:
        found = [i for i, a in enumerate(kept) if a is part]
        if not found:
            found = [len(kept)]
            kept.append(part)
            starts.append(rows)
            rows += part.shape[0]
        places.append(starts[found[0]])
    return jnp.concatenate(kept, axis=0), places


def operands_of(*tables):
    arrays, numbered = [], []
    for table in tables:
        new = {}
        for key, (array, row) in table.items():
            found = [i for i, a in enumerate(arrays) if a is array]
            if not found:
                found = [len(arrays)]
                arrays.append(array)
            new[key] = (found[0], row)
        numbered.append(new)
    return arrays, numbered


def local(inputs, mask_one, place_one, pooled_one, w_two, mask_two, place_two, grad_two):
    blocks = lax.axis_size("space")
    side = block_side(blocks)
    samples = inputs.shape[0]
    cells = inputs.shape[3]
    half_cells = HX * HY * HZ
    shape = jax.ShapeDtypeStruct
    vp_rows = 2 * samples * C_TWO
    four = 4 * samples * C_IN
    vp_row = BY * four
    to_x, own = call(
        functools.partial(prepare, samples),
        (shape((BY * four + vp_rows, LANES), bf16), shape((PACK, cells), bf16)),
        (grad_two, place_two, mask_two, inputs),
        far=4,
        flops=2 * 10**7,
        moved=2**20,
    )
    edge, to_y = call(
        functools.partial(ends, samples, vp_row),
        (shape((C_TWO, LANES), bf16), shape((4 * four + vp_rows, LANES), bf16)),
        (to_x, own),
        flops=10**7,
        moved=2**19,
    )
    chosen, folded_weights, expand = call(
        functools.partial(select_one, samples),
        (
            shape((samples * C_ONE, cells), bf16),
            shape((9 * C_ONE, 3 * C_TWO), bf16),
            shape((2 * LANES, TABLE), bf16),
        ),
        (place_one, mask_one, w_two),
        far=3,
        flops=2 * 10**7,
        moved=3 * 2**20,
    )
    vp_at, edge_at, face_at, line_at = {(0, 0): (to_x, vp_row)}, {}, {}, {}
    from_x = both_sides(to_x, side, 0)
    edge_z = both_sides(edge, side, 2)
    if side == 2:
        diagonal = from_block(edge, side, 1, 0, 1)
        edge_x = {nz: {nx: diagonal for nx in (-1, 1)} for nz in (-1, 1)}
    else:
        edge_x = {nz: {nx: from_block(edge, side, nx, 0, nz) for nx in (-1, 1)} for nz in (-1, 1)}
    first = both_sides(to_y, side, 1)
    end_tiles, x_tiles = (HX + 2) * 2, 2 * HY
    part_shape = shape((samples * C_ONE, half_cells), f32)
    total_shape = shape((9 * C_ONE, 3 * C_TWO), f32)
    arrays, tables = operands_of({(0, 0): vp_at[0, 0]}, {(0, 0, n): (edge_z[n], 0) for n in (-1, 1)})
    part, total_two, moved_x, moved_ends = call(
        functools.partial(layer_two_own, samples, *tables),
        (
            part_shape,
            total_shape,
            shape((samples, 9 * C_ONE, x_tiles * LANES), bf16),
            shape((samples, 9 * C_ONE, end_tiles * LANES), bf16),
        ),
        (*arrays, pooled_one, folded_weights, expand),
        scratch=(
            pltpu.VMEM((samples, 3 * C_TWO, half_cells), bf16),
            pltpu.VMEM((samples, 9 * C_ONE, half_cells), bf16),
        ),
        flops=5 * 10**8,
        moved=2**20,
    )
    ready = {n: lax.optimization_barrier((from_x[n], total_two))[0] for n in ((-1,) if side == 2 else (-1, 1))}
    parts = []
    for n in (-1, 1):
        again = n == 1 and side == 2
        parts += parts[:2] if again else [ready[n][vp_row:], ready[n][: 2 * four]]
    second, starts = stacked(parts)
    second = both_sides(second, side, 1)
    parts = [edge_z[-1], edge_z[1]] + [edge_x[nz][nx] for nz in (-1, 1) for nx in (-1, 1)]
    third, edge_starts = stacked(parts)
    third = both_sides(third, side, 1)
    for n in (-1, 1):
        vp_at[n, 0] = (from_x[n], vp_row)
        face_at[n] = (from_x[n], 0)
        vp_at[0, n] = (first[n], 4 * four)
        line_at[0, n] = (first[n], 0)
        edge_at[0, 0, n] = (edge_z[n], 0)
        for i, nx in enumerate((-1, 1)):
            edge_at[nx, 0, n] = (edge_x[n][nx], 0)
            vp_at[nx, n] = (second[n], starts[2 * i])
            line_at[nx, n] = (second[n], starts[2 * i + 1])
        for i, nz in enumerate((-1, 1)):
            edge_at[0, n, nz] = (third[n], edge_starts[i])
            for j, nx in enumerate((-1, 1)):
                edge_at[nx, n, nz] = (third[n], edge_starts[2 + 2 * i + j])
    total = lax.axis_size("dp") * samples * blocks * cells

    def near(table, y):
        return {key: value for key, value in table.items() if key[1] in y}

    arrays, tables = operands_of(
        {(n, 0): vp_at[n, 0] for n in (-1, 1)}, {key: edge_at[key] for key in edge_at if key[0] != 0 and key[1] == 0}
    )
    part, total_two = call(
        functools.partial(layer_two_x, samples, *tables),
        (part_shape, total_shape),
        (*arrays, folded_weights, expand, part, total_two, moved_x),
        scratch=(pltpu.VMEM((samples, 3 * C_TWO, x_tiles * LANES), bf16),),
        flops=5 * 10**8,
        moved=2**20,
    )
    arrays, tables = operands_of(face_at, near(edge_at, (0,)))
    ahead = call(
        functools.partial(layer_one_inside, samples, *tables),
        shape((3 * PACK, (BX + 2) * BY * BZ), bf16),
        (*arrays, own),
        flops=10**8,
        moved=2**20,
    )
    arrays, tables = operands_of(near(vp_at, (-1, 1)), near(edge_at, (-1, 1)))
    kept, sums = call(
        functools.partial(layer_two_ends, samples, float(total // 8) ** -0.5, *tables),
        (
            shape((samples * C_ONE, half_cells), bf16),
            shape((C_ONE, ONE_AT), f32),
        ),
        (*arrays, folded_weights, expand, part, total_two, moved_ends),
        scratch=(pltpu.VMEM((samples, 3 * C_TWO, end_tiles * LANES), bf16),),
        flops=5 * 10**8,
        moved=2**20,
    )
    arrays, tables = operands_of(line_at, near(edge_at, (-1, 1)))
    half = (lax.axis_index("dp") % 2).astype(i32).reshape(1)
    operands = (*arrays, own, ahead, kept, chosen, sums, half)
    half_sums = shape((HALF, WIDTH), f32)
    mine, other = call(
        functools.partial(layer_one, samples, float(total) ** -0.5, *tables),
        (half_sums, half_sums),
        operands,
        scratch=(
            pltpu.VMEM((3 * PACK, (BX + 2) * 2 * BZ), bf16),
            pltpu.VMEM((BX, 3 * samples * C_ONE, BY * BZ), bf16),
            pltpu.VMEM((BX, 3 * samples * C_ONE, 2 * BZ), bf16),
        ),
        flops=5 * 10**8,
        moved=2**20,
        scalars=(len(operands) - 1,),
    )
    grad_pooled = call(
        functools.partial(emit, samples),
        shape((samples, 1, C_ONE, half_cells), bf16),
        (kept,),
        flops=10**6,
        moved=2**18,
    )
    mine = mine + swapped(other, blocks)
    devices = lax.axis_size("dp") * blocks
    bits = [1 << k for k in range(devices.bit_length() - 1) if 1 << k > blocks]
    bits += [1 << k for k in range(devices.bit_length() - 1) if 1 << k < blocks]
    while len(bits) > 1:
        (a, b), bits = bits[:2], bits[2:]
        mine = (mine + swapped(mine, a ^ b)) + (swapped(mine, a) + swapped(mine, b))
    for a in bits:
        mine = mine + swapped(mine, a)
    grad_w_one, grad_w_two = call(
        finish,
        (shape((C_IN, C_ONE, 27), f32), shape((27, C_ONE, C_TWO), f32)),
        (half, mine, swapped(mine, blocks)),
        scalars=(0,),
    )
    return grad_pooled, jnp.transpose(grad_w_one, (2, 0, 1)), grad_w_two


def solution(mesh):
    split = P("dp", "space", None, None)
    return jax.shard_map(
        local,
        mesh=mesh,
        in_specs=(split, split, split, split, P(), split, split, split),
        out_specs=(split, P(), P()),
        check_vma=False,
    )
```

```python
import functools

import jax
import jax.numpy as jnp
from jax import lax
from jax.experimental import pallas as pl
from jax.experimental.pallas import tpu as pltpu
from jax.sharding import PartitionSpec as P

C_IN = 4
C_ONE = 16
C_TWO = 32
BX = 4
BY = 8
BZ = 256
HX, HY, HZ = BX // 2, BY // 2, BZ // 2
QY, QZ = HY // 2, HZ // 2
LANES = 128
PACK = 16
ENDS_AT = LANES - 2 * BX * BY
OFFS = (-1, 0, 1)
GRAD_W_TWO = 27 * C_TWO
WIDTH = 1024
ONE_AT = WIDTH - LANES
STRIDE_ONE = LANES // C_IN
HALF = C_ONE // 2
TABLE = 3 * QY * LANES
NT = (((1,), (1,)), ((), ()))
f32, bf16, i32 = jnp.float32, jnp.bfloat16, jnp.int32


def iota(shape, dim):
    return lax.broadcasted_iota(i32, shape, dim)


def doubling():
    return (iota((LANES, 2 * LANES), 0) == iota((LANES, 2 * LANES), 1) // 2).astype(bf16)


def fetch(pairs, sems):
    copies = [pltpu.make_async_copy(a, b, sems.at[i]) for i, (a, b) in enumerate(pairs)]
    for copy in copies:
        copy.start()
    return copies


def prepare(samples, *refs):
    far, (to_x, own), near, sems = refs[:4], refs[4:6], refs[6:10], refs[10]
    grad, place, mask, source = near
    copies = fetch(tuple(zip(far, near)), sems)
    rows = samples * C_TWO
    table = doubling()
    copies[0].wait()
    copies[1].wait()
    values = jnp.dot(grad[...].reshape(rows, LANES), table, preferred_element_type=f32)
    spots = place[...].reshape(rows, LANES).astype(f32).astype(bf16)
    wide = jnp.dot(spots, table, preferred_element_type=f32)
    parity = (iota((rows, LANES), 1) % 2).astype(f32)
    copies[2].wait()
    halves = []
    for qy in range(QY):
        v = values[:, qy * LANES : (qy + 1) * LANES]
        p = wide[:, qy * LANES : (qy + 1) * LANES] - parity
        total = jnp.zeros((rows, LANES), f32)
        for x in range(HX):
            for dy in range(2):
                at = (x * HY + 2 * qy + dy) * LANES
                on = mask[:, 0, :, at : at + LANES].reshape(rows, LANES) == 1
                total = total + jnp.where(on & (p == 4.0 * x + 2.0 * dy), v, 0.0)
        halves.append(total)
    kept = jnp.concatenate(halves, axis=1).astype(bf16)
    v = lax.dot_general(kept, table, NT, preferred_element_type=f32).astype(bf16)
    used = samples * C_IN
    at = BY * 4 * used
    to_x[at : at + rows] = v
    to_x[at + rows : at + 2 * rows] = spots
    copies[3].wait()
    pieces = [source[s, 0].astype(f32) for s in range(samples)]
    if used < PACK:
        pieces.append(jnp.zeros((PACK - used, BX * BY * BZ), f32))
    cells = jnp.concatenate(pieces, axis=0)
    own[...] = cells.astype(bf16)
    for t in range(BY):
        group = []
        for x in (0, BX - 1):
            for y in (t // 2, BY - 1 - t // 2):
                at = (x * BY + y) * BZ + (t % 2) * LANES
                group.append(cells[0:used, at : at + LANES])
        to_x[4 * used * t : 4 * used * (t + 1)] = jnp.concatenate(group, axis=0).astype(bf16)


def ends(samples, vp_row, to_x, own, edge, to_y):
    rows = samples * C_TWO
    lane = iota((LANES, LANES), 0)
    spot = (lane // QZ) * 2 + (lane % QZ == QZ - 1).astype(i32)
    spot = jnp.where((lane % QZ == 0) | (lane % QZ == QZ - 1), spot, -LANES)
    column = iota((LANES, LANES), 1)
    packed = jnp.zeros((C_TWO, LANES), f32)
    for s in range(samples):
        for t in range(2):
            pick = (spot + (8 * s + 4 * t) == column).astype(bf16)
            at = vp_row + t * rows + s * C_TWO
            packed = packed + jnp.dot(to_x[at : at + C_TWO], pick, preferred_element_type=f32)
    lane = iota((PACK, LANES), 1)
    cells = packed[0:PACK]
    for row in range(BX * BY):
        left = own[:, row * BZ : row * BZ + LANES].astype(f32)
        right = own[:, (row + 1) * BZ - LANES : (row + 1) * BZ].astype(f32)
        cells = jnp.where(lane == ENDS_AT + 2 * row, left[:, 0:1], cells)
        cells = jnp.where(lane == ENDS_AT + 2 * row + 1, right[:, LANES - 1 :], cells)
    edge[0:PACK] = cells.astype(bf16)
    edge[PACK:] = packed[PACK:].astype(bf16)
    used = samples * C_IN
    to_y[4 * 4 * used :] = to_x[vp_row:]
    for t in range(4):
        group = []
        for x in range(BX):
            at = (x * BY + (BY - 1) * (t // 2)) * BZ + (t % 2) * LANES
            group.append(own[:, at : at + LANES].astype(f32)[0:used])
        to_y[4 * used * t : 4 * used * (t + 1)] = jnp.concatenate(group, axis=0).astype(bf16)


def select_one(samples, *refs):
    far, (chosen, folded_weights, expand), near, sems = refs[:3], refs[3:6], refs[6:9], refs[9]
    place, mask, weights = near
    copies = fetch(tuple(zip(far, near)), sems)
    k = iota((2 * LANES, TABLE), 0)
    j = iota((1, TABLE), 1)
    shift = j // (QY * LANES) - 1
    qy = (j // LANES) % QY
    z = j % LANES - shift
    beyond = LANES + qy * 2 + (z < 0).astype(i32)
    expand[...] = (k == jnp.where((z >= 0) & (z < LANES), qy * QZ + z // 2, beyond)).astype(bf16)
    rows = samples * C_ONE
    table = doubling()
    parity = (iota((rows, BZ), 1) % 2).astype(f32)
    copies[2].wait()
    folded_weights[...] = jnp.concatenate(
        [jnp.concatenate([weights[3 * o + i] for i in range(3)], axis=1) for o in range(9)], axis=0
    )
    copies[0].wait()
    copies[1].wait()
    for x in range(HX):
        for y in range(HY):
            at = (x * HY + y) * LANES
            spots = place[:, 0, :, at : at + LANES].reshape(rows, LANES).astype(f32).astype(bf16)
            wide = jnp.dot(spots, table, preferred_element_type=f32) - parity
            for dx in range(2):
                for dy in range(2):
                    to = ((2 * x + dx) * BY + 2 * y + dy) * BZ
                    on = mask[:, 0, :, to : to + BZ].reshape(rows, BZ) == 1
                    hit = on & (wide == 4.0 * dx + 2.0 * dy)
                    chosen[:, to : to + BZ] = jnp.where(hit, 1.0, 0.0).astype(bf16)


def expand_windows(samples, vp_at, edge_at, tile_of, blocks, expand, fields):
    rows = samples * C_TWO
    lane = iota((rows, LANES), 1)
    odd = iota((C_TWO, LANES), 1) % 2 == 1
    groups = {}
    for nx, ny in vp_at:
        key = (vp_at[nx, ny], edge_at[nx, ny, -1], edge_at[nx, ny, 1])
        groups.setdefault(key, []).append((nx, ny))
    for ((ref, at), low, high), places in groups.items():
        edge = blocks[low[0]][low[1] : low[1] + C_TWO].astype(f32)
        if low != high:
            other = blocks[high[0]][high[1] : high[1] + C_TWO].astype(f32)
            edge = jnp.where(odd, edge, other)
        parts = []
        for t in range(2):
            for s in range(samples):
                by = 8 * s + 4 * t
                parts.append(pltpu.roll(edge, LANES - by, 1) if by else edge)
        both = jnp.concatenate(
            [blocks[ref][at : at + 2 * rows], jnp.concatenate(parts, axis=0).astype(bf16)], axis=1
        )
        wide = jnp.dot(both, expand[...], preferred_element_type=f32)
        for i, oz in enumerate(OFFS):
            parity = ((lane - oz) & 1).astype(f32)
            for qy in range(QY):
                lanes = slice((i * QY + qy) * LANES, (i * QY + qy + 1) * LANES)
                v = wide[0:rows, lanes].astype(bf16)
                p = (wide[rows : 2 * rows, lanes] - parity).astype(bf16)
                for x in range(HX):
                    for dy in range(2):
                        y = 2 * qy + dy
                        spots = []
                        for nx, ny in places:
                            near_x = nx == 0 or x == (HX - 1 if nx < 0 else 0)
                            near_y = ny == 0 or y == (HY - 1 if ny < 0 else 0)
                            if near_x and near_y:
                                spots.append(tile_of[x + 1 + nx * HX, y + 1 + ny * HY])
                        if not spots:
                            continue
                        cells = jnp.where(p == 4.0 * x + 2.0 * dy, v, jnp.zeros_like(v))
                        for spot in spots:
                            for s in range(samples):
                                fields[s, i * C_TWO : (i + 1) * C_TWO, spot * LANES : (spot + 1) * LANES] = (
                                    cells[s * C_TWO : (s + 1) * C_TWO]
                                )


def tiles_own():
    return {(px, py): (px - 1) * HY + py - 1 for px in range(1, HX + 1) for py in range(1, HY + 1)}


def tiles_sides():
    tiles = [(px, py) for px in (0, HX + 1) for py in range(1, HY + 1)]
    tiles += [(px, py) for px in range(1, HX + 1) for py in (0, HY + 1)]
    return {key: i for i, key in enumerate(tiles)}


def tiles_corners():
    return {(px, py): 2 * (px > 0) + (py > 0) for px in (0, HX + 1) for py in (0, HY + 1)}


def shift_pooled(samples, tile_of, pooled, moved):
    for (px, py), tile in tile_of.items():
        k = 0
        for ox in OFFS:
            for oy in OFFS:
                x, y = px - 1 + ox, py - 1 + oy
                inside = 0 <= x < HX and 0 <= y < HY
                for s in range(samples):
                    if inside:
                        at = (x * HY + y) * LANES
                        value = pooled[s, 0, :, at : at + LANES]
                    else:
                        value = jnp.zeros((C_ONE, LANES), bf16)
                    moved[s, k * C_ONE : (k + 1) * C_ONE, tile * LANES : (tile + 1) * LANES] = value
                k += 1


def products_two(samples, tile_of, fields, moved, weights, sums, totals):
    for s in range(samples):
        wide = jnp.dot(weights[...], fields[s], preferred_element_type=f32)
        for x in range(HX):
            for y in range(HY):
                k = 0
                for ox in OFFS:
                    for oy in OFFS:
                        tile = tile_of.get((x + 1 - ox, y + 1 - oy))
                        if tile is not None:
                            part = wide[k * C_ONE : (k + 1) * C_ONE, tile * LANES : (tile + 1) * LANES]
                            old = sums[s].get((x, y))
                            sums[s][x, y] = part if old is None else old + part
                        k += 1
        totals = totals + lax.dot_general(moved[s], fields[s], NT, preferred_element_type=f32)
    return totals


def parts_of(samples, part):
    return [
        {
            (x, y): part[s * C_ONE : (s + 1) * C_ONE, (x * HY + y) * LANES : (x * HY + y + 1) * LANES]
            for x in range(HX)
            for y in range(HY)
        }
        for s in range(samples)
    ]


def store_parts(sums, part):
    for s, tiles in enumerate(sums):
        for (x, y), value in tiles.items():
            at = (x * HY + y) * LANES
            part[s * C_ONE : (s + 1) * C_ONE, at : at + LANES] = value.astype(part.dtype)


def layer_two_own(samples, vp_at, edge_at, *refs):
    blocks, (pooled, weights, expand, part, total, fields, moved) = refs[:-7], refs[-7:]
    tile_of = tiles_own()
    expand_windows(samples, vp_at, edge_at, tile_of, blocks, expand, fields)
    shift_pooled(samples, tile_of, pooled, moved)
    sums = [{} for _ in range(samples)]
    totals = jnp.zeros((9 * C_ONE, 3 * C_TWO), f32)
    total[...] = products_two(samples, tile_of, fields, moved, weights, sums, totals)
    store_parts(sums, part)


def layer_two_sides(samples, vp_at, edge_at, *refs):
    blocks, (pooled, weights, expand, old, old_total, part, total, fields, moved) = refs[:-9], refs[-9:]
    tile_of = tiles_sides()
    expand_windows(samples, vp_at, edge_at, tile_of, blocks, expand, fields)
    shift_pooled(samples, tile_of, pooled, moved)
    sums = parts_of(samples, old)
    total[...] = products_two(samples, tile_of, fields, moved, weights, sums, old_total[...])
    store_parts(sums, part)


def layer_two_corners(samples, scale, vp_at, edge_at, *refs):
    blocks, (pooled, weights, expand, part, total, kept, message, fields, moved) = refs[:-9], refs[-9:]
    tile_of = tiles_corners()
    expand_windows(samples, vp_at, edge_at, tile_of, blocks, expand, fields)
    shift_pooled(samples, tile_of, pooled, moved)
    sums = parts_of(samples, part)
    totals = products_two(samples, tile_of, fields, moved, weights, sums, total[...]) * scale
    store_parts(sums, kept)
    width = 3 * C_TWO
    for k in range(9):
        message[:, k * width : (k + 1) * width] = totals[k * C_ONE : (k + 1) * C_ONE]
    message[:, GRAD_W_TWO:ONE_AT] = jnp.zeros((C_ONE, ONE_AT - GRAD_W_TWO), f32)


def shift_input(samples, rows_of, face_at, line_at, edge_at, blocks, own, ahead):
    used = samples * C_IN
    lane = iota((PACK, BZ), 1)
    for (px, py), line in rows_of.items():
        nx = -1 if px == 0 else 1 if px == BX + 1 else 0
        ny = -1 if py == 0 else 1 if py == BY + 1 else 0
        x, y = (px - 1) % BX, (py - 1) % BY
        if nx == 0 and ny == 0:
            row = own[:, (x * BY + y) * BZ : (x * BY + y + 1) * BZ].astype(f32)
        else:
            if nx != 0:
                ref, at = face_at[nx] if ny == 0 else line_at[nx, ny]
                tile = 2 * min(y, BY - 1 - y)
                chunk = 2 * (0 if x == 0 else 1) + (1 if y >= BY // 2 else 0)
            else:
                ref, at = line_at[nx, ny]
                tile = 2 * (0 if y == 0 else 1)
                chunk = x
            halves = []
            for t in (tile, tile + 1):
                four = blocks[ref][at + 4 * used * t : at + 4 * used * (t + 1)].astype(f32)
                halves.append(four[chunk * used : (chunk + 1) * used])
            row = jnp.concatenate(halves, axis=1)
            if used < PACK:
                row = jnp.concatenate([row, jnp.zeros((PACK - used, BZ), f32)], axis=0)
        ends = []
        for nz in (-1, 1):
            ref, at = edge_at[nx, ny, nz]
            ends.append(blocks[ref][at : at + PACK].astype(f32))
        at = ENDS_AT + 2 * (x * BY + y)
        to = line * BZ
        before = jnp.where(lane == 0, ends[0][:, at + 1 : at + 2], pltpu.roll(row, 1, 1))
        after = jnp.where(lane == BZ - 1, ends[1][:, at : at + 1], pltpu.roll(row, BZ - 1, 1))
        for i, piece in enumerate((before, row, after)):
            ahead[i * PACK : (i + 1) * PACK, to : to + BZ] = piece.astype(bf16)


def lines_inside():
    return {(px, py): px * BY + py - 1 for px in range(BX + 2) for py in range(1, BY + 1)}


def lines_ends():
    return {(px, py): 2 * px + (py > 0) for px in range(BX + 2) for py in (0, BY + 1)}


def emit(samples, kept, out):
    for s in range(samples):
        out[s, 0] = kept[s * C_ONE : (s + 1) * C_ONE]


def layer_one_inside(samples, face_at, edge_at, *refs):
    blocks, (own, ahead) = refs[:-2], refs[-2:]
    shift_input(samples, lines_inside(), face_at, {}, edge_at, blocks, own, ahead)


def layer_one(samples, scale, line_at, edge_at, *refs):
    blocks, (own, ahead, grad, chosen, before_sums, half, mine, other, ahead_ends, inside, ends) = refs[:-11], refs[-11:]
    shift_input(samples, lines_ends(), {}, line_at, edge_at, blocks, own, ahead_ends)
    rows = samples * C_ONE
    table = doubling()
    empty = jnp.zeros((rows, BZ), bf16)
    for x in range(BX):
        inside[x, 0:rows, (BY - 1) * BZ :] = empty
        inside[x, 2 * rows :, 0:BZ] = empty
        ends[x, 0:rows, BZ:] = empty
        ends[x, rows : 2 * rows, 0:BZ] = empty
        ends[x, rows : 2 * rows, BZ:] = empty
        ends[x, 2 * rows :, 0:BZ] = empty
    for x in range(HX):
        for y in range(HY):
            at = (x * HY + y) * LANES
            wide = jnp.dot(grad[:, at : at + LANES], table, preferred_element_type=f32).astype(bf16)
            for dx in range(2):
                for dy in range(2):
                    cx, cy = 2 * x + dx, 2 * y + dy
                    value = wide * chosen[:, (cx * BY + cy) * BZ : (cx * BY + cy + 1) * BZ]
                    for j, oy in enumerate(OFFS):
                        to = cy + oy
                        here = slice(j * rows, (j + 1) * rows)
                        if to < 0:
                            ends[cx, here, 0:BZ] = value
                        elif to >= BY:
                            ends[cx, here, BZ:] = value
                        else:
                            inside[cx, here, to * BZ : (to + 1) * BZ] = value
    width = 3 * 3 * PACK
    product = jnp.zeros((3 * rows, width), f32)
    for x in range(BX):
        for left, right, size in ((inside, ahead, BY * BZ), (ends, ahead_ends, 2 * BZ)):
            pieces = [right[:, (x + 1 + ox) * size : (x + 2 + ox) * size] for ox in OFFS]
            product = product + lax.dot_general(
                left[x], jnp.concatenate(pieces, axis=0), NT, preferred_element_type=f32
            )
    sample_of = (iota((C_ONE, width), 1) % PACK) // C_IN
    k = iota((width, LANES), 0)
    to = (k % C_IN) * STRIDE_ONE + (k // (3 * PACK)) * 9 + (k // PACK) % 3
    total = jnp.zeros((C_ONE, LANES), f32)
    for j in range(3):
        folded = jnp.zeros((C_ONE, width), f32)
        for s in range(samples):
            at = j * rows + s * C_ONE
            folded = folded + jnp.where(sample_of == s, product[at : at + C_ONE], 0.0)
        fold = (to + 3 * j == iota((width, LANES), 1)).astype(bf16)
        parts = []
        for _ in range(3):
            parts.append(folded.astype(bf16))
            folded = folded - parts[-1].astype(f32)
        got = jnp.dot(jnp.concatenate(parts, axis=0), fold, preferred_element_type=f32)
        total = total + (got[2 * C_ONE :] + got[C_ONE : 2 * C_ONE] + got[0:C_ONE])
    sums = jnp.concatenate([before_sums[...], total * scale], axis=1)
    top, bottom = sums[0:HALF], sums[HALF:]
    first = half[0] == 0
    mine[...] = jnp.where(first, top, bottom)
    other[...] = jnp.where(first, bottom, top)


def finish(half, mine, theirs, grad_one, grad_two):
    first = half[0] == 0
    top = jnp.where(first, mine[...], theirs[...])
    bottom = jnp.where(first, theirs[...], mine[...])
    for rows, part in ((slice(0, HALF), top), (slice(HALF, C_ONE), bottom)):
        for o in range(27):
            grad_two[o, rows] = part[:, o * C_TWO : (o + 1) * C_TWO]
        for c in range(C_IN):
            at = ONE_AT + c * STRIDE_ONE
            grad_one[c, rows] = part[:, at : at + 27]


def call(body, shapes, operands, far=0, scratch=(), flops=0, moved=0, scalars=()):
    if far:
        scratch = [pltpu.VMEM(a.shape, a.dtype) for a in operands[:far]]
        scratch.append(pltpu.SemaphoreType.DMA((far,)))
        away = [pltpu.with_memory_space_constraint(a, pltpu.HBM) for a in operands[:far]]
        operands = (*away, *operands[far:])
    spaces = [pltpu.HBM] * far + [pltpu.VMEM] * (len(operands) - far)
    for i in scalars:
        spaces[i] = pltpu.SMEM
    return pl.pallas_call(
        body,
        out_shape=shapes,
        in_specs=[pl.BlockSpec(memory_space=space) for space in spaces],
        out_specs=jax.tree.map(lambda _: pl.BlockSpec(memory_space=pltpu.VMEM), shapes),
        scratch_shapes=list(scratch),
        compiler_params=pltpu.CompilerParams(vmem_limit_bytes=32 * 2**20),
        cost_estimate=pl.CostEstimate(flops=flops, bytes_accessed=moved, transcendentals=0),
    )(*operands)


def block_side(blocks):
    return min(k for k in range(1, blocks + 1) if k * k * k >= blocks)


def from_block(array, side, *offset):
    pairs = []
    for i in range(lax.axis_size("space")):
        at = (i // (side * side), i // side % side, i % side)
        x, y, z = ((c + o) % side for c, o in zip(at, offset))
        pairs.append(((x * side + y) * side + z, i))
    return lax.ppermute(array, "space", pairs)


def both_sides(array, side, axis):
    below = from_block(array, side, *(-1 if a == axis else 0 for a in range(3)))
    if side == 2:
        return {-1: below, 1: below}
    return {-1: below, 1: from_block(array, side, *(1 if a == axis else 0 for a in range(3)))}


def swapped(array, bits):
    devices = lax.axis_size("dp") * lax.axis_size("space")
    return lax.ppermute(array, ("dp", "space"), [(i, i ^ bits) for i in range(devices)])


def stacked(parts):
    kept, starts, places = [], [], []
    rows = 0
    for part in parts:
        found = [i for i, a in enumerate(kept) if a is part]
        if not found:
            found = [len(kept)]
            kept.append(part)
            starts.append(rows)
            rows += part.shape[0]
        places.append(starts[found[0]])
    return jnp.concatenate(kept, axis=0), places


def operands_of(*tables):
    arrays, numbered = [], []
    for table in tables:
        new = {}
        for key, (array, row) in table.items():
            found = [i for i, a in enumerate(arrays) if a is array]
            if not found:
                found = [len(arrays)]
                arrays.append(array)
            new[key] = (found[0], row)
        numbered.append(new)
    return arrays, numbered


def local(inputs, mask_one, place_one, pooled_one, w_two, mask_two, place_two, grad_two):
    blocks = lax.axis_size("space")
    side = block_side(blocks)
    samples = inputs.shape[0]
    cells = inputs.shape[3]
    half_cells = HX * HY * HZ
    shape = jax.ShapeDtypeStruct
    vp_rows = 2 * samples * C_TWO
    four = 4 * samples * C_IN
    vp_row = BY * four
    to_x, own = call(
        functools.partial(prepare, samples),
        (shape((BY * four + vp_rows, LANES), bf16), shape((PACK, cells), bf16)),
        (grad_two, place_two, mask_two, inputs),
        far=4,
        flops=2 * 10**7,
        moved=2**20,
    )
    edge, to_y = call(
        functools.partial(ends, samples, vp_row),
        (shape((C_TWO, LANES), bf16), shape((4 * four + vp_rows, LANES), bf16)),
        (to_x, own),
        flops=10**7,
        moved=2**19,
    )
    chosen, folded_weights, expand = call(
        functools.partial(select_one, samples),
        (
            shape((samples * C_ONE, cells), bf16),
            shape((9 * C_ONE, 3 * C_TWO), bf16),
            shape((2 * LANES, TABLE), bf16),
        ),
        (place_one, mask_one, w_two),
        far=3,
        flops=2 * 10**7,
        moved=3 * 2**20,
    )
    vp_at, edge_at, face_at, line_at = {(0, 0): (to_x, vp_row)}, {}, {}, {}
    from_x = both_sides(to_x, side, 0)
    edge_z = both_sides(edge, side, 2)
    if side == 2:
        diagonal = from_block(edge, side, 1, 0, 1)
        edge_x = {nz: {nx: diagonal for nx in (-1, 1)} for nz in (-1, 1)}
    else:
        edge_x = {nz: {nx: from_block(edge, side, nx, 0, nz) for nx in (-1, 1)} for nz in (-1, 1)}
    first, first_starts = stacked([to_y, edge_z[-1], edge_z[1]])
    first = both_sides(first, side, 1)
    side_tiles, corner_tiles = len(tiles_sides()), len(tiles_corners())
    part_shape = shape((samples * C_ONE, half_cells), f32)
    total_shape = shape((9 * C_ONE, 3 * C_TWO), f32)
    arrays, tables = operands_of({(0, 0): vp_at[0, 0]}, {(0, 0, n): (edge_z[n], 0) for n in (-1, 1)})
    part, total_two = call(
        functools.partial(layer_two_own, samples, *tables),
        (
            part_shape,
            total_shape,
        ),
        (*arrays, pooled_one, folded_weights, expand),
        scratch=(
            pltpu.VMEM((samples, 3 * C_TWO, half_cells), bf16),
            pltpu.VMEM((samples, 9 * C_ONE, half_cells), bf16),
        ),
        flops=1000,
        moved=1000,
    )
    ready = {n: lax.optimization_barrier((from_x[n], total_two))[0] for n in ((-1,) if side == 2 else (-1, 1))}
    parts = []
    for n in (-1, 1):
        again = n == 1 and side == 2
        parts += parts[:2] if again else [ready[n][vp_row:], ready[n][: 2 * four]]
    second, starts = stacked(parts)
    second = both_sides(second, side, 1)
    third, edge_starts = stacked([edge_z[-1], edge_z[1]] + [edge_x[nz][nx] for nz in (-1, 1) for nx in (-1, 1)])
    third = both_sides(third, side, 1)
    for n in (-1, 1):
        vp_at[n, 0] = (from_x[n], vp_row)
        face_at[n] = (from_x[n], 0)
        vp_at[0, n] = (first[n], 4 * four)
        line_at[0, n] = (first[n], 0)
        edge_at[0, 0, n] = (edge_z[n], 0)
        for i, nx in enumerate((-1, 1)):
            edge_at[nx, 0, n] = (edge_x[n][nx], 0)
            vp_at[nx, n] = (second[n], starts[2 * i])
            line_at[nx, n] = (second[n], starts[2 * i + 1])
        for i, nz in enumerate((-1, 1)):
            edge_at[0, n, nz] = (first[n], first_starts[1 + i])
            for j, nx in enumerate((-1, 1)):
                edge_at[nx, n, nz] = (third[n], edge_starts[2 + 2 * i + j])
    total = lax.axis_size("dp") * samples * blocks * cells

    def near(table, y):
        return {key: value for key, value in table.items() if key[1] in y}

    arrays, tables = operands_of(
        {key: value for key, value in vp_at.items() if (key[0] == 0) != (key[1] == 0)},
        {key: value for key, value in edge_at.items() if (key[0] == 0) != (key[1] == 0)},
    )
    part, total_two = call(
        functools.partial(layer_two_sides, samples, *tables),
        (part_shape, total_shape),
        (*arrays, pooled_one, folded_weights, expand, part, total_two),
        scratch=(
            pltpu.VMEM((samples, 3 * C_TWO, side_tiles * LANES), bf16),
            pltpu.VMEM((samples, 9 * C_ONE, side_tiles * LANES), bf16),
        ),
        flops=1000,
        moved=1000,
    )
    arrays, tables = operands_of(face_at, near(edge_at, (0,)))
    ahead = call(
        functools.partial(layer_one_inside, samples, *tables),
        shape((3 * PACK, (BX + 2) * BY * BZ), bf16),
        (*arrays, own),
        flops=10**8,
        moved=2**20,
    )
    arrays, tables = operands_of(
        {key: value for key, value in vp_at.items() if key[0] != 0 and key[1] != 0},
        {key: value for key, value in edge_at.items() if key[0] != 0 and key[1] != 0},
    )
    kept, sums = call(
        functools.partial(layer_two_corners, samples, float(total // 8) ** -0.5, *tables),
        (
            shape((samples * C_ONE, half_cells), bf16),
            shape((C_ONE, ONE_AT), f32),
        ),
        (*arrays, pooled_one, folded_weights, expand, part, total_two),
        scratch=(
            pltpu.VMEM((samples, 3 * C_TWO, corner_tiles * LANES), bf16),
            pltpu.VMEM((samples, 9 * C_ONE, corner_tiles * LANES), bf16),
        ),
        flops=5 * 10**8,
        moved=2**20,
    )
    arrays, tables = operands_of(line_at, near(edge_at, (-1, 1)))
    half = (lax.axis_index("dp") % 2).astype(i32).reshape(1)
    operands = (*arrays, own, ahead, kept, chosen, sums, half)
    half_sums = shape((HALF, WIDTH), f32)
    mine, other = call(
        functools.partial(layer_one, samples, float(total) ** -0.5, *tables),
        (half_sums, half_sums),
        operands,
        scratch=(
            pltpu.VMEM((3 * PACK, (BX + 2) * 2 * BZ), bf16),
            pltpu.VMEM((BX, 3 * samples * C_ONE, BY * BZ), bf16),
            pltpu.VMEM((BX, 3 * samples * C_ONE, 2 * BZ), bf16),
        ),
        flops=5 * 10**8,
        moved=2**20,
        scalars=(len(operands) - 1,),
    )
    grad_pooled = call(
        functools.partial(emit, samples),
        shape((samples, 1, C_ONE, half_cells), bf16),
        (kept,),
        flops=10**6,
        moved=2**18,
    )
    mine = mine + swapped(other, blocks)
    devices = lax.axis_size("dp") * blocks
    bits = [1 << k for k in range(devices.bit_length() - 1) if 1 << k > blocks]
    bits += [1 << k for k in range(devices.bit_length() - 1) if 1 << k < blocks]
    while len(bits) > 1:
        (a, b), bits = bits[:2], bits[2:]
        mine = (mine + swapped(mine, a ^ b)) + (swapped(mine, a) + swapped(mine, b))
    for a in bits:
        mine = mine + swapped(mine, a)
    grad_w_one, grad_w_two = call(
        finish,
        (shape((C_IN, C_ONE, 27), f32), shape((27, C_ONE, C_TWO), f32)),
        (half, mine, swapped(mine, blocks)),
        scalars=(0,),
    )
    return grad_pooled, jnp.transpose(grad_w_one, (2, 0, 1)), grad_w_two


def solution(mesh):
    split = P("dp", "space", None, None)
    return jax.shard_map(
        local,
        mesh=mesh,
        in_specs=(split, split, split, split, P(), split, split, split),
        out_specs=(split, P(), P()),
        check_vma=False,
    )
```

```python
import functools

import jax
import jax.numpy as jnp
from jax import lax
from jax.experimental import pallas as pl
from jax.experimental.pallas import tpu as pltpu
from jax.sharding import PartitionSpec as P

C_IN = 4
C_ONE = 16
C_TWO = 32
BX = 4
BY = 8
BZ = 256
HX, HY, HZ = BX // 2, BY // 2, BZ // 2
QY, QZ = HY // 2, HZ // 2
LANES = 128
PACK = 16
ENDS_AT = LANES - 2 * BX * BY
OFFS = (-1, 0, 1)
GRAD_W_TWO = 27 * C_TWO
WIDTH = 1024
ONE_AT = WIDTH - LANES
STRIDE_ONE = LANES // C_IN
HALF = C_ONE // 2
TABLE = 3 * QY * LANES
NT = (((1,), (1,)), ((), ()))
f32, bf16, i32 = jnp.float32, jnp.bfloat16, jnp.int32


def iota(shape, dim):
    return lax.broadcasted_iota(i32, shape, dim)


def doubling():
    return (iota((LANES, 2 * LANES), 0) == iota((LANES, 2 * LANES), 1) // 2).astype(bf16)


def fetch(pairs, sems):
    copies = [pltpu.make_async_copy(a, b, sems.at[i]) for i, (a, b) in enumerate(pairs)]
    for copy in copies:
        copy.start()
    return copies


def prepare(samples, *refs):
    far, (to_x, own), near, sems = refs[:4], refs[4:6], refs[6:10], refs[10]
    grad, place, mask, source = near
    copies = fetch(tuple(zip(far, near)), sems)
    rows = samples * C_TWO
    table = doubling()
    copies[0].wait()
    copies[1].wait()
    values = jnp.dot(grad[...].reshape(rows, LANES), table, preferred_element_type=f32)
    spots = place[...].reshape(rows, LANES).astype(f32).astype(bf16)
    wide = jnp.dot(spots, table, preferred_element_type=f32)
    parity = (iota((rows, LANES), 1) % 2).astype(f32)
    copies[2].wait()
    halves = []
    for qy in range(QY):
        v = values[:, qy * LANES : (qy + 1) * LANES]
        p = wide[:, qy * LANES : (qy + 1) * LANES] - parity
        total = jnp.zeros((rows, LANES), f32)
        for x in range(HX):
            for dy in range(2):
                at = (x * HY + 2 * qy + dy) * LANES
                on = mask[:, 0, :, at : at + LANES].reshape(rows, LANES) == 1
                total = total + jnp.where(on & (p == 4.0 * x + 2.0 * dy), v, 0.0)
        halves.append(total)
    kept = jnp.concatenate(halves, axis=1).astype(bf16)
    v = lax.dot_general(kept, table, NT, preferred_element_type=f32).astype(bf16)
    used = samples * C_IN
    at = BY * 4 * used
    to_x[at : at + rows] = v
    to_x[at + rows : at + 2 * rows] = spots
    copies[3].wait()
    pieces = [source[s, 0].astype(f32) for s in range(samples)]
    if used < PACK:
        pieces.append(jnp.zeros((PACK - used, BX * BY * BZ), f32))
    cells = jnp.concatenate(pieces, axis=0)
    own[...] = cells.astype(bf16)
    for t in range(BY):
        group = []
        for x in (0, BX - 1):
            for y in (t // 2, BY - 1 - t // 2):
                at = (x * BY + y) * BZ + (t % 2) * LANES
                group.append(cells[0:used, at : at + LANES])
        to_x[4 * used * t : 4 * used * (t + 1)] = jnp.concatenate(group, axis=0).astype(bf16)


def ends(samples, vp_row, to_x, own, edge, to_y):
    rows = samples * C_TWO
    lane = iota((LANES, LANES), 0)
    spot = (lane // QZ) * 2 + (lane % QZ == QZ - 1).astype(i32)
    spot = jnp.where((lane % QZ == 0) | (lane % QZ == QZ - 1), spot, -LANES)
    column = iota((LANES, LANES), 1)
    packed = jnp.zeros((C_TWO, LANES), f32)
    for s in range(samples):
        for t in range(2):
            pick = (spot + (8 * s + 4 * t) == column).astype(bf16)
            at = vp_row + t * rows + s * C_TWO
            packed = packed + jnp.dot(to_x[at : at + C_TWO], pick, preferred_element_type=f32)
    lane = iota((PACK, LANES), 1)
    cells = packed[0:PACK]
    for row in range(BX * BY):
        left = own[:, row * BZ : row * BZ + LANES].astype(f32)
        right = own[:, (row + 1) * BZ - LANES : (row + 1) * BZ].astype(f32)
        cells = jnp.where(lane == ENDS_AT + 2 * row, left[:, 0:1], cells)
        cells = jnp.where(lane == ENDS_AT + 2 * row + 1, right[:, LANES - 1 :], cells)
    edge[0:PACK] = cells.astype(bf16)
    edge[PACK:] = packed[PACK:].astype(bf16)
    used = samples * C_IN
    to_y[4 * 4 * used :] = to_x[vp_row:]
    for t in range(4):
        group = []
        for x in range(BX):
            at = (x * BY + (BY - 1) * (t // 2)) * BZ + (t % 2) * LANES
            group.append(own[:, at : at + LANES].astype(f32)[0:used])
        to_y[4 * used * t : 4 * used * (t + 1)] = jnp.concatenate(group, axis=0).astype(bf16)


def select_one(samples, *refs):
    far, (chosen, folded_weights, expand), near, sems = refs[:3], refs[3:6], refs[6:9], refs[9]
    place, mask, weights = near
    copies = fetch(tuple(zip(far, near)), sems)
    k = iota((2 * LANES, TABLE), 0)
    j = iota((1, TABLE), 1)
    shift = j // (QY * LANES) - 1
    qy = (j // LANES) % QY
    z = j % LANES - shift
    beyond = LANES + qy * 2 + (z < 0).astype(i32)
    expand[...] = (k == jnp.where((z >= 0) & (z < LANES), qy * QZ + z // 2, beyond)).astype(bf16)
    rows = samples * C_ONE
    table = doubling()
    parity = (iota((rows, BZ), 1) % 2).astype(f32)
    copies[2].wait()
    folded_weights[...] = jnp.concatenate(
        [jnp.concatenate([weights[3 * o + i] for i in range(3)], axis=1) for o in range(9)], axis=0
    )
    copies[0].wait()
    copies[1].wait()
    for x in range(HX):
        for y in range(HY):
            at = (x * HY + y) * LANES
            spots = place[:, 0, :, at : at + LANES].reshape(rows, LANES).astype(f32).astype(bf16)
            wide = jnp.dot(spots, table, preferred_element_type=f32) - parity
            for dx in range(2):
                for dy in range(2):
                    to = ((2 * x + dx) * BY + 2 * y + dy) * BZ
                    on = mask[:, 0, :, to : to + BZ].reshape(rows, BZ) == 1
                    hit = on & (wide == 4.0 * dx + 2.0 * dy)
                    chosen[:, to : to + BZ] = jnp.where(hit, 1.0, 0.0).astype(bf16)


def expand_windows(samples, vp_at, edge_at, tile_of, blocks, expand, fields):
    rows = samples * C_TWO
    lane = iota((rows, LANES), 1)
    odd = iota((C_TWO, LANES), 1) % 2 == 1
    groups = {}
    for nx, ny in vp_at:
        key = (vp_at[nx, ny], edge_at[nx, ny, -1], edge_at[nx, ny, 1])
        groups.setdefault(key, []).append((nx, ny))
    for ((ref, at), low, high), places in groups.items():
        edge = blocks[low[0]][low[1] : low[1] + C_TWO].astype(f32)
        if low != high:
            other = blocks[high[0]][high[1] : high[1] + C_TWO].astype(f32)
            edge = jnp.where(odd, edge, other)
        parts = []
        for t in range(2):
            for s in range(samples):
                by = 8 * s + 4 * t
                parts.append(pltpu.roll(edge, LANES - by, 1) if by else edge)
        both = jnp.concatenate(
            [blocks[ref][at : at + 2 * rows], jnp.concatenate(parts, axis=0).astype(bf16)], axis=1
        )
        wide = jnp.dot(both, expand[...], preferred_element_type=f32)
        for i, oz in enumerate(OFFS):
            parity = ((lane - oz) & 1).astype(f32)
            for qy in range(QY):
                lanes = slice((i * QY + qy) * LANES, (i * QY + qy + 1) * LANES)
                v = wide[0:rows, lanes].astype(bf16)
                p = (wide[rows : 2 * rows, lanes] - parity).astype(bf16)
                for x in range(HX):
                    for dy in range(2):
                        y = 2 * qy + dy
                        spots = []
                        for nx, ny in places:
                            near_x = nx == 0 or x == (HX - 1 if nx < 0 else 0)
                            near_y = ny == 0 or y == (HY - 1 if ny < 0 else 0)
                            if near_x and near_y:
                                spots.append(tile_of[x + 1 + nx * HX, y + 1 + ny * HY])
                        if not spots:
                            continue
                        cells = jnp.where(p == 4.0 * x + 2.0 * dy, v, jnp.zeros_like(v))
                        for spot in spots:
                            for s in range(samples):
                                fields[s, i * C_TWO : (i + 1) * C_TWO, spot * LANES : (spot + 1) * LANES] = (
                                    cells[s * C_TWO : (s + 1) * C_TWO]
                                )


def tiles_own():
    return {(px, py): (px - 1) * HY + py - 1 for px in range(1, HX + 1) for py in range(1, HY + 1)}


def tiles_sides():
    tiles = [(px, py) for px in (0, HX + 1) for py in range(1, HY + 1)]
    tiles += [(px, py) for px in range(1, HX + 1) for py in (0, HY + 1)]
    return {key: i for i, key in enumerate(tiles)}


def tiles_corners():
    return {(px, py): 2 * (px > 0) + (py > 0) for px in (0, HX + 1) for py in (0, HY + 1)}


def shift_pooled(samples, tile_of, pooled, moved):
    for (px, py), tile in tile_of.items():
        k = 0
        for ox in OFFS:
            for oy in OFFS:
                x, y = px - 1 + ox, py - 1 + oy
                inside = 0 <= x < HX and 0 <= y < HY
                for s in range(samples):
                    if inside:
                        at = (x * HY + y) * LANES
                        value = pooled[s, 0, :, at : at + LANES]
                    else:
                        value = jnp.zeros((C_ONE, LANES), bf16)
                    moved[s, k * C_ONE : (k + 1) * C_ONE, tile * LANES : (tile + 1) * LANES] = value
                k += 1


def products_two(samples, tile_of, fields, moved, weights, sums, totals):
    for s in range(samples):
        wide = jnp.dot(weights[...], fields[s], preferred_element_type=f32)
        for x in range(HX):
            for y in range(HY):
                k = 0
                for ox in OFFS:
                    for oy in OFFS:
                        tile = tile_of.get((x + 1 - ox, y + 1 - oy))
                        if tile is not None:
                            part = wide[k * C_ONE : (k + 1) * C_ONE, tile * LANES : (tile + 1) * LANES]
                            old = sums[s].get((x, y))
                            sums[s][x, y] = part if old is None else old + part
                        k += 1
        totals = totals + lax.dot_general(moved[s], fields[s], NT, preferred_element_type=f32)
    return totals


def parts_of(samples, part):
    return [
        {
            (x, y): part[s * C_ONE : (s + 1) * C_ONE, (x * HY + y) * LANES : (x * HY + y + 1) * LANES]
            for x in range(HX)
            for y in range(HY)
        }
        for s in range(samples)
    ]


def store_parts(sums, part):
    for s, tiles in enumerate(sums):
        for (x, y), value in tiles.items():
            at = (x * HY + y) * LANES
            part[s * C_ONE : (s + 1) * C_ONE, at : at + LANES] = value.astype(part.dtype)


def layer_two_own(samples, vp_at, edge_at, *refs):
    blocks, (pooled, weights, expand, part, total, fields, moved) = refs[:-7], refs[-7:]
    tile_of = tiles_own()
    expand_windows(samples, vp_at, edge_at, tile_of, blocks, expand, fields)
    shift_pooled(samples, tile_of, pooled, moved)
    sums = [{} for _ in range(samples)]
    totals = jnp.zeros((9 * C_ONE, 3 * C_TWO), f32)
    total[...] = products_two(samples, tile_of, fields, moved, weights, sums, totals)
    store_parts(sums, part)


def layer_two_sides(samples, vp_at, edge_at, *refs):
    blocks, (pooled, weights, expand, old, old_total, part, total, fields, moved) = refs[:-9], refs[-9:]
    tile_of = tiles_sides()
    expand_windows(samples, vp_at, edge_at, tile_of, blocks, expand, fields)
    shift_pooled(samples, tile_of, pooled, moved)
    sums = parts_of(samples, old)
    total[...] = products_two(samples, tile_of, fields, moved, weights, sums, old_total[...])
    store_parts(sums, part)


def layer_two_corners(samples, scale, vp_at, edge_at, *refs):
    blocks, (pooled, weights, expand, part, total, kept, message, fields, moved) = refs[:-9], refs[-9:]
    tile_of = tiles_corners()
    expand_windows(samples, vp_at, edge_at, tile_of, blocks, expand, fields)
    shift_pooled(samples, tile_of, pooled, moved)
    sums = parts_of(samples, part)
    totals = products_two(samples, tile_of, fields, moved, weights, sums, total[...]) * scale
    store_parts(sums, kept)
    width = 3 * C_TWO
    for k in range(9):
        message[:, k * width : (k + 1) * width] = totals[k * C_ONE : (k + 1) * C_ONE]
    message[:, GRAD_W_TWO:ONE_AT] = jnp.zeros((C_ONE, ONE_AT - GRAD_W_TWO), f32)


def shift_input(samples, rows_of, face_at, line_at, edge_at, blocks, own, ahead):
    used = samples * C_IN
    lane = iota((PACK, BZ), 1)
    for (px, py), line in rows_of.items():
        nx = -1 if px == 0 else 1 if px == BX + 1 else 0
        ny = -1 if py == 0 else 1 if py == BY + 1 else 0
        x, y = (px - 1) % BX, (py - 1) % BY
        if nx == 0 and ny == 0:
            row = own[:, (x * BY + y) * BZ : (x * BY + y + 1) * BZ].astype(f32)
        else:
            if nx != 0:
                ref, at = face_at[nx] if ny == 0 else line_at[nx, ny]
                tile = 2 * min(y, BY - 1 - y)
                chunk = 2 * (0 if x == 0 else 1) + (1 if y >= BY // 2 else 0)
            else:
                ref, at = line_at[nx, ny]
                tile = 2 * (0 if y == 0 else 1)
                chunk = x
            halves = []
            for t in (tile, tile + 1):
                four = blocks[ref][at + 4 * used * t : at + 4 * used * (t + 1)].astype(f32)
                halves.append(four[chunk * used : (chunk + 1) * used])
            row = jnp.concatenate(halves, axis=1)
            if used < PACK:
                row = jnp.concatenate([row, jnp.zeros((PACK - used, BZ), f32)], axis=0)
        ends = []
        for nz in (-1, 1):
            ref, at = edge_at[nx, ny, nz]
            ends.append(blocks[ref][at : at + PACK].astype(f32))
        at = ENDS_AT + 2 * (x * BY + y)
        to = line * BZ
        before = jnp.where(lane == 0, ends[0][:, at + 1 : at + 2], pltpu.roll(row, 1, 1))
        after = jnp.where(lane == BZ - 1, ends[1][:, at : at + 1], pltpu.roll(row, BZ - 1, 1))
        for i, piece in enumerate((before, row, after)):
            ahead[i * PACK : (i + 1) * PACK, to : to + BZ] = piece.astype(bf16)


def lines_inside():
    return {(px, py): px * BY + py - 1 for px in range(BX + 2) for py in range(1, BY + 1)}


def lines_ends():
    return {(px, py): 2 * px + (py > 0) for px in range(BX + 2) for py in (0, BY + 1)}


def emit(samples, kept, out):
    for s in range(samples):
        out[s, 0] = kept[s * C_ONE : (s + 1) * C_ONE]


def middle_lines():
    return range(3, BY - 3)


def layer_one_inside(samples, face_at, edge_at, *refs):
    blocks, (own, part, chosen, ahead, product, middle) = refs[:-6], refs[-6:]
    shift_input(samples, lines_inside(), face_at, {}, edge_at, blocks, own, ahead)
    rows = samples * C_ONE
    table = doubling()
    lines = middle_lines()
    for x in range(HX):
        for y in range(1, HY - 1):
            at = (x * HY + y) * LANES
            cells = part[:, at : at + LANES].astype(bf16)
            wide = jnp.dot(cells, table, preferred_element_type=f32).astype(bf16)
            for dx in range(2):
                for dy in range(2):
                    cx, cy = 2 * x + dx, 2 * y + dy
                    value = wide * chosen[:, (cx * BY + cy) * BZ : (cx * BY + cy + 1) * BZ]
                    for j, oy in enumerate(OFFS):
                        if cy + oy in lines:
                            to = (cy + oy - lines.start) * BZ
                            middle[cx, j * rows : (j + 1) * rows, to : to + BZ] = value
    plane = BY * BZ
    total = jnp.zeros((3 * rows, 9 * PACK), f32)
    for x in range(BX):
        pieces = []
        for ox in OFFS:
            at = (x + 1 + ox) * plane
            pieces.append(ahead[:, at + lines.start * BZ : at + lines.stop * BZ])
        total = total + lax.dot_general(
            middle[x], jnp.concatenate(pieces, axis=0), NT, preferred_element_type=f32
        )
    product[...] = total


def layer_one(samples, scale, line_at, edge_at, *refs):
    blocks, (own, ahead, begun, grad, chosen, before_sums, half, mine, other, ahead_ends, inside, ends) = (
        refs[:-12], refs[-12:],
    )
    shift_input(samples, lines_ends(), {}, line_at, edge_at, blocks, own, ahead_ends)
    lines = middle_lines()
    rows = samples * C_ONE
    table = doubling()
    empty = jnp.zeros((rows, BZ), bf16)
    for x in range(BX):
        inside[x, 0:rows, (BY - 1) * BZ :] = empty
        inside[x, 2 * rows :, 0:BZ] = empty
        ends[x, 0:rows, BZ:] = empty
        ends[x, rows : 2 * rows, 0:BZ] = empty
        ends[x, rows : 2 * rows, BZ:] = empty
        ends[x, 2 * rows :, 0:BZ] = empty
    for x in range(HX):
        for y in range(HY):
            at = (x * HY + y) * LANES
            wide = jnp.dot(grad[:, at : at + LANES], table, preferred_element_type=f32).astype(bf16)
            for dx in range(2):
                for dy in range(2):
                    cx, cy = 2 * x + dx, 2 * y + dy
                    value = wide * chosen[:, (cx * BY + cy) * BZ : (cx * BY + cy + 1) * BZ]
                    for j, oy in enumerate(OFFS):
                        to = cy + oy
                        here = slice(j * rows, (j + 1) * rows)
                        if to < 0:
                            ends[cx, here, 0:BZ] = value
                        elif to >= BY:
                            ends[cx, here, BZ:] = value
                        elif to not in lines:
                            inside[cx, here, to * BZ : (to + 1) * BZ] = value
    width = 3 * 3 * PACK
    product = begun[...]
    plane = BY * BZ
    for x in range(BX):
        for left, right, size, first, last in (
            (inside, ahead, plane, 0, lines.start * BZ),
            (inside, ahead, plane, lines.stop * BZ, plane),
            (ends, ahead_ends, 2 * BZ, 0, 2 * BZ),
        ):
            pieces = [right[:, (x + 1 + ox) * size + first : (x + 1 + ox) * size + last] for ox in OFFS]
            product = product + lax.dot_general(
                left[x, :, first:last], jnp.concatenate(pieces, axis=0), NT, preferred_element_type=f32
            )
    sample_of = (iota((C_ONE, width), 1) % PACK) // C_IN
    k = iota((width, LANES), 0)
    to = (k % C_IN) * STRIDE_ONE + (k // (3 * PACK)) * 9 + (k // PACK) % 3
    total = jnp.zeros((C_ONE, LANES), f32)
    for j in range(3):
        folded = jnp.zeros((C_ONE, width), f32)
        for s in range(samples):
            at = j * rows + s * C_ONE
            folded = folded + jnp.where(sample_of == s, product[at : at + C_ONE], 0.0)
        fold = (to + 3 * j == iota((width, LANES), 1)).astype(bf16)
        parts = []
        for _ in range(3):
            parts.append(folded.astype(bf16))
            folded = folded - parts[-1].astype(f32)
        got = jnp.dot(jnp.concatenate(parts, axis=0), fold, preferred_element_type=f32)
        total = total + (got[2 * C_ONE :] + got[C_ONE : 2 * C_ONE] + got[0:C_ONE])
    sums = jnp.concatenate([before_sums[...], total * scale], axis=1)
    top, bottom = sums[0:HALF], sums[HALF:]
    first = half[0] == 0
    mine[...] = jnp.where(first, top, bottom)
    other[...] = jnp.where(first, bottom, top)


def finish(half, mine, theirs, grad_one, grad_two):
    first = half[0] == 0
    top = jnp.where(first, mine[...], theirs[...])
    bottom = jnp.where(first, theirs[...], mine[...])
    for rows, part in ((slice(0, HALF), top), (slice(HALF, C_ONE), bottom)):
        for o in range(27):
            grad_two[o, rows] = part[:, o * C_TWO : (o + 1) * C_TWO]
        for c in range(C_IN):
            at = ONE_AT + c * STRIDE_ONE
            grad_one[c, rows] = part[:, at : at + 27]


def call(body, shapes, operands, far=0, scratch=(), flops=0, moved=0, scalars=()):
    if far:
        scratch = [pltpu.VMEM(a.shape, a.dtype) for a in operands[:far]]
        scratch.append(pltpu.SemaphoreType.DMA((far,)))
        away = [pltpu.with_memory_space_constraint(a, pltpu.HBM) for a in operands[:far]]
        operands = (*away, *operands[far:])
    spaces = [pltpu.HBM] * far + [pltpu.VMEM] * (len(operands) - far)
    for i in scalars:
        spaces[i] = pltpu.SMEM
    return pl.pallas_call(
        body,
        out_shape=shapes,
        in_specs=[pl.BlockSpec(memory_space=space) for space in spaces],
        out_specs=jax.tree.map(lambda _: pl.BlockSpec(memory_space=pltpu.VMEM), shapes),
        scratch_shapes=list(scratch),
        compiler_params=pltpu.CompilerParams(vmem_limit_bytes=32 * 2**20),
        cost_estimate=pl.CostEstimate(flops=flops, bytes_accessed=moved, transcendentals=0),
    )(*operands)


def block_side(blocks):
    return min(k for k in range(1, blocks + 1) if k * k * k >= blocks)


def from_block(array, side, *offset):
    pairs = []
    for i in range(lax.axis_size("space")):
        at = (i // (side * side), i // side % side, i % side)
        x, y, z = ((c + o) % side for c, o in zip(at, offset))
        pairs.append(((x * side + y) * side + z, i))
    return lax.ppermute(array, "space", pairs)


def both_sides(array, side, axis):
    below = from_block(array, side, *(-1 if a == axis else 0 for a in range(3)))
    if side == 2:
        return {-1: below, 1: below}
    return {-1: below, 1: from_block(array, side, *(1 if a == axis else 0 for a in range(3)))}


def swapped(array, bits):
    devices = lax.axis_size("dp") * lax.axis_size("space")
    return lax.ppermute(array, ("dp", "space"), [(i, i ^ bits) for i in range(devices)])


def stacked(parts):
    kept, starts, places = [], [], []
    rows = 0
    for part in parts:
        found = [i for i, a in enumerate(kept) if a is part]
        if not found:
            found = [len(kept)]
            kept.append(part)
            starts.append(rows)
            rows += part.shape[0]
        places.append(starts[found[0]])
    return jnp.concatenate(kept, axis=0), places


def operands_of(*tables):
    arrays, numbered = [], []
    for table in tables:
        new = {}
        for key, (array, row) in table.items():
            found = [i for i, a in enumerate(arrays) if a is array]
            if not found:
                found = [len(arrays)]
                arrays.append(array)
            new[key] = (found[0], row)
        numbered.append(new)
    return arrays, numbered


def local(inputs, mask_one, place_one, pooled_one, w_two, mask_two, place_two, grad_two):
    blocks = lax.axis_size("space")
    side = block_side(blocks)
    samples = inputs.shape[0]
    cells = inputs.shape[3]
    half_cells = HX * HY * HZ
    shape = jax.ShapeDtypeStruct
    vp_rows = 2 * samples * C_TWO
    four = 4 * samples * C_IN
    vp_row = BY * four
    to_x, own = call(
        functools.partial(prepare, samples),
        (shape((BY * four + vp_rows, LANES), bf16), shape((PACK, cells), bf16)),
        (grad_two, place_two, mask_two, inputs),
        far=4,
        flops=2 * 10**7,
        moved=2**20,
    )
    edge, to_y = call(
        functools.partial(ends, samples, vp_row),
        (shape((C_TWO, LANES), bf16), shape((4 * four + vp_rows, LANES), bf16)),
        (to_x, own),
        flops=10**7,
        moved=2**19,
    )
    chosen, folded_weights, expand = call(
        functools.partial(select_one, samples),
        (
            shape((samples * C_ONE, cells), bf16),
            shape((9 * C_ONE, 3 * C_TWO), bf16),
            shape((2 * LANES, TABLE), bf16),
        ),
        (place_one, mask_one, w_two),
        far=3,
        flops=2 * 10**7,
        moved=3 * 2**20,
    )
    vp_at, edge_at, face_at, line_at = {(0, 0): (to_x, vp_row)}, {}, {}, {}
    from_x = both_sides(to_x, side, 0)
    edge_z = both_sides(edge, side, 2)
    if side == 2:
        diagonal = from_block(edge, side, 1, 0, 1)
        edge_x = {nz: {nx: diagonal for nx in (-1, 1)} for nz in (-1, 1)}
    else:
        edge_x = {nz: {nx: from_block(edge, side, nx, 0, nz) for nx in (-1, 1)} for nz in (-1, 1)}
    first, first_starts = stacked([to_y, edge_z[-1], edge_z[1]])
    first = both_sides(first, side, 1)
    side_tiles, corner_tiles = len(tiles_sides()), len(tiles_corners())
    part_shape = shape((samples * C_ONE, half_cells), f32)
    total_shape = shape((9 * C_ONE, 3 * C_TWO), f32)
    arrays, tables = operands_of({(0, 0): vp_at[0, 0]}, {(0, 0, n): (edge_z[n], 0) for n in (-1, 1)})
    part, total_two = call(
        functools.partial(layer_two_own, samples, *tables),
        (
            part_shape,
            total_shape,
        ),
        (*arrays, pooled_one, folded_weights, expand),
        scratch=(
            pltpu.VMEM((samples, 3 * C_TWO, half_cells), bf16),
            pltpu.VMEM((samples, 9 * C_ONE, half_cells), bf16),
        ),
        flops=1000,
        moved=1000,
    )
    ready = {n: lax.optimization_barrier((from_x[n], total_two))[0] for n in ((-1,) if side == 2 else (-1, 1))}
    parts = []
    for n in (-1, 1):
        again = n == 1 and side == 2
        parts += parts[:2] if again else [ready[n][vp_row:], ready[n][: 2 * four]]
    second, starts = stacked(parts)
    second = both_sides(second, side, 1)
    third, edge_starts = stacked([edge_z[-1], edge_z[1]] + [edge_x[nz][nx] for nz in (-1, 1) for nx in (-1, 1)])
    third = both_sides(third, side, 1)
    for n in (-1, 1):
        vp_at[n, 0] = (from_x[n], vp_row)
        face_at[n] = (from_x[n], 0)
        vp_at[0, n] = (first[n], 4 * four)
        line_at[0, n] = (first[n], 0)
        edge_at[0, 0, n] = (edge_z[n], 0)
        for i, nx in enumerate((-1, 1)):
            edge_at[nx, 0, n] = (edge_x[n][nx], 0)
            vp_at[nx, n] = (second[n], starts[2 * i])
            line_at[nx, n] = (second[n], starts[2 * i + 1])
        for i, nz in enumerate((-1, 1)):
            edge_at[0, n, nz] = (first[n], first_starts[1 + i])
            for j, nx in enumerate((-1, 1)):
                edge_at[nx, n, nz] = (third[n], edge_starts[2 + 2 * i + j])
    total = lax.axis_size("dp") * samples * blocks * cells

    def near(table, y):
        return {key: value for key, value in table.items() if key[1] in y}

    arrays, tables = operands_of(
        {key: value for key, value in vp_at.items() if (key[0] == 0) != (key[1] == 0)},
        {key: value for key, value in edge_at.items() if (key[0] == 0) != (key[1] == 0)},
    )
    part, total_two = call(
        functools.partial(layer_two_sides, samples, *tables),
        (part_shape, total_shape),
        (*arrays, pooled_one, folded_weights, expand, part, total_two),
        scratch=(
            pltpu.VMEM((samples, 3 * C_TWO, side_tiles * LANES), bf16),
            pltpu.VMEM((samples, 9 * C_ONE, side_tiles * LANES), bf16),
        ),
        flops=1000,
        moved=1000,
    )
    arrays, tables = operands_of(face_at, near(edge_at, (0,)))
    ahead, begun = call(
        functools.partial(layer_one_inside, samples, *tables),
        (
            shape((3 * PACK, (BX + 2) * BY * BZ), bf16),
            shape((3 * samples * C_ONE, 9 * PACK), f32),
        ),
        (*arrays, own, part, chosen),
        scratch=(pltpu.VMEM((BX, 3 * samples * C_ONE, len(middle_lines()) * BZ), bf16),),
        flops=10**8,
        moved=2**20,
    )
    arrays, tables = operands_of(
        {key: value for key, value in vp_at.items() if key[0] != 0 and key[1] != 0},
        {key: value for key, value in edge_at.items() if key[0] != 0 and key[1] != 0},
    )
    kept, sums = call(
        functools.partial(layer_two_corners, samples, float(total // 8) ** -0.5, *tables),
        (
            shape((samples * C_ONE, half_cells), bf16),
            shape((C_ONE, ONE_AT), f32),
        ),
        (*arrays, pooled_one, folded_weights, expand, part, total_two),
        scratch=(
            pltpu.VMEM((samples, 3 * C_TWO, corner_tiles * LANES), bf16),
            pltpu.VMEM((samples, 9 * C_ONE, corner_tiles * LANES), bf16),
        ),
        flops=5 * 10**8,
        moved=2**20,
    )
    arrays, tables = operands_of(line_at, near(edge_at, (-1, 1)))
    half = (lax.axis_index("dp") % 2).astype(i32).reshape(1)
    operands = (*arrays, own, ahead, begun, kept, chosen, sums, half)
    half_sums = shape((HALF, WIDTH), f32)
    mine, other = call(
        functools.partial(layer_one, samples, float(total) ** -0.5, *tables),
        (half_sums, half_sums),
        operands,
        scratch=(
            pltpu.VMEM((3 * PACK, (BX + 2) * 2 * BZ), bf16),
            pltpu.VMEM((BX, 3 * samples * C_ONE, BY * BZ), bf16),
            pltpu.VMEM((BX, 3 * samples * C_ONE, 2 * BZ), bf16),
        ),
        flops=5 * 10**8,
        moved=2**20,
        scalars=(len(operands) - 1,),
    )
    grad_pooled = call(
        functools.partial(emit, samples),
        shape((samples, 1, C_ONE, half_cells), bf16),
        (kept,),
        flops=10**6,
        moved=2**18,
    )
    mine = mine + swapped(other, blocks)
    devices = lax.axis_size("dp") * blocks
    bits = [1 << k for k in range(devices.bit_length() - 1) if 1 << k > blocks]
    bits += [1 << k for k in range(devices.bit_length() - 1) if 1 << k < blocks]
    while len(bits) > 1:
        (a, b), bits = bits[:2], bits[2:]
        mine = (mine + swapped(mine, a)) + (swapped(mine, b) + swapped(mine, a ^ b))
    for a in bits:
        mine = mine + swapped(mine, a)
    grad_w_one, grad_w_two = call(
        finish,
        (shape((C_IN, C_ONE, 27), f32), shape((27, C_ONE, C_TWO), f32)),
        (half, mine, swapped(mine, blocks)),
        scalars=(0,),
    )
    return grad_pooled, jnp.transpose(grad_w_one, (2, 0, 1)), grad_w_two


def solution(mesh):
    split = P("dp", "space", None, None)
    return jax.shard_map(
        local,
        mesh=mesh,
        in_specs=(split, split, split, split, P(), split, split, split),
        out_specs=(split, P(), P()),
        check_vma=False,
    )
```

```python
import functools

import jax
import jax.numpy as jnp
from jax import lax
from jax.experimental import pallas as pl
from jax.experimental.pallas import tpu as pltpu
from jax.sharding import PartitionSpec as P

C_IN = 4
C_ONE = 16
C_TWO = 32
BX = 4
BY = 8
BZ = 256
HX, HY, HZ = BX // 2, BY // 2, BZ // 2
QY, QZ = HY // 2, HZ // 2
LANES = 128
PACK = 16
ENDS_AT = LANES - 2 * BX * BY
OFFS = (-1, 0, 1)
GRAD_W_TWO = 27 * C_TWO
WIDTH = 1024
ONE_AT = WIDTH - LANES
STRIDE_ONE = LANES // C_IN
HALF = C_ONE // 2
TABLE = 3 * QY * LANES
NT = (((1,), (1,)), ((), ()))
f32, bf16, i32 = jnp.float32, jnp.bfloat16, jnp.int32


def iota(shape, dim):
    return lax.broadcasted_iota(i32, shape, dim)


def doubling():
    return (iota((LANES, 2 * LANES), 0) == iota((LANES, 2 * LANES), 1) // 2).astype(bf16)


def fetch(pairs, sems):
    copies = [pltpu.make_async_copy(a, b, sems.at[i]) for i, (a, b) in enumerate(pairs)]
    for copy in copies:
        copy.start()
    return copies


def prepare(samples, *refs):
    far, (to_x, own), near, sems = refs[:4], refs[4:6], refs[6:10], refs[10]
    grad, place, mask, source = near
    copies = fetch(tuple(zip(far, near)), sems)
    rows = samples * C_TWO
    table = doubling()
    copies[0].wait()
    copies[1].wait()
    values = jnp.dot(grad[...].reshape(rows, LANES), table, preferred_element_type=f32)
    spots = place[...].reshape(rows, LANES).astype(f32).astype(bf16)
    wide = jnp.dot(spots, table, preferred_element_type=f32)
    parity = (iota((rows, LANES), 1) % 2).astype(f32)
    copies[2].wait()
    halves = []
    for qy in range(QY):
        v = values[:, qy * LANES : (qy + 1) * LANES]
        p = wide[:, qy * LANES : (qy + 1) * LANES] - parity
        total = jnp.zeros((rows, LANES), f32)
        for x in range(HX):
            for dy in range(2):
                at = (x * HY + 2 * qy + dy) * LANES
                on = mask[:, 0, :, at : at + LANES].reshape(rows, LANES) == 1
                total = total + jnp.where(on & (p == 4.0 * x + 2.0 * dy), v, 0.0)
        halves.append(total)
    kept = jnp.concatenate(halves, axis=1).astype(bf16)
    v = lax.dot_general(kept, table, NT, preferred_element_type=f32).astype(bf16)
    used = samples * C_IN
    at = BY * 4 * used
    to_x[at : at + rows] = v
    to_x[at + rows : at + 2 * rows] = spots
    copies[3].wait()
    pieces = [source[s, 0].astype(f32) for s in range(samples)]
    if used < PACK:
        pieces.append(jnp.zeros((PACK - used, BX * BY * BZ), f32))
    cells = jnp.concatenate(pieces, axis=0)
    own[...] = cells.astype(bf16)
    for t in range(BY):
        group = []
        for x in (0, BX - 1):
            for y in (t // 2, BY - 1 - t // 2):
                at = (x * BY + y) * BZ + (t % 2) * LANES
                group.append(cells[0:used, at : at + LANES])
        to_x[4 * used * t : 4 * used * (t + 1)] = jnp.concatenate(group, axis=0).astype(bf16)


def ends(samples, vp_row, to_x, own, edge, to_y):
    rows = samples * C_TWO
    lane = iota((LANES, LANES), 0)
    spot = (lane // QZ) * 2 + (lane % QZ == QZ - 1).astype(i32)
    spot = jnp.where((lane % QZ == 0) | (lane % QZ == QZ - 1), spot, -LANES)
    column = iota((LANES, LANES), 1)
    packed = jnp.zeros((C_TWO, LANES), f32)
    for s in range(samples):
        for t in range(2):
            pick = (spot + (8 * s + 4 * t) == column).astype(bf16)
            at = vp_row + t * rows + s * C_TWO
            packed = packed + jnp.dot(to_x[at : at + C_TWO], pick, preferred_element_type=f32)
    lane = iota((PACK, LANES), 1)
    cells = packed[0:PACK]
    for row in range(BX * BY):
        left = own[:, row * BZ : row * BZ + LANES].astype(f32)
        right = own[:, (row + 1) * BZ - LANES : (row + 1) * BZ].astype(f32)
        cells = jnp.where(lane == ENDS_AT + 2 * row, left[:, 0:1], cells)
        cells = jnp.where(lane == ENDS_AT + 2 * row + 1, right[:, LANES - 1 :], cells)
    edge[0:PACK] = cells.astype(bf16)
    edge[PACK:] = packed[PACK:].astype(bf16)
    used = samples * C_IN
    to_y[4 * 4 * used :] = to_x[vp_row:]
    for t in range(4):
        group = []
        for x in range(BX):
            at = (x * BY + (BY - 1) * (t // 2)) * BZ + (t % 2) * LANES
            group.append(own[:, at : at + LANES].astype(f32)[0:used])
        to_y[4 * used * t : 4 * used * (t + 1)] = jnp.concatenate(group, axis=0).astype(bf16)


def select_one(samples, *refs):
    far, (chosen, folded_weights, expand), near, sems = refs[:3], refs[3:6], refs[6:9], refs[9]
    place, mask, weights = near
    copies = fetch(tuple(zip(far, near)), sems)
    k = iota((2 * LANES, TABLE), 0)
    j = iota((1, TABLE), 1)
    shift = j // (QY * LANES) - 1
    qy = (j // LANES) % QY
    z = j % LANES - shift
    beyond = LANES + qy * 2 + (z < 0).astype(i32)
    expand[...] = (k == jnp.where((z >= 0) & (z < LANES), qy * QZ + z // 2, beyond)).astype(bf16)
    rows = samples * C_ONE
    table = doubling()
    parity = (iota((rows, BZ), 1) % 2).astype(f32)
    copies[2].wait()
    folded_weights[...] = jnp.concatenate(
        [jnp.concatenate([weights[3 * o + i] for i in range(3)], axis=1) for o in range(9)], axis=0
    )
    copies[0].wait()
    copies[1].wait()
    for x in range(HX):
        for y in range(HY):
            at = (x * HY + y) * LANES
            spots = place[:, 0, :, at : at + LANES].reshape(rows, LANES).astype(f32).astype(bf16)
            wide = jnp.dot(spots, table, preferred_element_type=f32) - parity
            for dx in range(2):
                for dy in range(2):
                    to = ((2 * x + dx) * BY + 2 * y + dy) * BZ
                    on = mask[:, 0, :, to : to + BZ].reshape(rows, BZ) == 1
                    hit = on & (wide == 4.0 * dx + 2.0 * dy)
                    chosen[:, to : to + BZ] = jnp.where(hit, 1.0, 0.0).astype(bf16)


def expand_windows(samples, vp_at, edge_at, tile_of, blocks, expand, fields):
    rows = samples * C_TWO
    lane = iota((rows, LANES), 1)
    odd = iota((C_TWO, LANES), 1) % 2 == 1
    groups = {}
    for nx, ny in vp_at:
        key = (vp_at[nx, ny], edge_at[nx, ny, -1], edge_at[nx, ny, 1])
        groups.setdefault(key, []).append((nx, ny))
    for ((ref, at), low, high), places in groups.items():
        edge = blocks[low[0]][low[1] : low[1] + C_TWO].astype(f32)
        if low != high:
            other = blocks[high[0]][high[1] : high[1] + C_TWO].astype(f32)
            edge = jnp.where(odd, edge, other)
        parts = []
        for t in range(2):
            for s in range(samples):
                by = 8 * s + 4 * t
                parts.append(pltpu.roll(edge, LANES - by, 1) if by else edge)
        both = jnp.concatenate(
            [blocks[ref][at : at + 2 * rows], jnp.concatenate(parts, axis=0).astype(bf16)], axis=1
        )
        wide = jnp.dot(both, expand[...], preferred_element_type=f32)
        for i, oz in enumerate(OFFS):
            parity = ((lane - oz) & 1).astype(f32)
            for qy in range(QY):
                lanes = slice((i * QY + qy) * LANES, (i * QY + qy + 1) * LANES)
                v = wide[0:rows, lanes].astype(bf16)
                p = (wide[rows : 2 * rows, lanes] - parity).astype(bf16)
                for x in range(HX):
                    for dy in range(2):
                        y = 2 * qy + dy
                        spots = []
                        for nx, ny in places:
                            near_x = nx == 0 or x == (HX - 1 if nx < 0 else 0)
                            near_y = ny == 0 or y == (HY - 1 if ny < 0 else 0)
                            if near_x and near_y:
                                spots.append(tile_of[x + 1 + nx * HX, y + 1 + ny * HY])
                        if not spots:
                            continue
                        cells = jnp.where(p == 4.0 * x + 2.0 * dy, v, jnp.zeros_like(v))
                        for spot in spots:
                            for s in range(samples):
                                fields[s, i * C_TWO : (i + 1) * C_TWO, spot * LANES : (spot + 1) * LANES] = (
                                    cells[s * C_TWO : (s + 1) * C_TWO]
                                )


def tiles_own():
    return {(px, py): (px - 1) * HY + py - 1 for px in range(1, HX + 1) for py in range(1, HY + 1)}


def tiles_sides():
    tiles = [(px, py) for px in (0, HX + 1) for py in range(1, HY + 1)]
    tiles += [(px, py) for px in range(1, HX + 1) for py in (0, HY + 1)]
    return {key: i for i, key in enumerate(tiles)}


def tiles_corners():
    return {(px, py): 2 * (px > 0) + (py > 0) for px in (0, HX + 1) for py in (0, HY + 1)}


def shift_pooled(samples, tile_of, pooled, moved):
    for (px, py), tile in tile_of.items():
        k = 0
        for ox in OFFS:
            for oy in OFFS:
                x, y = px - 1 + ox, py - 1 + oy
                inside = 0 <= x < HX and 0 <= y < HY
                for s in range(samples):
                    if inside:
                        at = (x * HY + y) * LANES
                        value = pooled[s, 0, :, at : at + LANES]
                    else:
                        value = jnp.zeros((C_ONE, LANES), bf16)
                    moved[s, k * C_ONE : (k + 1) * C_ONE, tile * LANES : (tile + 1) * LANES] = value
                k += 1


def products_two(samples, tile_of, fields, moved, weights, sums, totals):
    for s in range(samples):
        wide = jnp.dot(weights[...], fields[s], preferred_element_type=f32)
        for x in range(HX):
            for y in range(HY):
                k = 0
                for ox in OFFS:
                    for oy in OFFS:
                        tile = tile_of.get((x + 1 - ox, y + 1 - oy))
                        if tile is not None:
                            part = wide[k * C_ONE : (k + 1) * C_ONE, tile * LANES : (tile + 1) * LANES]
                            old = sums[s].get((x, y))
                            sums[s][x, y] = part if old is None else old + part
                        k += 1
        totals = totals + lax.dot_general(moved[s], fields[s], NT, preferred_element_type=f32)
    return totals


def parts_of(samples, part):
    return [
        {
            (x, y): part[s * C_ONE : (s + 1) * C_ONE, (x * HY + y) * LANES : (x * HY + y + 1) * LANES]
            for x in range(HX)
            for y in range(HY)
        }
        for s in range(samples)
    ]


def store_parts(sums, part):
    for s, tiles in enumerate(sums):
        for (x, y), value in tiles.items():
            at = (x * HY + y) * LANES
            part[s * C_ONE : (s + 1) * C_ONE, at : at + LANES] = value.astype(part.dtype)


def layer_two_own(samples, vp_at, edge_at, *refs):
    blocks, (pooled, weights, expand, part, total, fields, moved) = refs[:-7], refs[-7:]
    tile_of = tiles_own()
    expand_windows(samples, vp_at, edge_at, tile_of, blocks, expand, fields)
    shift_pooled(samples, tile_of, pooled, moved)
    sums = [{} for _ in range(samples)]
    totals = jnp.zeros((9 * C_ONE, 3 * C_TWO), f32)
    total[...] = products_two(samples, tile_of, fields, moved, weights, sums, totals)
    store_parts(sums, part)


def layer_two_sides(samples, vp_at, edge_at, *refs):
    blocks, (pooled, weights, expand, old, old_total, part, total, fields, moved) = refs[:-9], refs[-9:]
    tile_of = tiles_sides()
    expand_windows(samples, vp_at, edge_at, tile_of, blocks, expand, fields)
    shift_pooled(samples, tile_of, pooled, moved)
    sums = parts_of(samples, old)
    total[...] = products_two(samples, tile_of, fields, moved, weights, sums, old_total[...])
    store_parts(sums, part)


def layer_two_corners(samples, scale, vp_at, edge_at, *refs):
    blocks, (pooled, weights, expand, part, total, kept, message, fields) = refs[:-8], refs[-8:]
    tile_of = tiles_corners()
    expand_windows(samples, vp_at, edge_at, tile_of, blocks, expand, fields)
    sums = parts_of(samples, part)
    totals = [total[k * C_ONE : (k + 1) * C_ONE] for k in range(9)]
    for (px, py), tile in tile_of.items():
        x, ox = (0, 1) if px == 0 else (HX - 1, -1)
        y, oy = (0, 1) if py == 0 else (HY - 1, -1)
        k = 3 * (ox + 1) + oy + 1
        at = (x * HY + y) * LANES
        for s in range(samples):
            cells = fields[s, :, tile * LANES : (tile + 1) * LANES]
            sums[s][x, y] = sums[s][x, y] + jnp.dot(
                weights[k * C_ONE : (k + 1) * C_ONE], cells, preferred_element_type=f32
            )
            totals[k] = totals[k] + lax.dot_general(
                pooled[s, 0, :, at : at + LANES], cells, NT, preferred_element_type=f32
            )
    store_parts(sums, kept)
    width = 3 * C_TWO
    for k in range(9):
        message[:, k * width : (k + 1) * width] = totals[k] * scale
    message[:, GRAD_W_TWO:ONE_AT] = jnp.zeros((C_ONE, ONE_AT - GRAD_W_TWO), f32)


def shift_input(samples, rows_of, face_at, line_at, edge_at, blocks, own, ahead):
    used = samples * C_IN
    lane = iota((PACK, BZ), 1)
    for (px, py), line in rows_of.items():
        nx = -1 if px == 0 else 1 if px == BX + 1 else 0
        ny = -1 if py == 0 else 1 if py == BY + 1 else 0
        x, y = (px - 1) % BX, (py - 1) % BY
        if nx == 0 and ny == 0:
            row = own[:, (x * BY + y) * BZ : (x * BY + y + 1) * BZ].astype(f32)
        else:
            if nx != 0:
                ref, at = face_at[nx] if ny == 0 else line_at[nx, ny]
                tile = 2 * min(y, BY - 1 - y)
                chunk = 2 * (0 if x == 0 else 1) + (1 if y >= BY // 2 else 0)
            else:
                ref, at = line_at[nx, ny]
                tile = 2 * (0 if y == 0 else 1)
                chunk = x
            halves = []
            for t in (tile, tile + 1):
                four = blocks[ref][at + 4 * used * t : at + 4 * used * (t + 1)].astype(f32)
                halves.append(four[chunk * used : (chunk + 1) * used])
            row = jnp.concatenate(halves, axis=1)
            if used < PACK:
                row = jnp.concatenate([row, jnp.zeros((PACK - used, BZ), f32)], axis=0)
        ends = []
        for nz in (-1, 1):
            ref, at = edge_at[nx, ny, nz]
            ends.append(blocks[ref][at : at + PACK].astype(f32))
        at = ENDS_AT + 2 * (x * BY + y)
        to = line * BZ
        before = jnp.where(lane == 0, ends[0][:, at + 1 : at + 2], pltpu.roll(row, 1, 1))
        after = jnp.where(lane == BZ - 1, ends[1][:, at : at + 1], pltpu.roll(row, BZ - 1, 1))
        for i, piece in enumerate((before, row, after)):
            ahead[i * PACK : (i + 1) * PACK, to : to + BZ] = piece.astype(bf16)


def lines_inside():
    return {(px, py): px * BY + py - 1 for px in range(BX + 2) for py in range(1, BY + 1)}


def lines_ends():
    return {(px, py): 2 * px + (py > 0) for px in range(BX + 2) for py in (0, BY + 1)}


def emit(samples, kept, out):
    for s in range(samples):
        out[s, 0] = kept[s * C_ONE : (s + 1) * C_ONE]


def middle_lines():
    return range(3, BY - 3)


def layer_one_inside(samples, face_at, edge_at, *refs):
    blocks, (own, part, chosen, ahead, product, middle) = refs[:-6], refs[-6:]
    shift_input(samples, lines_inside(), face_at, {}, edge_at, blocks, own, ahead)
    rows = samples * C_ONE
    table = doubling()
    lines = middle_lines()
    for x in range(HX):
        for y in range(1, HY - 1):
            at = (x * HY + y) * LANES
            cells = part[:, at : at + LANES].astype(bf16)
            wide = jnp.dot(cells, table, preferred_element_type=f32).astype(bf16)
            for dx in range(2):
                for dy in range(2):
                    cx, cy = 2 * x + dx, 2 * y + dy
                    value = wide * chosen[:, (cx * BY + cy) * BZ : (cx * BY + cy + 1) * BZ]
                    for j, oy in enumerate(OFFS):
                        if cy + oy in lines:
                            to = (cy + oy - lines.start) * BZ
                            middle[cx, j * rows : (j + 1) * rows, to : to + BZ] = value
    plane = BY * BZ
    total = jnp.zeros((3 * rows, 9 * PACK), f32)
    for x in range(BX):
        pieces = []
        for ox in OFFS:
            at = (x + 1 + ox) * plane
            pieces.append(ahead[:, at + lines.start * BZ : at + lines.stop * BZ])
        total = total + lax.dot_general(
            middle[x], jnp.concatenate(pieces, axis=0), NT, preferred_element_type=f32
        )
    product[...] = total


def layer_one(samples, scale, line_at, edge_at, *refs):
    blocks, (own, ahead, begun, grad, chosen, before_sums, half, mine, other, ahead_ends, inside, ends) = (
        refs[:-12], refs[-12:],
    )
    shift_input(samples, lines_ends(), {}, line_at, edge_at, blocks, own, ahead_ends)
    lines = middle_lines()
    rows = samples * C_ONE
    table = doubling()
    empty = jnp.zeros((rows, BZ), bf16)
    for x in range(BX):
        inside[x, 0:rows, (BY - 1) * BZ :] = empty
        inside[x, 2 * rows :, 0:BZ] = empty
        ends[x, 0:rows, BZ:] = empty
        ends[x, rows : 2 * rows, 0:BZ] = empty
        ends[x, rows : 2 * rows, BZ:] = empty
        ends[x, 2 * rows :, 0:BZ] = empty
    for x in range(HX):
        for y in range(HY):
            at = (x * HY + y) * LANES
            wide = jnp.dot(grad[:, at : at + LANES], table, preferred_element_type=f32).astype(bf16)
            for dx in range(2):
                for dy in range(2):
                    cx, cy = 2 * x + dx, 2 * y + dy
                    value = wide * chosen[:, (cx * BY + cy) * BZ : (cx * BY + cy + 1) * BZ]
                    for j, oy in enumerate(OFFS):
                        to = cy + oy
                        here = slice(j * rows, (j + 1) * rows)
                        if to < 0:
                            ends[cx, here, 0:BZ] = value
                        elif to >= BY:
                            ends[cx, here, BZ:] = value
                        elif to not in lines:
                            inside[cx, here, to * BZ : (to + 1) * BZ] = value
    width = 3 * 3 * PACK
    product = begun[...]
    plane = BY * BZ
    for x in range(BX):
        for left, right, size, first, last in (
            (inside, ahead, plane, 0, lines.start * BZ),
            (inside, ahead, plane, lines.stop * BZ, plane),
            (ends, ahead_ends, 2 * BZ, 0, 2 * BZ),
        ):
            pieces = [right[:, (x + 1 + ox) * size + first : (x + 1 + ox) * size + last] for ox in OFFS]
            product = product + lax.dot_general(
                left[x, :, first:last], jnp.concatenate(pieces, axis=0), NT, preferred_element_type=f32
            )
    sample_of = (iota((C_ONE, width), 1) % PACK) // C_IN
    k = iota((width, LANES), 0)
    to = (k % C_IN) * STRIDE_ONE + (k // (3 * PACK)) * 9 + (k // PACK) % 3
    total = jnp.zeros((C_ONE, LANES), f32)
    for j in range(3):
        folded = jnp.zeros((C_ONE, width), f32)
        for s in range(samples):
            at = j * rows + s * C_ONE
            folded = folded + jnp.where(sample_of == s, product[at : at + C_ONE], 0.0)
        fold = (to + 3 * j == iota((width, LANES), 1)).astype(bf16)
        parts = []
        for _ in range(3):
            parts.append(folded.astype(bf16))
            folded = folded - parts[-1].astype(f32)
        got = jnp.dot(jnp.concatenate(parts, axis=0), fold, preferred_element_type=f32)
        total = total + (got[2 * C_ONE :] + got[C_ONE : 2 * C_ONE] + got[0:C_ONE])
    sums = jnp.concatenate([before_sums[...], total * scale], axis=1)
    top, bottom = sums[0:HALF], sums[HALF:]
    first = half[0] == 0
    mine[...] = jnp.where(first, top, bottom)
    other[...] = jnp.where(first, bottom, top)


def finish(half, mine, theirs, grad_one, grad_two):
    first = half[0] == 0
    top = jnp.where(first, mine[...], theirs[...])
    bottom = jnp.where(first, theirs[...], mine[...])
    for rows, part in ((slice(0, HALF), top), (slice(HALF, C_ONE), bottom)):
        for o in range(27):
            grad_two[o, rows] = part[:, o * C_TWO : (o + 1) * C_TWO]
        for c in range(C_IN):
            at = ONE_AT + c * STRIDE_ONE
            grad_one[c, rows] = part[:, at : at + 27]


def call(body, shapes, operands, far=0, scratch=(), flops=0, moved=0, scalars=()):
    if far:
        scratch = [pltpu.VMEM(a.shape, a.dtype) for a in operands[:far]]
        scratch.append(pltpu.SemaphoreType.DMA((far,)))
        away = [pltpu.with_memory_space_constraint(a, pltpu.HBM) for a in operands[:far]]
        operands = (*away, *operands[far:])
    spaces = [pltpu.HBM] * far + [pltpu.VMEM] * (len(operands) - far)
    for i in scalars:
        spaces[i] = pltpu.SMEM
    return pl.pallas_call(
        body,
        out_shape=shapes,
        in_specs=[pl.BlockSpec(memory_space=space) for space in spaces],
        out_specs=jax.tree.map(lambda _: pl.BlockSpec(memory_space=pltpu.VMEM), shapes),
        scratch_shapes=list(scratch),
        compiler_params=pltpu.CompilerParams(vmem_limit_bytes=32 * 2**20),
        cost_estimate=pl.CostEstimate(flops=flops, bytes_accessed=moved, transcendentals=0),
    )(*operands)


def block_side(blocks):
    return min(k for k in range(1, blocks + 1) if k * k * k >= blocks)


def from_block(array, side, *offset):
    pairs = []
    for i in range(lax.axis_size("space")):
        at = (i // (side * side), i // side % side, i % side)
        x, y, z = ((c + o) % side for c, o in zip(at, offset))
        pairs.append(((x * side + y) * side + z, i))
    return lax.ppermute(array, "space", pairs)


def both_sides(array, side, axis):
    below = from_block(array, side, *(-1 if a == axis else 0 for a in range(3)))
    if side == 2:
        return {-1: below, 1: below}
    return {-1: below, 1: from_block(array, side, *(1 if a == axis else 0 for a in range(3)))}


def swapped(array, bits):
    devices = lax.axis_size("dp") * lax.axis_size("space")
    return lax.ppermute(array, ("dp", "space"), [(i, i ^ bits) for i in range(devices)])


def stacked(parts):
    kept, starts, places = [], [], []
    rows = 0
    for part in parts:
        found = [i for i, a in enumerate(kept) if a is part]
        if not found:
            found = [len(kept)]
            kept.append(part)
            starts.append(rows)
            rows += part.shape[0]
        places.append(starts[found[0]])
    return jnp.concatenate(kept, axis=0), places


def operands_of(*tables):
    arrays, numbered = [], []
    for table in tables:
        new = {}
        for key, (array, row) in table.items():
            found = [i for i, a in enumerate(arrays) if a is array]
            if not found:
                found = [len(arrays)]
                arrays.append(array)
            new[key] = (found[0], row)
        numbered.append(new)
    return arrays, numbered


def local(inputs, mask_one, place_one, pooled_one, w_two, mask_two, place_two, grad_two):
    blocks = lax.axis_size("space")
    side = block_side(blocks)
    samples = inputs.shape[0]
    cells = inputs.shape[3]
    half_cells = HX * HY * HZ
    shape = jax.ShapeDtypeStruct
    vp_rows = 2 * samples * C_TWO
    four = 4 * samples * C_IN
    vp_row = BY * four
    to_x, own = call(
        functools.partial(prepare, samples),
        (shape((BY * four + vp_rows, LANES), bf16), shape((PACK, cells), bf16)),
        (grad_two, place_two, mask_two, inputs),
        far=4,
        flops=2 * 10**7,
        moved=2**20,
    )
    edge, to_y = call(
        functools.partial(ends, samples, vp_row),
        (shape((C_TWO, LANES), bf16), shape((4 * four + vp_rows, LANES), bf16)),
        (to_x, own),
        flops=10**7,
        moved=2**19,
    )
    chosen, folded_weights, expand = call(
        functools.partial(select_one, samples),
        (
            shape((samples * C_ONE, cells), bf16),
            shape((9 * C_ONE, 3 * C_TWO), bf16),
            shape((2 * LANES, TABLE), bf16),
        ),
        (place_one, mask_one, w_two),
        far=3,
        flops=2 * 10**7,
        moved=3 * 2**20,
    )
    vp_at, edge_at, face_at, line_at = {(0, 0): (to_x, vp_row)}, {}, {}, {}
    from_x = both_sides(to_x, side, 0)
    edge_z = both_sides(edge, side, 2)
    if side == 2:
        diagonal = from_block(edge, side, 1, 0, 1)
        edge_x = {nz: {nx: diagonal for nx in (-1, 1)} for nz in (-1, 1)}
    else:
        edge_x = {nz: {nx: from_block(edge, side, nx, 0, nz) for nx in (-1, 1)} for nz in (-1, 1)}
    first, first_starts = stacked([to_y, edge_z[-1], edge_z[1]])
    first = both_sides(first, side, 1)
    side_tiles, corner_tiles = len(tiles_sides()), len(tiles_corners())
    part_shape = shape((samples * C_ONE, half_cells), f32)
    total_shape = shape((9 * C_ONE, 3 * C_TWO), f32)
    arrays, tables = operands_of({(0, 0): vp_at[0, 0]}, {(0, 0, n): (edge_z[n], 0) for n in (-1, 1)})
    part, total_two = call(
        functools.partial(layer_two_own, samples, *tables),
        (
            part_shape,
            total_shape,
        ),
        (*arrays, pooled_one, folded_weights, expand),
        scratch=(
            pltpu.VMEM((samples, 3 * C_TWO, half_cells), bf16),
            pltpu.VMEM((samples, 9 * C_ONE, half_cells), bf16),
        ),
        flops=1000,
        moved=1000,
    )
    ready = {n: lax.optimization_barrier((from_x[n], total_two))[0] for n in ((-1,) if side == 2 else (-1, 1))}
    parts = []
    for n in (-1, 1):
        again = n == 1 and side == 2
        parts += parts[:2] if again else [ready[n][vp_row:], ready[n][: 2 * four]]
    second, starts = stacked(parts)
    second = both_sides(second, side, 1)
    third, edge_starts = stacked([edge_z[-1], edge_z[1]] + [edge_x[nz][nx] for nz in (-1, 1) for nx in (-1, 1)])
    third = both_sides(third, side, 1)
    for n in (-1, 1):
        vp_at[n, 0] = (from_x[n], vp_row)
        face_at[n] = (from_x[n], 0)
        vp_at[0, n] = (first[n], 4 * four)
        line_at[0, n] = (first[n], 0)
        edge_at[0, 0, n] = (edge_z[n], 0)
        for i, nx in enumerate((-1, 1)):
            edge_at[nx, 0, n] = (edge_x[n][nx], 0)
            vp_at[nx, n] = (second[n], starts[2 * i])
            line_at[nx, n] = (second[n], starts[2 * i + 1])
        for i, nz in enumerate((-1, 1)):
            edge_at[0, n, nz] = (first[n], first_starts[1 + i])
            for j, nx in enumerate((-1, 1)):
                edge_at[nx, n, nz] = (third[n], edge_starts[2 + 2 * i + j])
    total = lax.axis_size("dp") * samples * blocks * cells

    def near(table, y):
        return {key: value for key, value in table.items() if key[1] in y}

    arrays, tables = operands_of(
        {key: value for key, value in vp_at.items() if (key[0] == 0) != (key[1] == 0)},
        {key: value for key, value in edge_at.items() if (key[0] == 0) != (key[1] == 0)},
    )
    part, total_two = call(
        functools.partial(layer_two_sides, samples, *tables),
        (part_shape, total_shape),
        (*arrays, pooled_one, folded_weights, expand, part, total_two),
        scratch=(
            pltpu.VMEM((samples, 3 * C_TWO, side_tiles * LANES), bf16),
            pltpu.VMEM((samples, 9 * C_ONE, side_tiles * LANES), bf16),
        ),
        flops=1000,
        moved=1000,
    )
    arrays, tables = operands_of(face_at, near(edge_at, (0,)))
    ahead, begun = call(
        functools.partial(layer_one_inside, samples, *tables),
        (
            shape((3 * PACK, (BX + 2) * BY * BZ), bf16),
            shape((3 * samples * C_ONE, 9 * PACK), f32),
        ),
        (*arrays, own, part, chosen),
        scratch=(pltpu.VMEM((BX, 3 * samples * C_ONE, len(middle_lines()) * BZ), bf16),),
        flops=10**8,
        moved=2**20,
    )
    arrays, tables = operands_of(
        {key: value for key, value in vp_at.items() if key[0] != 0 and key[1] != 0},
        {key: value for key, value in edge_at.items() if key[0] != 0 and key[1] != 0},
    )
    kept, sums = call(
        functools.partial(layer_two_corners, samples, float(total // 8) ** -0.5, *tables),
        (
            shape((samples * C_ONE, half_cells), bf16),
            shape((C_ONE, ONE_AT), f32),
        ),
        (*arrays, pooled_one, folded_weights, expand, part, total_two),
        scratch=(pltpu.VMEM((samples, 3 * C_TWO, corner_tiles * LANES), bf16),),
        flops=5 * 10**8,
        moved=2**20,
    )
    arrays, tables = operands_of(line_at, near(edge_at, (-1, 1)))
    half = (lax.axis_index("dp") % 2).astype(i32).reshape(1)
    operands = (*arrays, own, ahead, begun, kept, chosen, sums, half)
    half_sums = shape((HALF, WIDTH), f32)
    mine, other = call(
        functools.partial(layer_one, samples, float(total) ** -0.5, *tables),
        (half_sums, half_sums),
        operands,
        scratch=(
            pltpu.VMEM((3 * PACK, (BX + 2) * 2 * BZ), bf16),
            pltpu.VMEM((BX, 3 * samples * C_ONE, BY * BZ), bf16),
            pltpu.VMEM((BX, 3 * samples * C_ONE, 2 * BZ), bf16),
        ),
        flops=5 * 10**8,
        moved=2**20,
        scalars=(len(operands) - 1,),
    )
    grad_pooled = call(
        functools.partial(emit, samples),
        shape((samples, 1, C_ONE, half_cells), bf16),
        (kept,),
        flops=10**6,
        moved=2**18,
    )
    mine = mine + swapped(other, blocks)
    devices = lax.axis_size("dp") * blocks
    bits = [1 << k for k in range(devices.bit_length() - 1) if 1 << k > blocks]
    bits += [1 << k for k in range(devices.bit_length() - 1) if 1 << k < blocks]
    while len(bits) > 1:
        (a, b), bits = bits[:2], bits[2:]
        mine = (mine + swapped(mine, a)) + (swapped(mine, b) + swapped(mine, a ^ b))
    for a in bits:
        mine = mine + swapped(mine, a)
    grad_w_one, grad_w_two = call(
        finish,
        (shape((C_IN, C_ONE, 27), f32), shape((27, C_ONE, C_TWO), f32)),
        (half, mine, swapped(mine, blocks)),
        scalars=(0,),
    )
    return grad_pooled, jnp.transpose(grad_w_one, (2, 0, 1)), grad_w_two


def solution(mesh):
    split = P("dp", "space", None, None)
    return jax.shard_map(
        local,
        mesh=mesh,
        in_specs=(split, split, split, split, P(), split, split, split),
        out_specs=(split, P(), P()),
        check_vma=False,
    )
```
